512 devices in a mesh: section: 16 (over y, core), dp: 16 (over x, z_hi), mp: 2 (over z_lo).
Axes of the slice: x: 4, y: 8, z: 8 (z_hi: 4, z_lo: 2; z = z_hi * 2 + z_lo), core: 2. Of those that a mesh axis runs over, the one named last changes fastest.
Arguments:
- section_in: bfloat16 [16, 16, 104, 7168], P('section', 'dp', None, 'mp'), may hold values from -6 to 6
- vision_rows: bfloat16 [16, 24, 7168], P('dp', None, 'mp'), may hold values from -6 to 6
- alternate: int32 [16, 104], P('dp'), may hold values from -1 to 23, as said below
- grad_in: bfloat16 [16, 16, 104, 7168], P('section', 'dp', None, 'mp'), may hold values from -1.5 to 1.5
- parked: bfloat16 [16, 16, 104, 7168], P('section', 'dp', None, 'mp'), may hold values from -6 to 6
- w_down: bfloat16 [16, 256, 7168], P('section', 'dp', 'mp'), may hold values from -0.0625 to 0.0625
- w_up: bfloat16 [16, 256, 7168], P('section', 'dp', 'mp'), may hold values from -0.375 to 0.375
Outputs:
- section_out: bfloat16 [16, 16, 104, 7168], P('section', 'dp', None, 'mp')
- parked_out: bfloat16 [16, 16, 104, 7168], P('section', 'dp', None, 'mp')
- input_grad: bfloat16 [16, 16, 104, 7168], P('section', 'dp', None, 'mp')
- up_grad: bfloat16 [16, 256, 7168], P('section', 'dp', 'mp')
- down_grad: bfloat16 [16, 256, 7168], P('section', 'dp', 'mp')
The draws below stay inside these ranges and needn't reach their ends.
Inputs may be any that keep to these rules, and one draw needn't show every extreme that they name: `alternate`: in each replica every image-token row 0 to 23 fills exactly one row, in increasing order along the rows; all other entries are -1.
All inputs are finite; a program needn't handle non-finite values.
Results may differ from the reference program's by a relative error of at most 0.019.
Values may be sent and summed in bfloat16 or wider, within the bound.
A program may use at most 64 MiB of HBM per device.

```python
import jax
import jax.numpy as jnp
from jax import lax

D = 7168
R = 256
ROWS = 104
VISION = 24
SECTIONS = 16
REPLICAS = 16


def draw_alternate(key, part):
    key = jax.random.fold_in(key, 11)

    def one_replica(replica):
        subkey = jax.random.fold_in(key, replica)
        order = jax.random.permutation(subkey, ROWS)
        marks = jnp.zeros((ROWS,), jnp.int32).at[order[:VISION]].set(1)
        ranks = jnp.cumsum(marks) - 1
        return jnp.where(marks == 1, ranks, -1).astype(jnp.int32)
    return jax.vmap(one_replica)(jnp.arange(REPLICAS))


def level_of(rng, extent, pieces, low, high):
    loudness, own = 1.0, jax.random.fold_in(rng, 6)
    for axis_at, parts in pieces:
        steps = jnp.exp(jax.random.uniform(jax.random.fold_in(own, axis_at), (parts,), jnp.float32, low / len(pieces), high / len(pieces)))
        loudness = loudness * jnp.repeat(steps, extent[axis_at] // parts).reshape([-1 if axis == axis_at else 1 for axis in range(len(extent))])
    return loudness


def scatter_about(own_key, dims, spread, most, pieces=(), kind=jnp.bfloat16):
    values = jax.random.normal(own_key, dims, jnp.float32) * spread
    if len(pieces) > 0:
        values = level_of(own_key, dims, pieces, -0.22, 0.18) * values
    return jnp.clip(values, min=-most, max=most).astype(kind)


def setup_inputs(seed: int = 0) -> dict:
    arg_keys = jax.random.split(jax.random.key(seed), 8)
    return {
        "section_in": scatter_about(arg_keys[0], (SECTIONS, REPLICAS, ROWS, D), 1.0, 6.0, ((0, 16), (1, 16), (3, 2))),
        "vision_rows": scatter_about(arg_keys[1], (REPLICAS, VISION, D), 1.0, 6.0, ((0, 16), (2, 2))),
        "alternate": draw_alternate(jax.random.fold_in(arg_keys[7], 71), 0),
        "grad_in": scatter_about(arg_keys[3], (SECTIONS, REPLICAS, ROWS, D), 0.25, 1.5, ((0, 16), (1, 16), (3, 2))),
        "parked": scatter_about(arg_keys[4], (SECTIONS, REPLICAS, ROWS, D), 1.0, 6.0, ((0, 16), (1, 16), (3, 2))),
        "w_down": scatter_about(arg_keys[5], (SECTIONS, R, D), D ** -0.5, 0.0625, ((0, 16), (1, 16), (2, 2))),
        "w_up": scatter_about(arg_keys[6], (SECTIONS, R, D), R ** -0.5, 0.375, ((0, 16), (1, 16), (2, 2))),
    }


def gelu_slope(values, upstream):
    return jax.vjp(lambda inner: jax.nn.gelu(inner, approximate=True), values)[1](upstream)[0]

def one_section(bundle):
    forward_rows, backward_rows, upstream, down_weight, up_weight = bundle
    down_f = down_weight.astype(jnp.float32)
    up_f = up_weight.astype(jnp.float32)
    fwd_pre = jnp.einsum('rnd,kd->rnk', forward_rows.astype(jnp.float32), down_f)
    fwd_act = jax.nn.gelu(fwd_pre, approximate=True).astype(jnp.bfloat16)
    outputs = (forward_rows.astype(jnp.float32) + jnp.einsum('rnk,kd->rnd', fwd_act.astype(jnp.float32), up_f)).astype(jnp.bfloat16)
    bwd_pre = jnp.einsum('rnd,kd->rnk', backward_rows.astype(jnp.float32), down_f)
    bwd_act = jax.nn.gelu(bwd_pre, approximate=True).astype(jnp.bfloat16)
    slope_pre = jnp.einsum('rnd,kd->rnk', upstream.astype(jnp.float32), up_f)
    pre_grad = gelu_slope(bwd_pre, slope_pre).astype(jnp.bfloat16)
    input_grad = (upstream.astype(jnp.float32) + jnp.einsum('rnk,kd->rnd', pre_grad.astype(jnp.float32), down_f)).astype(jnp.bfloat16)
    up_part = jnp.einsum('rnk,rnd->rkd', bwd_act.astype(jnp.float32), upstream.astype(jnp.float32)).astype(jnp.bfloat16)
    down_part = jnp.einsum('rnk,rnd->rkd', pre_grad.astype(jnp.float32), backward_rows.astype(jnp.float32)).astype(jnp.bfloat16)
    up_grad = (lax.optimization_barrier(jnp.sum(up_part.astype(jnp.float32), axis=0)) * (1.0 / REPLICAS)).astype(jnp.bfloat16)
    down_grad = (lax.optimization_barrier(jnp.sum(down_part.astype(jnp.float32), axis=0)) * (1.0 / REPLICAS)).astype(jnp.bfloat16)
    return (outputs, input_grad, up_grad, down_grad)

def reference(section_in, vision_rows, alternate, grad_in, parked, w_down, w_up):
    picks = jnp.maximum(alternate, 0).astype(jnp.int32)
    chosen = jnp.take_along_axis(vision_rows, picks[:, :, None], axis=1)
    first_in = jnp.where((alternate >= 0)[:, :, None], chosen, section_in[0])
    forward_in = jnp.concatenate([first_in[None], section_in[1:]], axis=0)
    backward_in = parked[::-1]
    outputs, input_grad, up_grad, down_grad = lax.map(one_section, (forward_in, backward_in, grad_in, w_down, w_up))
    section_out = jnp.roll(outputs, 1, axis=0)
    parked_out = forward_in[::-1]
    return (section_out, parked_out, input_grad, up_grad, down_grad)
```

```python
import functools
import math

import jax
import jax.numpy as jnp
from jax import lax
from jax.experimental import pallas as pl
from jax.experimental.pallas import tpu as pltpu
from jax.sharding import PartitionSpec as P

MESH = pl.DeviceIdType.MESH
BF16, F32 = jnp.bfloat16, jnp.float32

D = 3584
R = 256
ROWS = 104
VISION = 24
SHARE = 16
TILE = 256
PIECES = 4
PIECE = D // PIECES
TILES = D // TILE
NX, NZ = 4, 4
SPLIT = 3 * TILE

N_GATHER = 16
N_REDUCE = 12

NT = (((1,), (1,)), ((), ()))
TN = (((0,), (0,)), ((), ()))

SCALE = math.sqrt(2 / math.pi)


def gelu(v):
    return 0.5 * v * (1.0 + jnp.tanh(SCALE * (v + 0.044715 * (v * v * v))))


def gelu_slope(v):
    t = jnp.tanh(SCALE * (v + 0.044715 * (v * v * v)))
    return 0.5 * (1.0 + t) + 0.5 * v * (1.0 - t * t) * (SCALE * (1.0 + 3 * 0.044715 * (v * v)))


def kernel(
    section_ref, vision_ref, alternate_ref, grad_ref, parked_ref, wd_ref, wu_ref,
    o_section, o_parked, o_input_grad, o_up, o_down,
    sec, vis, alt, grad, fwd, bwd, out, weights, parts,
    pre_out, pre_in, act, slope_act, act_t, grad_t,
    opp_up, opp_dn, from_up, from_dn, opp2_up, opp2_dn, from2_up, from2_dn, sums,
    local_sem, g_send, g_recv, r_send, r_recv, m_send, m_recv, y_send, y_recv,
):
    section = lax.axis_index("section")
    dp = lax.axis_index("dp")
    mp = lax.axis_index("mp")
    x, z = lax.div(dp, NZ), lax.rem(dp, NZ)

    def at(value, count):
        return lax.rem(value + count, count)

    def chunk(xi, zi):
        return at(xi, NX) * NZ + at(zi, NZ)

    mirror = {"section": 15 - section}
    following = {"section": lax.rem(section + 1, 16)}
    preceding = {"section": lax.rem(section + 15, 16)}
    other = {"mp": 1 - mp}
    right, left = {"dp": chunk(x + 1, z)}, {"dp": chunk(x - 1, z)}
    plus, minus = {"dp": chunk(x, z + 1)}, {"dp": chunk(x, z - 1)}

    pending = []

    def remote(src, dst, send, recv, to):
        copy = pltpu.make_async_remote_copy(
            src_ref=src, dst_ref=dst, send_sem=send, recv_sem=recv,
            device_id=to, device_id_type=MESH,
        )
        return copy

    def go(copy):
        copy.start()
        pending.append(copy)

    w_refs = (wd_ref, wu_ref)
    loads = [
        pltpu.make_async_copy(section_ref, sec, local_sem.at[0]),
        pltpu.make_async_copy(vision_ref, vis, local_sem.at[1]),
        pltpu.make_async_copy(alternate_ref, alt, local_sem.at[2]),
        pltpu.make_async_copy(grad_ref, grad, local_sem.at[3]),
        pltpu.make_async_copy(wd_ref, weights.at[0, x, z], local_sem.at[4]),
        pltpu.make_async_copy(wu_ref, weights.at[1, x, z], local_sem.at[5]),
    ]
    for load in loads:
        load.start()

    barrier = pltpu.get_barrier_semaphore()
    for partner in (mirror, following, preceding, other, right, left, plus, minus):
        pl.semaphore_signal(barrier, inc=1, device_id=partner, device_id_type=MESH)
    pl.semaphore_wait(barrier, 8)

    def y_piece(src, dst, index, piece, to):
        cols = pl.ds(piece * PIECE, PIECE)
        return remote(
            src.at[:, cols], dst.at[:, cols], y_send.at[index], y_recv.at[index], to
        )

    parked_copies = [y_piece(parked_ref, bwd, i, i, mirror) for i in range(PIECES)]
    forward_copies = [y_piece(fwd, o_parked, PIECES + i, i, mirror) for i in range(PIECES)]
    shift_copies = [y_piece(out, o_section, 2 * PIECES + i, i, following) for i in range(PIECES)]
    for copy in parked_copies:
        go(copy)

    def forward_behind_parked(i):
        parked_copies[i].wait_recv()
        go(forward_copies[i])

    class Gather:
        def __init__(self, number, w, start, stop, x_first):
            self.base, self.w, self.start, self.stop = number * N_GATHER, w, start, stop
            self.x_first = x_first
            self.a, self.b = (x, z) if x_first else (z, x)
            xs, zs = (right, left), (plus, minus)
            (self.up, self.dn), (self.up2, self.dn2) = (xs, zs) if x_first else (zs, xs)
            middle = (start + stop) // 2
            self.all = pl.ds(start, stop - start)
            self.low, self.high = pl.ds(start, middle - start), pl.ds(middle, stop - middle)

        def copy(self, m, to, a=0, b=0, cols=None):
            cols = self.all if cols is None else cols
            a, b = at(self.a + a, 4), at(self.b + b, 4)
            xi, zi = (a, b) if self.x_first else (b, a)
            place = weights.at[self.w, xi, zi, :, cols]
            index = self.base + m
            return remote(place, place, g_send.at[index], g_recv.at[index], to)

        def start1(self):
            go(self.copy(0, self.up))
            go(self.copy(1, self.dn))

        def start2(self, k):
            go(self.copy(4 + k, self.up2, a=k))
            go(self.copy(8 + k, self.dn2, a=k))

        def near1(self):
            self.copy(0, self.up).wait_recv()
            go(self.copy(2, self.up, a=-1, cols=self.low))
            self.start2(3)
            self.copy(1, self.dn).wait_recv()
            go(self.copy(3, self.dn, a=1, cols=self.high))
            self.start2(1)

        def far1(self):
            self.copy(2, self.up, cols=self.low).wait_recv()
            self.copy(3, self.dn, cols=self.high).wait_recv()
            self.start2(2)

        def near2(self, k):
            self.copy(4 + k, self.up2).wait_recv()
            if k % 2 == 0:
                go(self.copy(12 + k // 2, self.up2, a=k, b=-1))
            self.copy(8 + k, self.dn2).wait_recv()
            if k % 2 == 1:
                go(self.copy(14 + k // 2, self.dn2, a=k, b=1))

        def far2(self, k):
            if k % 2 == 0:
                self.copy(12 + k // 2, self.up2).wait_recv()
            else:
                self.copy(14 + k // 2, self.dn2).wait_recv()

    down = Gather(0, 0, SPLIT, D, False)
    up = Gather(1, 1, SPLIT, D, False)
    both = Gather(2, slice(None), 0, SPLIT, True)

    def tile(i):
        return pl.ds(pl.multiple_of(i * TILE, TILE), TILE)

    def exchange(slot):
        return remote(
            pre_out.at[slot], pre_in.at[slot], m_send.at[slot], m_recv.at[slot], other
        )

    def weight(w, cols):
        block = weights[w, :, :, :, cols]
        return block.reshape(R, block.shape[-1])

    def partial(slot, rows, w):
        def body(i, total):
            cols = pl.ds(pl.multiple_of(i * 512, 512), 512)
            return total + lax.dot_general(
                rows[:, cols], weight(w, cols), NT, preferred_element_type=F32
            )

        total = lax.fori_loop(0, D // 512, body, jnp.zeros((ROWS, R), F32))
        pre_out[slot] = total.astype(BF16)
        go(exchange(slot))

    def summed(slot):
        exchange(slot).wait_recv()
        return pre_out[slot].astype(F32) + pre_in[slot].astype(F32)

    for load in loads[4:]:
        load.wait()
    down.start1()
    down.start2(0)
    both.start1()
    both.start2(0)
    up.start2(0)

    for load in loads[:3]:
        load.wait()
    picks = jnp.where(section == 0, alt[...], -1)
    chosen_t = (lax.broadcasted_iota(jnp.int32, (VISION, ROWS), 0) == picks).astype(BF16)
    hit = lax.dot_general(
        chosen_t, jnp.ones((VISION, TILE), BF16), TN, preferred_element_type=F32
    )

    def choose(i, carry):
        cols = tile(i)
        chosen = lax.dot_general(chosen_t, vis[:, cols], TN, preferred_element_type=F32)
        fwd[:, cols] = jnp.where(hit > 0.5, chosen, sec[:, cols].astype(F32)).astype(BF16)
        return carry

    lax.fori_loop(0, TILES, choose, 0)

    down.near1()
    up.start1()
    both.near1()
    down.near2(0)
    both.far1()
    both.near2(0)
    down.far1()
    down.near2(3)
    down.near2(1)
    both.near2(3)
    both.near2(1)
    up.near1()
    down.far2(0)
    down.near2(2)
    up.far1()
    both.near2(2)
    up.near2(0)
    up.near2(3)
    up.near2(1)
    up.far2(0)
    up.near2(2)
    forward_behind_parked(0)
    forward_behind_parked(1)
    for k in (3, 1, 2):
        down.far2(k)
    for k in (0, 3, 1, 2):
        both.far2(k)
    partial(0, fwd, 0)
    forward_behind_parked(2)
    forward_behind_parked(3)
    partial(2, bwd, 0)
    for k in (3, 1, 2):
        up.far2(k)
    loads[3].wait()
    partial(1, grad, 1)

    bwd_pre = summed(2)
    bwd_act = gelu(bwd_pre).astype(BF16)
    act_t[...] = bwd_act.T
    pre_grad = (summed(1) * gelu_slope(bwd_pre)).astype(BF16)
    slope_act[...] = pre_grad
    grad_t[...] = pre_grad.T

    def output(i, carry):
        cols = pl.ds(pl.multiple_of(i * 128, 128), 128)
        product = jnp.dot(act[...], weight(1, cols), preferred_element_type=F32)
        out[:, cols] = (fwd[:, cols].astype(F32) + product).astype(BF16)
        return carry

    def outputs():
        act[...] = gelu(summed(0)).astype(BF16)
        for i in range(PIECES):
            lax.fori_loop(i * PIECE // 128, (i + 1) * PIECE // 128, output, 0)
            go(shift_copies[i])

    def add_into(total, term):
        total[...] = (total[...].astype(F32) + term[...].astype(F32)).astype(BF16)

    class Reduce:
        def __init__(self, number, w, start, stop, x_first):
            self.base, self.w, self.start, self.stop = number * N_REDUCE, w, start, stop
            self.x_first = x_first
            self.a, self.b = (x, z) if x_first else (z, x)
            xs, zs = (right, left), (plus, minus)
            (self.up, self.dn), (self.up2, self.dn2) = (xs, zs) if x_first else (zs, xs)
            middle = (start + stop) // 2
            self.all = pl.ds(start, stop - start)
            self.low, self.high = pl.ds(start, middle - start), pl.ds(middle, stop - middle)

        def block(self, a, b0, count):
            a = at(self.a + a, 4)
            if self.x_first:
                return parts.at[self.w, a, pl.ds(b0, count), :, self.all]
            return parts.at[self.w, pl.ds(b0, count), a, :, self.all]

        def term(self, ref, b0, count):
            return ref.at[self.w, pl.ds(b0, count), :, self.all]

        def total(self, b, cols):
            return sums.at[self.w, at(self.b + b, 4), :, cols]

        def copy(self, m):
            w = self.w
            src, dst, to = (
                lambda: (self.block(2, 0, 2), self.term(opp_up, 0, 2), self.dn),
                lambda: (self.block(2, 2, 2), self.term(opp_dn, 0, 2), self.up),
                lambda: (self.block(-1, 2, 2), self.term(from_up, 2, 2), self.dn),
                lambda: (self.block(1, 0, 2), self.term(from_dn, 0, 2), self.up),
                lambda: (self.block(-1, 0, 2), self.term(from_up, 0, 2), self.dn),
                lambda: (self.block(1, 2, 2), self.term(from_dn, 2, 2), self.up),
                lambda: (self.total(2, self.low), opp2_up.at[w, :, self.low], self.dn2),
                lambda: (self.total(2, self.high), opp2_dn.at[w, :, self.high], self.up2),
                lambda: (self.total(-1, self.high), from2_up.at[w, :, self.high], self.dn2),
                lambda: (self.total(1, self.low), from2_dn.at[w, :, self.low], self.up2),
                lambda: (self.total(-1, self.low), from2_up.at[w, :, self.low], self.dn2),
                lambda: (self.total(1, self.high), from2_dn.at[w, :, self.high], self.up2),
            )[m]()
            index = self.base + m
            return remote(src, dst, r_send.at[index], r_recv.at[index], to)

        def stage_a(self):
            lhs, rhs = ((act_t, grad), (grad_t, bwd))[self.w]

            def body(i, carry):
                cols = tile(i)
                product = jnp.dot(lhs[...], rhs[:, cols], preferred_element_type=F32)
                parts[self.w, :, :, :, cols] = product.astype(BF16).reshape(NX, NZ, SHARE, TILE)
                return carry

            lax.fori_loop(self.start // TILE, self.stop // TILE, body, 0)
            for m in range(4):
                go(self.copy(m))

        def stage_b(self):
            self.copy(0).wait_recv()
            add_into(self.block(-1, 0, 2), self.term(opp_up, 0, 2))
            go(self.copy(4))
            self.copy(1).wait_recv()
            add_into(self.block(1, 2, 2), self.term(opp_dn, 0, 2))
            go(self.copy(5))

        def stage_c(self):
            for m in (2, 3, 4, 5):
                self.copy(m).wait_recv()
            self.term(sums, 0, 4)[...] = (
                self.block(0, 0, 4)[...].astype(F32)
                + self.term(from_up, 0, 4)[...].astype(F32)
                + self.term(from_dn, 0, 4)[...].astype(F32)
            ).astype(BF16)
            for m in (6, 7, 8, 9):
                go(self.copy(m))

        def stage_d(self):
            w = self.w
            self.copy(6).wait_recv()
            add_into(self.total(-1, self.low), opp2_up.at[w, :, self.low])
            go(self.copy(10))
            self.copy(7).wait_recv()
            add_into(self.total(1, self.high), opp2_dn.at[w, :, self.high])
            go(self.copy(11))

        def stage_e(self):
            w, cols = self.w, self.all
            for m in (8, 9, 10, 11):
                self.copy(m).wait_recv()
            total = (
                parts[w, x, z, :, cols].astype(F32)
                + from_up[w, self.b, :, cols].astype(F32)
                + from_dn[w, self.b, :, cols].astype(F32)
                + from2_up[w, :, cols].astype(F32)
                + from2_dn[w, :, cols].astype(F32)
            )
            (o_up, o_down)[w][:, cols] = (total * (1.0 / 16)).astype(BF16)

    def input_grad(i, carry):
        cols = tile(i)
        product = jnp.dot(slope_act[...], weight(0, cols), preferred_element_type=F32)
        o_input_grad[:, cols] = (grad[:, cols].astype(F32) + product).astype(BF16)
        return carry

    cut = SPLIT + 6 * TILE
    u0, u1 = Reduce(0, 0, SPLIT, cut, True), Reduce(1, 0, cut, D, True)
    d0, d1 = Reduce(2, 1, SPLIT, cut, True), Reduce(3, 1, cut, D, True)
    uz, dz = Reduce(4, 0, 0, SPLIT, False), Reduce(5, 1, 0, SPLIT, False)
    u0.stage_a()
    uz.stage_a()
    u1.stage_a()
    u0.stage_b()
    uz.stage_b()
    outputs()
    d0.stage_a()
    dz.stage_a()
    u1.stage_b()
    u0.stage_c()
    uz.stage_c()
    d1.stage_a()
    lax.fori_loop(0, TILES, input_grad, 0)
    d0.stage_b()
    u0.stage_d()
    uz.stage_d()
    dz.stage_b()
    u1.stage_c()
    u1.stage_d()
    dz.stage_c()
    u0.stage_e()
    uz.stage_e()
    d1.stage_b()
    d0.stage_c()
    dz.stage_d()
    d0.stage_d()
    u1.stage_e()
    d1.stage_c()
    d1.stage_d()
    dz.stage_e()
    d0.stage_e()
    d1.stage_e()

    for copy in forward_copies + shift_copies:
        copy.wait_recv()
    for copy in pending:
        copy.wait_send()


def write_out(*refs):
    copies = [
        pltpu.make_async_copy(refs[i], refs[5 + i], refs[10].at[i]) for i in range(5)
    ]
    for copy in copies:
        copy.start()
    for copy in copies:
        copy.wait()


def local(section_in, vision_rows, alternate, grad_in, parked, w_down, w_up):
    rows = jax.ShapeDtypeStruct((ROWS, D), BF16)
    shares = jax.ShapeDtypeStruct((SHARE, D), BF16)
    dma = pltpu.SemaphoreType.DMA
    outs = pl.pallas_call(
        kernel,
        out_shape=(pltpu.VMEM((ROWS, D), BF16),) * 3 + (pltpu.VMEM((SHARE, D), BF16),) * 2,
        in_specs=[pl.BlockSpec(memory_space=pltpu.HBM)] * 7,
        out_specs=[pl.BlockSpec(memory_space=pltpu.VMEM)] * 5,
        scratch_shapes=[
            pltpu.VMEM((ROWS, D), BF16),
            pltpu.VMEM((VISION, D), BF16),
            pltpu.VMEM((1, ROWS), jnp.int32),
            pltpu.VMEM((ROWS, D), BF16),
            pltpu.VMEM((ROWS, D), BF16),
            pltpu.VMEM((ROWS, D), BF16),
            pltpu.VMEM((ROWS, D), BF16),
            pltpu.VMEM((2, NX, NZ, SHARE, D), BF16),
            pltpu.VMEM((2, NX, NZ, SHARE, D), BF16),
            pltpu.VMEM((3, ROWS, R), BF16),
            pltpu.VMEM((3, ROWS, R), BF16),
            pltpu.VMEM((ROWS, R), BF16),
            pltpu.VMEM((ROWS, R), BF16),
            pltpu.VMEM((R, ROWS), BF16),
            pltpu.VMEM((R, ROWS), BF16),
            pltpu.VMEM((2, 2, SHARE, D), BF16),
            pltpu.VMEM((2, 2, SHARE, D), BF16),
            pltpu.VMEM((2, 4, SHARE, D), BF16),
            pltpu.VMEM((2, 4, SHARE, D), BF16),
            pltpu.VMEM((2, SHARE, D), BF16),
            pltpu.VMEM((2, SHARE, D), BF16),
            pltpu.VMEM((2, SHARE, D), BF16),
            pltpu.VMEM((2, SHARE, D), BF16),
            pltpu.VMEM((2, 4, SHARE, D), BF16),
            dma((6,)),
            dma((3 * N_GATHER,)),
            dma((3 * N_GATHER,)),
            dma((6 * N_REDUCE,)),
            dma((6 * N_REDUCE,)),
            dma((3,)),
            dma((3,)),
            dma((3 * PIECES,)),
            dma((3 * PIECES,)),
        ],
        compiler_params=pltpu.CompilerParams(
            collective_id=0, has_side_effects=True, vmem_limit_bytes=40 * 2**20
        ),
        cost_estimate=pl.CostEstimate(
            flops=14 * ROWS * D * R, bytes_accessed=12 * ROWS * D, transcendentals=3 * ROWS * R
        ),
        name="relay_tick",
    )(*(
        pltpu.with_memory_space_constraint(operand, pltpu.HBM)
        for operand in (
            section_in[0, 0], vision_rows[0], alternate, grad_in[0, 0], parked[0, 0],
            w_down[0], w_up[0],
        )
    ))
    received, stash, input_grad, up_grad, down_grad = pl.pallas_call(
        write_out,
        out_shape=(rows, rows, rows, shares, shares),
        in_specs=[pl.BlockSpec(memory_space=pltpu.VMEM)] * 5,
        out_specs=[pl.BlockSpec(memory_space=pltpu.HBM)] * 5,
        scratch_shapes=[dma((5,))],
        name="write_out",
    )(*(pltpu.with_memory_space_constraint(out, pltpu.VMEM) for out in outs))
    return (
        received[None, None],
        stash[None, None],
        input_grad[None, None],
        up_grad[None],
        down_grad[None],
    )


def solution(mesh):
    rows = P("section", "dp", None, "mp")
    shares = P("section", "dp", "mp")
    return jax.shard_map(
        local,
        mesh=mesh,
        in_specs=(rows, P("dp", None, "mp"), P("dp", None), rows, rows, shares, shares),
        out_specs=(rows, rows, rows, shares, shares),
        check_vma=False,
    )
```

```python
import functools
import math

import jax
import jax.numpy as jnp
from jax import lax
from jax.experimental import pallas as pl
from jax.experimental.pallas import tpu as pltpu
from jax.sharding import PartitionSpec as P

MESH = pl.DeviceIdType.MESH
BF16, F32 = jnp.bfloat16, jnp.float32

D = 3584
R = 256
ROWS = 104
VISION = 24
SHARE = 16
TILE = 256
PIECES = 4
PIECE = D // PIECES
TILES = D // TILE
NX, NZ = 4, 4
SPLIT = 3 * TILE

N_GATHER = 16
N_REDUCE = 12

NT = (((1,), (1,)), ((), ()))
TN = (((0,), (0,)), ((), ()))

SCALE = math.sqrt(2 / math.pi)


def gelu(v):
    return 0.5 * v * (1.0 + jnp.tanh(SCALE * (v + 0.044715 * (v * v * v))))


def gelu_slope(v):
    t = jnp.tanh(SCALE * (v + 0.044715 * (v * v * v)))
    return 0.5 * (1.0 + t) + 0.5 * v * (1.0 - t * t) * (SCALE * (1.0 + 3 * 0.044715 * (v * v)))


def kernel(
    section_ref, vision_ref, alternate_ref, grad_ref, parked_ref, wd_ref, wu_ref,
    o_section, o_parked, o_input_grad, o_up, o_down,
    sec, vis, alt, grad, fwd, bwd, out, weights, parts,
    pre_out, pre_in, act, slope_act, act_t, grad_t,
    opp_up, opp_dn, from_up, from_dn, opp2_up, opp2_dn, from2_up, from2_dn, sums,
    local_sem, g_send, g_recv, r_send, r_recv, m_send, m_recv, y_send, y_recv,
):
    section = lax.axis_index("section")
    dp = lax.axis_index("dp")
    mp = lax.axis_index("mp")
    x, z = lax.div(dp, NZ), lax.rem(dp, NZ)

    def at(value, count):
        return lax.rem(value + count, count)

    def chunk(xi, zi):
        return at(xi, NX) * NZ + at(zi, NZ)

    mirror = {"section": 15 - section}
    following = {"section": lax.rem(section + 1, 16)}
    preceding = {"section": lax.rem(section + 15, 16)}
    other = {"mp": 1 - mp}
    right, left = {"dp": chunk(x + 1, z)}, {"dp": chunk(x - 1, z)}
    plus, minus = {"dp": chunk(x, z + 1)}, {"dp": chunk(x, z - 1)}

    pending = []

    def remote(src, dst, send, recv, to):
        copy = pltpu.make_async_remote_copy(
            src_ref=src, dst_ref=dst, send_sem=send, recv_sem=recv,
            device_id=to, device_id_type=MESH,
        )
        return copy

    def go(copy):
        copy.start()
        pending.append(copy)

    w_refs = (wd_ref, wu_ref)
    loads = [
        pltpu.make_async_copy(section_ref, sec, local_sem.at[0]),
        pltpu.make_async_copy(vision_ref, vis, local_sem.at[1]),
        pltpu.make_async_copy(alternate_ref, alt, local_sem.at[2]),
        pltpu.make_async_copy(grad_ref, grad, local_sem.at[3]),
        pltpu.make_async_copy(wd_ref, weights.at[0, x, z], local_sem.at[4]),
        pltpu.make_async_copy(wu_ref, weights.at[1, x, z], local_sem.at[5]),
    ]
    for load in loads:
        load.start()

    barrier = pltpu.get_barrier_semaphore()
    for partner in (mirror, following, preceding, other, right, left, plus, minus):
        pl.semaphore_signal(barrier, inc=1, device_id=partner, device_id_type=MESH)
    pl.semaphore_wait(barrier, 8)

    def y_piece(src, dst, index, piece, to):
        cols = pl.ds(piece * PIECE, PIECE)
        return remote(
            src.at[:, cols], dst.at[:, cols], y_send.at[index], y_recv.at[index], to
        )

    parked_copies = [y_piece(parked_ref, bwd, i, i, mirror) for i in range(PIECES)]
    forward_copies = [y_piece(fwd, o_parked, PIECES + i, i, mirror) for i in range(PIECES)]
    shift_copies = [y_piece(out, o_section, 2 * PIECES + i, i, following) for i in range(PIECES)]
    for copy in parked_copies:
        go(copy)

    y = lax.div(section, 2)
    near = jnp.logical_or(lax.rem(y, 4) == 0, lax.rem(y, 4) == 3)

    def send_forward(pieces, when):
        @pl.when(when)
        def _():
            for i in pieces:
                forward_copies[i].start()

    class Gather:
        def __init__(self, number, w, start, stop, x_first):
            self.base, self.w, self.start, self.stop = number * N_GATHER, w, start, stop
            self.x_first = x_first
            self.a, self.b = (x, z) if x_first else (z, x)
            xs, zs = (right, left), (plus, minus)
            (self.up, self.dn), (self.up2, self.dn2) = (xs, zs) if x_first else (zs, xs)
            middle = (start + stop) // 2
            self.all = pl.ds(start, stop - start)
            self.low, self.high = pl.ds(start, middle - start), pl.ds(middle, stop - middle)

        def copy(self, m, to, a=0, b=0, cols=None):
            cols = self.all if cols is None else cols
            a, b = at(self.a + a, 4), at(self.b + b, 4)
            xi, zi = (a, b) if self.x_first else (b, a)
            place = weights.at[self.w, xi, zi, :, cols]
            index = self.base + m
            return remote(place, place, g_send.at[index], g_recv.at[index], to)

        def start1(self):
            go(self.copy(0, self.up))
            go(self.copy(1, self.dn))

        def start2(self, k):
            go(self.copy(4 + k, self.up2, a=k))
            go(self.copy(8 + k, self.dn2, a=k))

        def near1(self):
            self.copy(0, self.up).wait_recv()
            go(self.copy(2, self.up, a=-1, cols=self.low))
            self.start2(3)
            self.copy(1, self.dn).wait_recv()
            go(self.copy(3, self.dn, a=1, cols=self.high))
            self.start2(1)

        def far1(self):
            self.copy(2, self.up, cols=self.low).wait_recv()
            self.copy(3, self.dn, cols=self.high).wait_recv()
            self.start2(2)

        def near2(self, k):
            self.copy(4 + k, self.up2).wait_recv()
            if k % 2 == 0:
                go(self.copy(12 + k // 2, self.up2, a=k, b=-1))
            self.copy(8 + k, self.dn2).wait_recv()
            if k % 2 == 1:
                go(self.copy(14 + k // 2, self.dn2, a=k, b=1))

        def far2(self, k):
            if k % 2 == 0:
                self.copy(12 + k // 2, self.up2).wait_recv()
            else:
                self.copy(14 + k // 2, self.dn2).wait_recv()

    down = Gather(0, 0, SPLIT, D, False)
    up = Gather(1, 1, SPLIT, D, False)
    both = Gather(2, slice(None), 0, SPLIT, True)

    def tile(i):
        return pl.ds(pl.multiple_of(i * TILE, TILE), TILE)

    def exchange(slot):
        return remote(
            pre_out.at[slot], pre_in.at[slot], m_send.at[slot], m_recv.at[slot], other
        )

    def weight(w, cols):
        block = weights[w, :, :, :, cols]
        return block.reshape(R, block.shape[-1])

    def partial(slot, rows, w):
        def body(i, total):
            cols = pl.ds(pl.multiple_of(i * 512, 512), 512)
            return total + lax.dot_general(
                rows[:, cols], weight(w, cols), NT, preferred_element_type=F32
            )

        send_partial(slot, lax.fori_loop(0, D // 512, body, jnp.zeros((ROWS, R), F32)))

    def send_partial(slot, total):
        pre_out[slot] = total.astype(BF16)
        go(exchange(slot))

    def summed(slot):
        exchange(slot).wait_recv()
        return pre_out[slot].astype(F32) + pre_in[slot].astype(F32)

    for load in loads[4:]:
        load.wait()
    down.start1()
    down.start2(0)
    both.start1()
    both.start2(0)
    up.start2(0)

    for load in loads[:3]:
        load.wait()
    picks = jnp.where(section == 0, alt[...], -1)
    chosen_t = (lax.broadcasted_iota(jnp.int32, (VISION, ROWS), 0) == picks).astype(BF16)
    hit = lax.dot_general(
        chosen_t, jnp.ones((VISION, TILE), BF16), TN, preferred_element_type=F32
    )

    def choose(i, carry):
        cols = tile(i)
        chosen = lax.dot_general(chosen_t, vis[:, cols], TN, preferred_element_type=F32)
        fwd[:, cols] = jnp.where(hit > 0.5, chosen, sec[:, cols].astype(F32)).astype(BF16)
        return carry

    lax.fori_loop(0, TILES, choose, 0)

    down.near1()
    up.start1()
    both.near1()
    down.near2(0)
    both.far1()
    both.near2(0)
    down.far1()
    down.near2(3)
    down.near2(1)
    both.near2(3)
    both.near2(1)
    up.near1()
    down.far2(0)
    down.near2(2)
    up.far1()
    both.near2(2)
    up.near2(0)
    up.near2(3)
    up.near2(1)
    up.far2(0)
    up.near2(2)
    for k in (3, 1, 2):
        down.far2(k)
    for k in (0, 3, 1, 2):
        both.far2(k)
    partial(0, fwd, 0)
    for k in (3, 1, 2):
        up.far2(k)
    loads[3].wait()
    partial(1, grad, 1)

    total = jnp.zeros((ROWS, R), F32)
    for i in range(PIECES):
        parked_copies[i].wait_recv()
        send_forward([i], near)
        cols = pl.ds(i * PIECE, PIECE)
        total += lax.dot_general(bwd[:, cols], weight(0, cols), NT, preferred_element_type=F32)
    send_partial(2, total)

    bwd_pre = summed(2)
    bwd_act = gelu(bwd_pre).astype(BF16)
    act_t[...] = bwd_act.T
    pre_grad = (summed(1) * gelu_slope(bwd_pre)).astype(BF16)
    slope_act[...] = pre_grad
    grad_t[...] = pre_grad.T

    def output(i, carry):
        cols = pl.ds(pl.multiple_of(i * 128, 128), 128)
        product = jnp.dot(act[...], weight(1, cols), preferred_element_type=F32)
        out[:, cols] = (fwd[:, cols].astype(F32) + product).astype(BF16)
        return carry

    def outputs(i):
        lax.fori_loop(i * PIECE // 128, (i + 1) * PIECE // 128, output, 0)
        go(shift_copies[i])

    def add_into(total, term):
        total[...] = (total[...].astype(F32) + term[...].astype(F32)).astype(BF16)

    class Reduce:
        def __init__(self, number, w, start, stop, x_first):
            self.base, self.w, self.start, self.stop = number * N_REDUCE, w, start, stop
            self.x_first = x_first
            self.a, self.b = (x, z) if x_first else (z, x)
            xs, zs = (right, left), (plus, minus)
            (self.up, self.dn), (self.up2, self.dn2) = (xs, zs) if x_first else (zs, xs)
            middle = (start + stop) // 2
            self.all = pl.ds(start, stop - start)
            self.low, self.high = pl.ds(start, middle - start), pl.ds(middle, stop - middle)

        def block(self, a, b0, count):
            a = at(self.a + a, 4)
            if self.x_first:
                return parts.at[self.w, a, pl.ds(b0, count), :, self.all]
            return parts.at[self.w, pl.ds(b0, count), a, :, self.all]

        def term(self, ref, b0, count):
            return ref.at[self.w, pl.ds(b0, count), :, self.all]

        def total(self, b, cols):
            return sums.at[self.w, at(self.b + b, 4), :, cols]

        def copy(self, m):
            w = self.w
            src, dst, to = (
                lambda: (self.block(2, 0, 2), self.term(opp_up, 0, 2), self.dn),
                lambda: (self.block(2, 2, 2), self.term(opp_dn, 0, 2), self.up),
                lambda: (self.block(-1, 2, 2), self.term(from_up, 2, 2), self.dn),
                lambda: (self.block(1, 0, 2), self.term(from_dn, 0, 2), self.up),
                lambda: (self.block(-1, 0, 2), self.term(from_up, 0, 2), self.dn),
                lambda: (self.block(1, 2, 2), self.term(from_dn, 2, 2), self.up),
                lambda: (self.total(2, self.low), opp2_up.at[w, :, self.low], self.dn2),
                lambda: (self.total(2, self.high), opp2_dn.at[w, :, self.high], self.up2),
                lambda: (self.total(-1, self.high), from2_up.at[w, :, self.high], self.dn2),
                lambda: (self.total(1, self.low), from2_dn.at[w, :, self.low], self.up2),
                lambda: (self.total(-1, self.low), from2_up.at[w, :, self.low], self.dn2),
                lambda: (self.total(1, self.high), from2_dn.at[w, :, self.high], self.up2),
            )[m]()
            index = self.base + m
            return remote(src, dst, r_send.at[index], r_recv.at[index], to)

        def stage_a(self):
            lhs, rhs = ((act_t, grad), (grad_t, bwd))[self.w]

            def body(i, carry):
                cols = tile(i)
                product = jnp.dot(lhs[...], rhs[:, cols], preferred_element_type=F32)
                parts[self.w, :, :, :, cols] = product.astype(BF16).reshape(NX, NZ, SHARE, TILE)
                return carry

            lax.fori_loop(self.start // TILE, self.stop // TILE, body, 0)
            for m in range(4):
                go(self.copy(m))

        def stage_b(self):
            self.copy(0).wait_recv()
            add_into(self.block(-1, 0, 2), self.term(opp_up, 0, 2))
            go(self.copy(4))
            self.copy(1).wait_recv()
            add_into(self.block(1, 2, 2), self.term(opp_dn, 0, 2))
            go(self.copy(5))

        def stage_c(self):
            for m in (2, 3, 4, 5):
                self.copy(m).wait_recv()
            self.term(sums, 0, 4)[...] = (
                self.block(0, 0, 4)[...].astype(F32)
                + self.term(from_up, 0, 4)[...].astype(F32)
                + self.term(from_dn, 0, 4)[...].astype(F32)
            ).astype(BF16)
            for m in (6, 7, 8, 9):
                go(self.copy(m))

        def stage_d(self):
            w = self.w
            self.copy(6).wait_recv()
            add_into(self.total(-1, self.low), opp2_up.at[w, :, self.low])
            go(self.copy(10))
            self.copy(7).wait_recv()
            add_into(self.total(1, self.high), opp2_dn.at[w, :, self.high])
            go(self.copy(11))

        def stage_e(self):
            w, cols = self.w, self.all
            for m in (8, 9, 10, 11):
                self.copy(m).wait_recv()
            total = (
                parts[w, x, z, :, cols].astype(F32)
                + from_up[w, self.b, :, cols].astype(F32)
                + from_dn[w, self.b, :, cols].astype(F32)
                + from2_up[w, :, cols].astype(F32)
                + from2_dn[w, :, cols].astype(F32)
            )
            (o_up, o_down)[w][:, cols] = (total * (1.0 / 16)).astype(BF16)

    def input_grad(i, carry):
        cols = tile(i)
        product = jnp.dot(slope_act[...], weight(0, cols), preferred_element_type=F32)
        o_input_grad[:, cols] = (grad[:, cols].astype(F32) + product).astype(BF16)
        return carry

    cut = SPLIT + 6 * TILE
    u0, u1 = Reduce(0, 0, SPLIT, cut, True), Reduce(1, 0, cut, D, True)
    d0, d1 = Reduce(2, 1, SPLIT, cut, True), Reduce(3, 1, cut, D, True)
    uz, dz = Reduce(4, 0, 0, SPLIT, False), Reduce(5, 1, 0, SPLIT, False)
    u0.stage_a()
    uz.stage_a()
    u1.stage_a()
    act[...] = gelu(summed(0)).astype(BF16)
    u0.stage_b()
    send_forward(range(PIECES), jnp.logical_not(near))
    uz.stage_b()
    d0.stage_a()
    outputs(0)
    dz.stage_a()
    u1.stage_b()
    u0.stage_c()
    uz.stage_c()
    outputs(1)
    d1.stage_a()
    outputs(2)
    d0.stage_b()
    u0.stage_d()
    uz.stage_d()
    outputs(3)
    dz.stage_b()
    u1.stage_c()
    u1.stage_d()
    dz.stage_c()
    lax.fori_loop(0, TILES // 2, input_grad, 0)
    d1.stage_b()
    d0.stage_c()
    u0.stage_e()
    uz.stage_e()
    dz.stage_d()
    d0.stage_d()
    u1.stage_e()
    lax.fori_loop(TILES // 2, TILES, input_grad, 0)
    d1.stage_c()
    d1.stage_d()
    dz.stage_e()
    d0.stage_e()
    d1.stage_e()

    for copy in forward_copies + shift_copies:
        copy.wait_recv()
    for copy in pending + forward_copies:
        copy.wait_send()


def write_out(*refs):
    copies = [
        pltpu.make_async_copy(refs[i], refs[5 + i], refs[10].at[i]) for i in range(5)
    ]
    for copy in copies:
        copy.start()
    for copy in copies:
        copy.wait()


def local(section_in, vision_rows, alternate, grad_in, parked, w_down, w_up):
    rows = jax.ShapeDtypeStruct((ROWS, D), BF16)
    shares = jax.ShapeDtypeStruct((SHARE, D), BF16)
    dma = pltpu.SemaphoreType.DMA
    outs = pl.pallas_call(
        kernel,
        out_shape=(pltpu.VMEM((ROWS, D), BF16),) * 3 + (pltpu.VMEM((SHARE, D), BF16),) * 2,
        in_specs=[pl.BlockSpec(memory_space=pltpu.HBM)] * 7,
        out_specs=[pl.BlockSpec(memory_space=pltpu.VMEM)] * 5,
        scratch_shapes=[
            pltpu.VMEM((ROWS, D), BF16),
            pltpu.VMEM((VISION, D), BF16),
            pltpu.VMEM((1, ROWS), jnp.int32),
            pltpu.VMEM((ROWS, D), BF16),
            pltpu.VMEM((ROWS, D), BF16),
            pltpu.VMEM((ROWS, D), BF16),
            pltpu.VMEM((ROWS, D), BF16),
            pltpu.VMEM((2, NX, NZ, SHARE, D), BF16),
            pltpu.VMEM((2, NX, NZ, SHARE, D), BF16),
            pltpu.VMEM((3, ROWS, R), BF16),
            pltpu.VMEM((3, ROWS, R), BF16),
            pltpu.VMEM((ROWS, R), BF16),
            pltpu.VMEM((ROWS, R), BF16),
            pltpu.VMEM((R, ROWS), BF16),
            pltpu.VMEM((R, ROWS), BF16),
            pltpu.VMEM((2, 2, SHARE, D), BF16),
            pltpu.VMEM((2, 2, SHARE, D), BF16),
            pltpu.VMEM((2, 4, SHARE, D), BF16),
            pltpu.VMEM((2, 4, SHARE, D), BF16),
            pltpu.VMEM((2, SHARE, D), BF16),
            pltpu.VMEM((2, SHARE, D), BF16),
            pltpu.VMEM((2, SHARE, D), BF16),
            pltpu.VMEM((2, SHARE, D), BF16),
            pltpu.VMEM((2, 4, SHARE, D), BF16),
            dma((6,)),
            dma((3 * N_GATHER,)),
            dma((3 * N_GATHER,)),
            dma((6 * N_REDUCE,)),
            dma((6 * N_REDUCE,)),
            dma((3,)),
            dma((3,)),
            dma((3 * PIECES,)),
            dma((3 * PIECES,)),
        ],
        compiler_params=pltpu.CompilerParams(
            collective_id=0, has_side_effects=True, vmem_limit_bytes=40 * 2**20
        ),
        cost_estimate=pl.CostEstimate(
            flops=14 * ROWS * D * R, bytes_accessed=12 * ROWS * D, transcendentals=3 * ROWS * R
        ),
        name="relay_tick",
    )(*(
        pltpu.with_memory_space_constraint(operand, pltpu.HBM)
        for operand in (
            section_in[0, 0], vision_rows[0], alternate, grad_in[0, 0], parked[0, 0],
            w_down[0], w_up[0],
        )
    ))
    received, stash, input_grad, up_grad, down_grad = pl.pallas_call(
        write_out,
        out_shape=(rows, rows, rows, shares, shares),
        in_specs=[pl.BlockSpec(memory_space=pltpu.VMEM)] * 5,
        out_specs=[pl.BlockSpec(memory_space=pltpu.HBM)] * 5,
        scratch_shapes=[dma((5,))],
        name="write_out",
    )(*(pltpu.with_memory_space_constraint(out, pltpu.VMEM) for out in outs))
    return (
        received[None, None],
        stash[None, None],
        input_grad[None, None],
        up_grad[None],
        down_grad[None],
    )


def solution(mesh):
    rows = P("section", "dp", None, "mp")
    shares = P("section", "dp", "mp")
    return jax.shard_map(
        local,
        mesh=mesh,
        in_specs=(rows, P("dp", None, "mp"), P("dp", None), rows, rows, shares, shares),
        out_specs=(rows, rows, rows, shares, shares),
        check_vma=False,
    )
```

```python
import functools
import math

import jax
import jax.numpy as jnp
from jax import lax
from jax.experimental import pallas as pl
from jax.experimental.pallas import tpu as pltpu
from jax.sharding import PartitionSpec as P

MESH = pl.DeviceIdType.MESH
BF16, F32 = jnp.bfloat16, jnp.float32

D = 3584
R = 256
ROWS = 104
VISION = 24
SHARE = 16
TILE = 256
PIECES = 4
PIECE = D // PIECES
NX, NZ = 4, 4
SPLIT = 3 * TILE

N_GATHER = 16
N_REDUCE = 12

NT = (((1,), (1,)), ((), ()))
TN = (((0,), (0,)), ((), ()))

SCALE = math.sqrt(2 / math.pi)


def gelu(v):
    return 0.5 * v * (1.0 + jnp.tanh(SCALE * (v + 0.044715 * (v * v * v))))


def gelu_slope(v):
    t = jnp.tanh(SCALE * (v + 0.044715 * (v * v * v)))
    return 0.5 * (1.0 + t) + 0.5 * v * (1.0 - t * t) * (SCALE * (1.0 + 3 * 0.044715 * (v * v)))


def kernel(
    section_ref, vision_ref, alternate_ref, grad_ref, parked_ref, wd_ref, wu_ref,
    o_section, o_parked, o_input_grad, o_up, o_down,
    sec, vis, alt, grad, fwd, bwd, out, weights, parts,
    pre_out, pre_in, act, slope_act, act_t, grad_t,
    opp_up, opp_dn, from_up, from_dn, opp2_up, opp2_dn, from2_up, from2_dn, sums,
    local_sem, g_send, g_recv, r_send, r_recv, m_send, m_recv, y_send, y_recv,
):
    section = lax.axis_index("section")
    dp = lax.axis_index("dp")
    mp = lax.axis_index("mp")
    x, z = lax.div(dp, NZ), lax.rem(dp, NZ)

    def at(value, count):
        return lax.rem(value + count, count)

    def chunk(xi, zi):
        return at(xi, NX) * NZ + at(zi, NZ)

    mirror = {"section": 15 - section}
    following = {"section": lax.rem(section + 1, 16)}
    preceding = {"section": lax.rem(section + 15, 16)}
    other = {"mp": 1 - mp}
    right, left = {"dp": chunk(x + 1, z)}, {"dp": chunk(x - 1, z)}
    plus, minus = {"dp": chunk(x, z + 1)}, {"dp": chunk(x, z - 1)}

    pending = []

    def remote(src, dst, send, recv, to):
        copy = pltpu.make_async_remote_copy(
            src_ref=src, dst_ref=dst, send_sem=send, recv_sem=recv,
            device_id=to, device_id_type=MESH,
        )
        return copy

    def go(copy):
        copy.start()
        pending.append(copy)

    w_refs = (wd_ref, wu_ref)
    loads = [
        pltpu.make_async_copy(section_ref, sec, local_sem.at[0]),
        pltpu.make_async_copy(vision_ref, vis, local_sem.at[1]),
        pltpu.make_async_copy(alternate_ref, alt, local_sem.at[2]),
        pltpu.make_async_copy(grad_ref, grad, local_sem.at[3]),
        pltpu.make_async_copy(wd_ref, weights.at[0, x, z], local_sem.at[4]),
        pltpu.make_async_copy(wu_ref, weights.at[1, x, z], local_sem.at[5]),
    ]
    for load in loads:
        load.start()

    barrier = pltpu.get_barrier_semaphore()
    for partner in (mirror, following, preceding, other, right, left, plus, minus):
        pl.semaphore_signal(barrier, inc=1, device_id=partner, device_id_type=MESH)
    pl.semaphore_wait(barrier, 8)

    def y_piece(src, dst, index, piece, to):
        cols = pl.ds(piece * PIECE, PIECE)
        return remote(
            src.at[:, cols], dst.at[:, cols], y_send.at[index], y_recv.at[index], to
        )

    parked_copies = [y_piece(parked_ref, bwd, i, i, mirror) for i in range(PIECES)]
    forward_copies = [y_piece(fwd, o_parked, PIECES + i, i, mirror) for i in range(PIECES)]
    shift_copies = [y_piece(out, o_section, 2 * PIECES + i, i, following) for i in range(PIECES)]
    for copy in parked_copies:
        go(copy)

    y = lax.div(section, 2)
    near = jnp.logical_or(lax.rem(y, 4) == 0, lax.rem(y, 4) == 3)

    def send_forward(pieces, when):
        @pl.when(when)
        def _():
            for i in pieces:
                forward_copies[i].start()

    class Gather:
        def __init__(self, number, w, start, stop, x_first):
            self.base, self.w, self.start, self.stop = number * N_GATHER, w, start, stop
            self.x_first = x_first
            self.a, self.b = (x, z) if x_first else (z, x)
            xs, zs = (right, left), (plus, minus)
            (self.up, self.dn), (self.up2, self.dn2) = (xs, zs) if x_first else (zs, xs)
            middle = (start + stop) // 2
            self.all = pl.ds(start, stop - start)
            self.low, self.high = pl.ds(start, middle - start), pl.ds(middle, stop - middle)

        def copy(self, m, to, a=0, b=0, cols=None):
            cols = self.all if cols is None else cols
            a, b = at(self.a + a, 4), at(self.b + b, 4)
            xi, zi = (a, b) if self.x_first else (b, a)
            place = weights.at[self.w, xi, zi, :, cols]
            index = self.base + m
            return remote(place, place, g_send.at[index], g_recv.at[index], to)

        def start1(self):
            go(self.copy(0, self.up))
            go(self.copy(1, self.dn))

        def start2(self, k):
            go(self.copy(4 + k, self.up2, a=k))
            go(self.copy(8 + k, self.dn2, a=k))

        def near1(self):
            self.copy(0, self.up).wait_recv()
            go(self.copy(2, self.up, a=-1, cols=self.low))
            self.start2(3)
            self.copy(1, self.dn).wait_recv()
            go(self.copy(3, self.dn, a=1, cols=self.high))
            self.start2(1)

        def far1(self):
            self.copy(2, self.up, cols=self.low).wait_recv()
            self.copy(3, self.dn, cols=self.high).wait_recv()
            self.start2(2)

        def near2(self, k):
            self.copy(4 + k, self.up2).wait_recv()
            if k % 2 == 0:
                go(self.copy(12 + k // 2, self.up2, a=k, b=-1))
            self.copy(8 + k, self.dn2).wait_recv()
            if k % 2 == 1:
                go(self.copy(14 + k // 2, self.dn2, a=k, b=1))

        def far2(self, k):
            if k % 2 == 0:
                self.copy(12 + k // 2, self.up2).wait_recv()
            else:
                self.copy(14 + k // 2, self.dn2).wait_recv()

    down = Gather(0, 0, SPLIT, D, False)
    up = Gather(1, 1, SPLIT, D, False)
    both = Gather(2, slice(None), 0, SPLIT, True)

    def piece(i):
        return pl.ds(i * PIECE, PIECE)

    def exchange(slot):
        return remote(
            pre_out.at[slot], pre_in.at[slot], m_send.at[slot], m_recv.at[slot], other
        )

    def weight(w, cols):
        block = weights[w, :, :, :, cols]
        return block.reshape(R, block.shape[-1])

    def partial(slot, rows, w):
        total = jnp.zeros((ROWS, R), F32)
        for i in range(PIECES):
            total += lax.dot_general(
                rows[:, piece(i)], weight(w, piece(i)), NT, preferred_element_type=F32
            )
        send_partial(slot, total)

    def send_partial(slot, total):
        pre_out[slot] = total.astype(BF16)
        go(exchange(slot))

    def summed(slot):
        exchange(slot).wait_recv()
        return pre_out[slot].astype(F32) + pre_in[slot].astype(F32)

    for load in loads[4:]:
        load.wait()
    down.start1()
    down.start2(0)
    both.start1()
    both.start2(0)
    up.start2(0)

    for load in loads[:3]:
        load.wait()
    picks = jnp.where(section == 0, alt[...], -1)
    chosen_t = (lax.broadcasted_iota(jnp.int32, (VISION, ROWS), 0) == picks).astype(BF16)
    hit = lax.dot_general(
        chosen_t, jnp.ones((VISION, PIECE), BF16), TN, preferred_element_type=F32
    )

    for i in range(PIECES):
        cols = piece(i)
        chosen = lax.dot_general(chosen_t, vis[:, cols], TN, preferred_element_type=F32)
        fwd[:, cols] = jnp.where(hit > 0.5, chosen, sec[:, cols].astype(F32)).astype(BF16)

    down.near1()
    up.start1()
    both.near1()
    down.near2(0)
    both.far1()
    both.near2(0)
    down.far1()
    down.near2(3)
    down.near2(1)
    both.near2(3)
    both.near2(1)
    up.near1()
    down.far2(0)
    down.near2(2)
    up.far1()
    both.near2(2)
    up.near2(0)
    up.near2(3)
    up.near2(1)
    up.far2(0)
    up.near2(2)
    for k in (3, 1, 2):
        down.far2(k)
    for k in (0, 3, 1, 2):
        both.far2(k)
    partial(0, fwd, 0)
    for k in (3, 1, 2):
        up.far2(k)
    loads[3].wait()
    partial(1, grad, 1)

    total = jnp.zeros((ROWS, R), F32)
    for i in range(PIECES):
        parked_copies[i].wait_recv()
        send_forward([i], near)
        cols = piece(i)
        total += lax.dot_general(bwd[:, cols], weight(0, cols), NT, preferred_element_type=F32)
    send_partial(2, total)

    bwd_pre = summed(2)
    bwd_act = gelu(bwd_pre).astype(BF16)
    act_t[...] = bwd_act.T
    pre_grad = (summed(1) * gelu_slope(bwd_pre)).astype(BF16)
    slope_act[...] = pre_grad
    grad_t[...] = pre_grad.T

    def outputs(i):
        cols = piece(i)
        product = jnp.dot(act[...], weight(1, cols), preferred_element_type=F32)
        out[:, cols] = (fwd[:, cols].astype(F32) + product).astype(BF16)
        go(shift_copies[i])

    def add_into(total, term):
        total[...] = (total[...].astype(F32) + term[...].astype(F32)).astype(BF16)

    class Reduce:
        def __init__(self, number, w, start, stop, x_first):
            self.base, self.w, self.start, self.stop = number * N_REDUCE, w, start, stop
            self.x_first = x_first
            self.a, self.b = (x, z) if x_first else (z, x)
            xs, zs = (right, left), (plus, minus)
            (self.up, self.dn), (self.up2, self.dn2) = (xs, zs) if x_first else (zs, xs)
            middle = (start + stop) // 2
            self.all = pl.ds(start, stop - start)
            self.low, self.high = pl.ds(start, middle - start), pl.ds(middle, stop - middle)

        def block(self, a, b0, count):
            a = at(self.a + a, 4)
            if self.x_first:
                return parts.at[self.w, a, pl.ds(b0, count), :, self.all]
            return parts.at[self.w, pl.ds(b0, count), a, :, self.all]

        def term(self, ref, b0, count):
            return ref.at[self.w, pl.ds(b0, count), :, self.all]

        def total(self, b, cols):
            return sums.at[self.w, at(self.b + b, 4), :, cols]

        def copy(self, m):
            w = self.w
            src, dst, to = (
                lambda: (self.block(2, 0, 2), self.term(opp_up, 0, 2), self.dn),
                lambda: (self.block(2, 2, 2), self.term(opp_dn, 0, 2), self.up),
                lambda: (self.block(-1, 2, 2), self.term(from_up, 2, 2), self.dn),
                lambda: (self.block(1, 0, 2), self.term(from_dn, 0, 2), self.up),
                lambda: (self.block(-1, 0, 2), self.term(from_up, 0, 2), self.dn),
                lambda: (self.block(1, 2, 2), self.term(from_dn, 2, 2), self.up),
                lambda: (self.total(2, self.low), opp2_up.at[w, :, self.low], self.dn2),
                lambda: (self.total(2, self.high), opp2_dn.at[w, :, self.high], self.up2),
                lambda: (self.total(-1, self.high), from2_up.at[w, :, self.high], self.dn2),
                lambda: (self.total(1, self.low), from2_dn.at[w, :, self.low], self.up2),
                lambda: (self.total(-1, self.low), from2_up.at[w, :, self.low], self.dn2),
                lambda: (self.total(1, self.high), from2_dn.at[w, :, self.high], self.up2),
            )[m]()
            index = self.base + m
            return remote(src, dst, r_send.at[index], r_recv.at[index], to)

        def stage_a(self):
            lhs, rhs = ((act_t, grad), (grad_t, bwd))[self.w]

            steps = max(1, (self.stop - self.start) // 640)
            width = (self.stop - self.start) // steps
            for i in range(steps):
                cols = pl.ds(self.start + i * width, width)
                product = jnp.dot(lhs[...], rhs[:, cols], preferred_element_type=F32)
                parts[self.w, :, :, :, cols] = product.astype(BF16).reshape(NX, NZ, SHARE, width)
            for m in range(4):
                go(self.copy(m))

        def stage_b(self):
            self.copy(0).wait_recv()
            add_into(self.block(-1, 0, 2), self.term(opp_up, 0, 2))
            go(self.copy(4))
            self.copy(1).wait_recv()
            add_into(self.block(1, 2, 2), self.term(opp_dn, 0, 2))
            go(self.copy(5))

        def stage_c(self):
            for m in (2, 3, 4, 5):
                self.copy(m).wait_recv()
            self.term(sums, 0, 4)[...] = (
                self.block(0, 0, 4)[...].astype(F32)
                + self.term(from_up, 0, 4)[...].astype(F32)
                + self.term(from_dn, 0, 4)[...].astype(F32)
            ).astype(BF16)
            for m in (6, 7, 8, 9):
                go(self.copy(m))

        def stage_d(self):
            w = self.w
            self.copy(6).wait_recv()
            add_into(self.total(-1, self.low), opp2_up.at[w, :, self.low])
            go(self.copy(10))
            self.copy(7).wait_recv()
            add_into(self.total(1, self.high), opp2_dn.at[w, :, self.high])
            go(self.copy(11))

        def stage_e(self):
            w, cols = self.w, self.all
            for m in (8, 9, 10, 11):
                self.copy(m).wait_recv()
            total = (
                parts[w, x, z, :, cols].astype(F32)
                + from_up[w, self.b, :, cols].astype(F32)
                + from_dn[w, self.b, :, cols].astype(F32)
                + from2_up[w, :, cols].astype(F32)
                + from2_dn[w, :, cols].astype(F32)
            )
            (o_up, o_down)[w][:, cols] = (total * (1.0 / 16)).astype(BF16)

    def input_grad(i):
        cols = piece(i)
        product = jnp.dot(slope_act[...], weight(0, cols), preferred_element_type=F32)
        o_input_grad[:, cols] = (grad[:, cols].astype(F32) + product).astype(BF16)

    cut = SPLIT + 6 * TILE
    u0, u1 = Reduce(0, 0, SPLIT, cut, True), Reduce(1, 0, cut, D, True)
    d0, d1 = Reduce(2, 1, SPLIT, cut, True), Reduce(3, 1, cut, D, True)
    uz, dz = Reduce(4, 0, 0, SPLIT, False), Reduce(5, 1, 0, SPLIT, False)
    u0.stage_a()
    uz.stage_a()
    u1.stage_a()
    act[...] = gelu(summed(0)).astype(BF16)
    u0.stage_b()
    send_forward(range(PIECES), jnp.logical_not(near))
    uz.stage_b()
    d0.stage_a()
    outputs(0)
    dz.stage_a()
    u1.stage_b()
    u0.stage_c()
    uz.stage_c()
    outputs(1)
    d1.stage_a()
    outputs(2)
    d0.stage_b()
    u0.stage_d()
    uz.stage_d()
    outputs(3)
    dz.stage_b()
    u1.stage_c()
    u1.stage_d()
    dz.stage_c()
    input_grad(0)
    input_grad(1)
    d1.stage_b()
    d0.stage_c()
    u0.stage_e()
    uz.stage_e()
    dz.stage_d()
    d0.stage_d()
    u1.stage_e()
    input_grad(2)
    input_grad(3)
    d1.stage_c()
    d1.stage_d()
    dz.stage_e()
    d0.stage_e()
    d1.stage_e()

    for copy in forward_copies + shift_copies:
        copy.wait_recv()
    for copy in pending + forward_copies:
        copy.wait_send()


def write_out(*refs):
    copies = [
        pltpu.make_async_copy(refs[i], refs[5 + i], refs[10].at[i]) for i in range(5)
    ]
    for copy in copies:
        copy.start()
    for copy in copies:
        copy.wait()


def local(section_in, vision_rows, alternate, grad_in, parked, w_down, w_up):
    rows = jax.ShapeDtypeStruct((ROWS, D), BF16)
    shares = jax.ShapeDtypeStruct((SHARE, D), BF16)
    dma = pltpu.SemaphoreType.DMA
    outs = pl.pallas_call(
        kernel,
        out_shape=(pltpu.VMEM((ROWS, D), BF16),) * 3 + (pltpu.VMEM((SHARE, D), BF16),) * 2,
        in_specs=[pl.BlockSpec(memory_space=pltpu.HBM)] * 7,
        out_specs=[pl.BlockSpec(memory_space=pltpu.VMEM)] * 5,
        scratch_shapes=[
            pltpu.VMEM((ROWS, D), BF16),
            pltpu.VMEM((VISION, D), BF16),
            pltpu.VMEM((1, ROWS), jnp.int32),
            pltpu.VMEM((ROWS, D), BF16),
            pltpu.VMEM((ROWS, D), BF16),
            pltpu.VMEM((ROWS, D), BF16),
            pltpu.VMEM((ROWS, D), BF16),
            pltpu.VMEM((2, NX, NZ, SHARE, D), BF16),
            pltpu.VMEM((2, NX, NZ, SHARE, D), BF16),
            pltpu.VMEM((3, ROWS, R), BF16),
            pltpu.VMEM((3, ROWS, R), BF16),
            pltpu.VMEM((ROWS, R), BF16),
            pltpu.VMEM((ROWS, R), BF16),
            pltpu.VMEM((R, ROWS), BF16),
            pltpu.VMEM((R, ROWS), BF16),
            pltpu.VMEM((2, 2, SHARE, D), BF16),
            pltpu.VMEM((2, 2, SHARE, D), BF16),
            pltpu.VMEM((2, 4, SHARE, D), BF16),
            pltpu.VMEM((2, 4, SHARE, D), BF16),
            pltpu.VMEM((2, SHARE, D), BF16),
            pltpu.VMEM((2, SHARE, D), BF16),
            pltpu.VMEM((2, SHARE, D), BF16),
            pltpu.VMEM((2, SHARE, D), BF16),
            pltpu.VMEM((2, 4, SHARE, D), BF16),
            dma((6,)),
            dma((3 * N_GATHER,)),
            dma((3 * N_GATHER,)),
            dma((6 * N_REDUCE,)),
            dma((6 * N_REDUCE,)),
            dma((3,)),
            dma((3,)),
            dma((3 * PIECES,)),
            dma((3 * PIECES,)),
        ],
        compiler_params=pltpu.CompilerParams(
            collective_id=0, has_side_effects=True, vmem_limit_bytes=40 * 2**20
        ),
        cost_estimate=pl.CostEstimate(
            flops=14 * ROWS * D * R, bytes_accessed=12 * ROWS * D, transcendentals=3 * ROWS * R
        ),
        name="relay_tick",
    )(*(
        pltpu.with_memory_space_constraint(operand, pltpu.HBM)
        for operand in (
            section_in[0, 0], vision_rows[0], alternate, grad_in[0, 0], parked[0, 0],
            w_down[0], w_up[0],
        )
    ))
    received, stash, input_grad, up_grad, down_grad = pl.pallas_call(
        write_out,
        out_shape=(rows, rows, rows, shares, shares),
        in_specs=[pl.BlockSpec(memory_space=pltpu.VMEM)] * 5,
        out_specs=[pl.BlockSpec(memory_space=pltpu.HBM)] * 5,
        scratch_shapes=[dma((5,))],
        name="write_out",
    )(*(pltpu.with_memory_space_constraint(out, pltpu.VMEM) for out in outs))
    return (
        received[None, None],
        stash[None, None],
        input_grad[None, None],
        up_grad[None],
        down_grad[None],
    )


def solution(mesh):
    rows = P("section", "dp", None, "mp")
    shares = P("section", "dp", "mp")
    return jax.shard_map(
        local,
        mesh=mesh,
        in_specs=(rows, P("dp", None, "mp"), P("dp", None), rows, rows, shares, shares),
        out_specs=(rows, rows, rows, shares, shares),
        check_vma=False,
    )
```

```python
import functools
import math

import jax
import jax.numpy as jnp
from jax import lax
from jax.experimental import pallas as pl
from jax.experimental.pallas import tpu as pltpu
from jax.sharding import PartitionSpec as P

MESH = pl.DeviceIdType.MESH
BF16, F32 = jnp.bfloat16, jnp.float32

D = 3584
R = 256
ROWS = 104
VISION = 24
SHARE = 16
TILE = 256
PIECES = 4
PIECE = D // PIECES
NX, NZ = 4, 4
SPLIT = 3 * TILE

N_GATHER = 16
N_REDUCE = 12

NT = (((1,), (1,)), ((), ()))
TN = (((0,), (0,)), ((), ()))

SCALE = math.sqrt(2 / math.pi)


def gelu(v):
    return 0.5 * v * (1.0 + jnp.tanh(SCALE * (v + 0.044715 * (v * v * v))))


def gelu_slope(v):
    t = jnp.tanh(SCALE * (v + 0.044715 * (v * v * v)))
    return 0.5 * (1.0 + t) + 0.5 * v * (1.0 - t * t) * (SCALE * (1.0 + 3 * 0.044715 * (v * v)))


def kernel(
    section_ref, vision_ref, alternate_ref, grad_ref, parked_ref, wd_ref, wu_ref,
    o_section, o_parked, o_input_grad, o_up, o_down,
    sec, vis, alt, grad, fwd, bwd, out, weights, parts,
    pre_out, pre_in, act, slope_act, act_t, grad_t,
    stop, opp_up, opp_dn, from_up, from_dn, opp2_up, opp2_dn, from2_up, from2_dn, sums,
    local_sem, g_send, g_recv, r_send, r_recv, m_send, m_recv, y_send, y_recv,
):
    section = lax.axis_index("section")
    dp = lax.axis_index("dp")
    mp = lax.axis_index("mp")
    x, z = lax.div(dp, NZ), lax.rem(dp, NZ)

    def at(value, count):
        return lax.rem(value + count, count)

    def chunk(xi, zi):
        return at(xi, NX) * NZ + at(zi, NZ)

    mirror = {"section": 15 - section}
    following = {"section": lax.rem(section + 1, 16)}
    preceding = {"section": lax.rem(section + 15, 16)}
    other = {"mp": 1 - mp}
    right, left = {"dp": chunk(x + 1, z)}, {"dp": chunk(x - 1, z)}
    plus, minus = {"dp": chunk(x, z + 1)}, {"dp": chunk(x, z - 1)}

    pending = []

    def remote(src, dst, send, recv, to):
        copy = pltpu.make_async_remote_copy(
            src_ref=src, dst_ref=dst, send_sem=send, recv_sem=recv,
            device_id=to, device_id_type=MESH,
        )
        return copy

    def go(copy):
        copy.start()
        pending.append(copy)

    w_refs = (wd_ref, wu_ref)
    loads = [
        pltpu.make_async_copy(section_ref, sec, local_sem.at[0]),
        pltpu.make_async_copy(vision_ref, vis, local_sem.at[1]),
        pltpu.make_async_copy(alternate_ref, alt, local_sem.at[2]),
        pltpu.make_async_copy(grad_ref, grad, local_sem.at[3]),
        pltpu.make_async_copy(wd_ref, weights.at[0, x, z], local_sem.at[4]),
        pltpu.make_async_copy(wu_ref, weights.at[1, x, z], local_sem.at[5]),
    ]
    for load in loads:
        load.start()

    y, core = lax.div(section, 2), lax.rem(section, 2)
    turn = lax.rem(y, 4)
    near = jnp.logical_or(turn == 0, turn == 3)
    far = jnp.logical_not(near)
    detours, stops, ends = turn == 2, turn == 0, turn == 1
    stop_at = {"section": lax.rem(section + 12, 16)}
    stop_from = {"section": lax.rem(section + 4, 16)}
    stop_to = {"section": lax.rem(y + 5, 8) * 2 + 1 - core}
    end_from = {"section": lax.rem(y + 3, 8) * 2 + 1 - core}

    barrier = pltpu.get_barrier_semaphore()

    def greet(*partners):
        for partner in partners:
            pl.semaphore_signal(barrier, inc=1, device_id=partner, device_id_type=MESH)

    greet(mirror, following, preceding, other, right, left, plus, minus)
    pl.when(detours)(lambda: greet(stop_at))
    pl.when(stops)(lambda: greet(stop_from, stop_to))
    pl.when(ends)(lambda: greet(end_from))
    extra = jnp.where(stops, 2, jnp.where(turn == 3, 0, 1))
    pl.semaphore_wait(barrier, 8 + extra)

    def piece(i):
        return pl.ds(i * PIECE, PIECE)

    def y_piece(src, dst, index, i, to):
        return remote(
            src.at[:, piece(i)], dst.at[:, piece(i)], y_send.at[index], y_recv.at[index], to
        )

    parked_copies = [y_piece(parked_ref, bwd, i, i, mirror) for i in range(PIECES)]
    forward_copies = [y_piece(fwd, o_parked, PIECES + i, i, mirror) for i in range(PIECES)]
    shift_copies = [y_piece(out, o_section, 2 * PIECES + i, i, following) for i in range(PIECES)]
    for copy in parked_copies:
        go(copy)

    def send_forward(pieces, when):
        @pl.when(when)
        def _():
            for i in pieces:
                forward_copies[i].start()

    last = PIECES - 1
    detour_in = remote(
        fwd.at[:, piece(last)], stop, y_send.at[3 * PIECES], y_recv.at[3 * PIECES], stop_at
    )
    detour_out = remote(
        stop, o_parked.at[:, piece(last)],
        y_send.at[3 * PIECES + 1], y_recv.at[PIECES + last], stop_to,
    )

    class Gather:
        def __init__(self, number, w, start, stop, x_first):
            self.base, self.w, self.start, self.stop = number * N_GATHER, w, start, stop
            self.x_first = x_first
            self.a, self.b = (x, z) if x_first else (z, x)
            xs, zs = (right, left), (plus, minus)
            (self.up, self.dn), (self.up2, self.dn2) = (xs, zs) if x_first else (zs, xs)
            middle = (start + stop) // 2
            self.all = pl.ds(start, stop - start)
            self.low, self.high = pl.ds(start, middle - start), pl.ds(middle, stop - middle)

        def copy(self, m, to, a=0, b=0, cols=None):
            cols = self.all if cols is None else cols
            a, b = at(self.a + a, 4), at(self.b + b, 4)
            xi, zi = (a, b) if self.x_first else (b, a)
            place = weights.at[self.w, xi, zi, :, cols]
            index = self.base + m
            return remote(place, place, g_send.at[index], g_recv.at[index], to)

        def start1(self):
            go(self.copy(0, self.up))
            go(self.copy(1, self.dn))

        def start2(self, k):
            go(self.copy(4 + k, self.up2, a=k))
            go(self.copy(8 + k, self.dn2, a=k))

        def near1(self):
            self.copy(0, self.up).wait_recv()
            go(self.copy(2, self.up, a=-1, cols=self.low))
            self.start2(3)
            self.copy(1, self.dn).wait_recv()
            go(self.copy(3, self.dn, a=1, cols=self.high))
            self.start2(1)

        def far1(self):
            self.copy(2, self.up, cols=self.low).wait_recv()
            self.copy(3, self.dn, cols=self.high).wait_recv()
            self.start2(2)

        def near2(self, k):
            self.copy(4 + k, self.up2).wait_recv()
            if k % 2 == 0:
                go(self.copy(12 + k // 2, self.up2, a=k, b=-1))
            self.copy(8 + k, self.dn2).wait_recv()
            if k % 2 == 1:
                go(self.copy(14 + k // 2, self.dn2, a=k, b=1))

        def far2(self, k):
            if k % 2 == 0:
                self.copy(12 + k // 2, self.up2).wait_recv()
            else:
                self.copy(14 + k // 2, self.dn2).wait_recv()

    down = Gather(0, 0, SPLIT, D, False)
    up = Gather(1, 1, SPLIT, D, False)
    both = Gather(2, slice(None), 0, SPLIT, True)

    def exchange(slot):
        return remote(
            pre_out.at[slot], pre_in.at[slot], m_send.at[slot], m_recv.at[slot], other
        )

    def weight(w, cols):
        block = weights[w, :, :, :, cols]
        return block.reshape(R, block.shape[-1])

    def partial(slot, rows, w):
        total = jnp.zeros((ROWS, R), F32)
        for i in range(PIECES):
            total += lax.dot_general(
                rows[:, piece(i)], weight(w, piece(i)), NT, preferred_element_type=F32
            )
        send_partial(slot, total)

    def send_partial(slot, total):
        pre_out[slot] = total.astype(BF16)
        go(exchange(slot))

    def summed(slot):
        exchange(slot).wait_recv()
        return pre_out[slot].astype(F32) + pre_in[slot].astype(F32)

    for load in loads[4:]:
        load.wait()
    down.start1()
    down.start2(0)
    both.start1()
    both.start2(0)
    up.start2(0)

    for load in loads[:3]:
        load.wait()
    picks = jnp.where(section == 0, alt[...], -1)
    chosen_t = (lax.broadcasted_iota(jnp.int32, (VISION, ROWS), 0) == picks).astype(BF16)
    hit = lax.dot_general(
        chosen_t, jnp.ones((VISION, PIECE), BF16), TN, preferred_element_type=F32
    )

    for i in range(PIECES):
        cols = piece(i)
        chosen = lax.dot_general(chosen_t, vis[:, cols], TN, preferred_element_type=F32)
        fwd[:, cols] = jnp.where(hit > 0.5, chosen, sec[:, cols].astype(F32)).astype(BF16)
    pl.when(detours)(detour_in.start)

    down.near1()
    up.start1()
    both.near1()
    down.near2(0)
    both.far1()
    both.near2(0)
    down.far1()
    down.near2(3)
    down.near2(1)
    both.near2(3)
    both.near2(1)
    up.near1()
    down.far2(0)
    down.near2(2)
    up.far1()
    both.near2(2)
    up.near2(0)
    up.near2(3)
    up.near2(1)
    up.far2(0)
    up.near2(2)
    for k in (3, 1, 2):
        down.far2(k)
    for k in (0, 3, 1, 2):
        both.far2(k)
    partial(0, fwd, 0)
    for k in (3, 1, 2):
        up.far2(k)
    loads[3].wait()
    partial(1, grad, 1)

    total = jnp.zeros((ROWS, R), F32)
    for i in range(PIECES):
        parked_copies[i].wait_recv()
        if i < last:
            send_forward([i], near)
        cols = piece(i)
        total += lax.dot_general(bwd[:, cols], weight(0, cols), NT, preferred_element_type=F32)
    send_partial(2, total)

    @pl.when(stops)
    def _():
        detour_in.wait_recv()
        detour_out.start()

    bwd_pre = summed(2)
    bwd_act = gelu(bwd_pre).astype(BF16)
    act_t[...] = bwd_act.T
    pre_grad = (summed(1) * gelu_slope(bwd_pre)).astype(BF16)
    slope_act[...] = pre_grad
    grad_t[...] = pre_grad.T

    def outputs(i):
        cols = piece(i)
        product = jnp.dot(act[...], weight(1, cols), preferred_element_type=F32)
        out[:, cols] = (fwd[:, cols].astype(F32) + product).astype(BF16)
        go(shift_copies[i])

    def add_into(total, term):
        total[...] = (total[...].astype(F32) + term[...].astype(F32)).astype(BF16)

    class Reduce:
        def __init__(self, number, w, start, stop, x_first):
            self.base, self.w, self.start, self.stop = number * N_REDUCE, w, start, stop
            self.x_first = x_first
            self.a, self.b = (x, z) if x_first else (z, x)
            xs, zs = (right, left), (plus, minus)
            (self.up, self.dn), (self.up2, self.dn2) = (xs, zs) if x_first else (zs, xs)
            middle = (start + stop) // 2
            self.all = pl.ds(start, stop - start)
            self.low, self.high = pl.ds(start, middle - start), pl.ds(middle, stop - middle)

        def block(self, a, b0, count):
            a = at(self.a + a, 4)
            if self.x_first:
                return parts.at[self.w, a, pl.ds(b0, count), :, self.all]
            return parts.at[self.w, pl.ds(b0, count), a, :, self.all]

        def term(self, ref, b0, count):
            return ref.at[self.w, pl.ds(b0, count), :, self.all]

        def total(self, b, cols):
            return sums.at[self.w, at(self.b + b, 4), :, cols]

        def copy(self, m):
            w = self.w
            src, dst, to = (
                lambda: (self.block(2, 0, 2), self.term(opp_up, 0, 2), self.dn),
                lambda: (self.block(2, 2, 2), self.term(opp_dn, 0, 2), self.up),
                lambda: (self.block(-1, 2, 2), self.term(from_up, 2, 2), self.dn),
                lambda: (self.block(1, 0, 2), self.term(from_dn, 0, 2), self.up),
                lambda: (self.block(-1, 0, 2), self.term(from_up, 0, 2), self.dn),
                lambda: (self.block(1, 2, 2), self.term(from_dn, 2, 2), self.up),
                lambda: (self.total(2, self.low), opp2_up.at[w, :, self.low], self.dn2),
                lambda: (self.total(2, self.high), opp2_dn.at[w, :, self.high], self.up2),
                lambda: (self.total(-1, self.high), from2_up.at[w, :, self.high], self.dn2),
                lambda: (self.total(1, self.low), from2_dn.at[w, :, self.low], self.up2),
                lambda: (self.total(-1, self.low), from2_up.at[w, :, self.low], self.dn2),
                lambda: (self.total(1, self.high), from2_dn.at[w, :, self.high], self.up2),
            )[m]()
            index = self.base + m
            return remote(src, dst, r_send.at[index], r_recv.at[index], to)

        def stage_a(self):
            lhs, rhs = ((act_t, grad), (grad_t, bwd))[self.w]

            steps = max(1, (self.stop - self.start) // 640)
            width = (self.stop - self.start) // steps
            for i in range(steps):
                cols = pl.ds(self.start + i * width, width)
                product = jnp.dot(lhs[...], rhs[:, cols], preferred_element_type=F32)
                parts[self.w, :, :, :, cols] = product.astype(BF16).reshape(NX, NZ, SHARE, width)
            for m in range(4):
                go(self.copy(m))

        def stage_b(self):
            self.copy(0).wait_recv()
            add_into(self.block(-1, 0, 2), self.term(opp_up, 0, 2))
            go(self.copy(4))
            self.copy(1).wait_recv()
            add_into(self.block(1, 2, 2), self.term(opp_dn, 0, 2))
            go(self.copy(5))

        def stage_c(self):
            for m in (2, 3, 4, 5):
                self.copy(m).wait_recv()
            self.term(sums, 0, 4)[...] = (
                self.block(0, 0, 4)[...].astype(F32)
                + self.term(from_up, 0, 4)[...].astype(F32)
                + self.term(from_dn, 0, 4)[...].astype(F32)
            ).astype(BF16)
            for m in (6, 7, 8, 9):
                go(self.copy(m))

        def stage_d(self):
            w = self.w
            self.copy(6).wait_recv()
            add_into(self.total(-1, self.low), opp2_up.at[w, :, self.low])
            go(self.copy(10))
            self.copy(7).wait_recv()
            add_into(self.total(1, self.high), opp2_dn.at[w, :, self.high])
            go(self.copy(11))

        def stage_e(self):
            w, cols = self.w, self.all
            for m in (8, 9, 10, 11):
                self.copy(m).wait_recv()
            total = (
                parts[w, x, z, :, cols].astype(F32)
                + from_up[w, self.b, :, cols].astype(F32)
                + from_dn[w, self.b, :, cols].astype(F32)
                + from2_up[w, :, cols].astype(F32)
                + from2_dn[w, :, cols].astype(F32)
            )
            (o_up, o_down)[w][:, cols] = (total * (1.0 / 16)).astype(BF16)

    def input_grad(i):
        cols = piece(i)
        product = jnp.dot(slope_act[...], weight(0, cols), preferred_element_type=F32)
        o_input_grad[:, cols] = (grad[:, cols].astype(F32) + product).astype(BF16)

    cut = SPLIT + 6 * TILE
    u0, u1 = Reduce(0, 0, SPLIT, cut, True), Reduce(1, 0, cut, D, True)
    d0, d1 = Reduce(2, 1, SPLIT, cut, True), Reduce(3, 1, cut, D, True)
    uz, dz = Reduce(4, 0, 0, SPLIT, False), Reduce(5, 1, 0, SPLIT, False)
    u0.stage_a()
    uz.stage_a()
    u1.stage_a()
    act[...] = gelu(summed(0)).astype(BF16)
    outputs(0)
    outputs(1)
    u0.stage_b()
    uz.stage_b()
    d0.stage_a()
    outputs(2)
    outputs(3)
    send_forward(range(last), far)
    send_forward([last], jnp.logical_not(detours))
    dz.stage_a()
    u1.stage_b()
    u0.stage_c()
    uz.stage_c()
    d1.stage_a()
    d0.stage_b()
    u0.stage_d()
    uz.stage_d()
    dz.stage_b()
    u1.stage_c()
    u1.stage_d()
    dz.stage_c()
    input_grad(0)
    input_grad(1)
    d1.stage_b()
    d0.stage_c()
    u0.stage_e()
    uz.stage_e()
    dz.stage_d()
    d0.stage_d()
    u1.stage_e()
    input_grad(2)
    input_grad(3)
    d1.stage_c()
    d1.stage_d()
    dz.stage_e()
    d0.stage_e()
    d1.stage_e()

    for copy in forward_copies + shift_copies:
        copy.wait_recv()
    for copy in pending + forward_copies[:last]:
        copy.wait_send()
    pl.when(jnp.logical_not(detours))(forward_copies[last].wait_send)
    pl.when(detours)(detour_in.wait_send)
    pl.when(stops)(detour_out.wait_send)


def write_out(*refs):
    copies = [
        pltpu.make_async_copy(refs[i], refs[5 + i], refs[10].at[i]) for i in range(5)
    ]
    for copy in copies:
        copy.start()
    for copy in copies:
        copy.wait()


def local(section_in, vision_rows, alternate, grad_in, parked, w_down, w_up):
    rows = jax.ShapeDtypeStruct((ROWS, D), BF16)
    shares = jax.ShapeDtypeStruct((SHARE, D), BF16)
    dma = pltpu.SemaphoreType.DMA
    outs = pl.pallas_call(
        kernel,
        out_shape=(pltpu.VMEM((ROWS, D), BF16),) * 3 + (pltpu.VMEM((SHARE, D), BF16),) * 2,
        in_specs=[pl.BlockSpec(memory_space=pltpu.HBM)] * 7,
        out_specs=[pl.BlockSpec(memory_space=pltpu.VMEM)] * 5,
        scratch_shapes=[
            pltpu.VMEM((ROWS, D), BF16),
            pltpu.VMEM((VISION, D), BF16),
            pltpu.VMEM((1, ROWS), jnp.int32),
            pltpu.VMEM((ROWS, D), BF16),
            pltpu.VMEM((ROWS, D), BF16),
            pltpu.VMEM((ROWS, D), BF16),
            pltpu.VMEM((ROWS, D), BF16),
            pltpu.VMEM((2, NX, NZ, SHARE, D), BF16),
            pltpu.VMEM((2, NX, NZ, SHARE, D), BF16),
            pltpu.VMEM((3, ROWS, R), BF16),
            pltpu.VMEM((3, ROWS, R), BF16),
            pltpu.VMEM((ROWS, R), BF16),
            pltpu.VMEM((ROWS, R), BF16),
            pltpu.VMEM((R, ROWS), BF16),
            pltpu.VMEM((R, ROWS), BF16),
            pltpu.VMEM((ROWS, PIECE), BF16),
            pltpu.VMEM((2, 2, SHARE, D), BF16),
            pltpu.VMEM((2, 2, SHARE, D), BF16),
            pltpu.VMEM((2, 4, SHARE, D), BF16),
            pltpu.VMEM((2, 4, SHARE, D), BF16),
            pltpu.VMEM((2, SHARE, D), BF16),
            pltpu.VMEM((2, SHARE, D), BF16),
            pltpu.VMEM((2, SHARE, D), BF16),
            pltpu.VMEM((2, SHARE, D), BF16),
            pltpu.VMEM((2, 4, SHARE, D), BF16),
            dma((6,)),
            dma((3 * N_GATHER,)),
            dma((3 * N_GATHER,)),
            dma((6 * N_REDUCE,)),
            dma((6 * N_REDUCE,)),
            dma((3,)),
            dma((3,)),
            dma((3 * PIECES + 2,)),
            dma((3 * PIECES + 1,)),
        ],
        compiler_params=pltpu.CompilerParams(
            collective_id=0, has_side_effects=True, vmem_limit_bytes=40 * 2**20
        ),
        cost_estimate=pl.CostEstimate(
            flops=14 * ROWS * D * R, bytes_accessed=12 * ROWS * D, transcendentals=3 * ROWS * R
        ),
        name="relay_tick",
    )(*(
        pltpu.with_memory_space_constraint(operand, pltpu.HBM)
        for operand in (
            section_in[0, 0], vision_rows[0], alternate, grad_in[0, 0], parked[0, 0],
            w_down[0], w_up[0],
        )
    ))
    received, stash, input_grad, up_grad, down_grad = pl.pallas_call(
        write_out,
        out_shape=(rows, rows, rows, shares, shares),
        in_specs=[pl.BlockSpec(memory_space=pltpu.VMEM)] * 5,
        out_specs=[pl.BlockSpec(memory_space=pltpu.HBM)] * 5,
        scratch_shapes=[dma((5,))],
        name="write_out",
    )(*(pltpu.with_memory_space_constraint(out, pltpu.VMEM) for out in outs))
    return (
        received[None, None],
        stash[None, None],
        input_grad[None, None],
        up_grad[None],
        down_grad[None],
    )


def solution(mesh):
    rows = P("section", "dp", None, "mp")
    shares = P("section", "dp", "mp")
    return jax.shard_map(
        local,
        mesh=mesh,
        in_specs=(rows, P("dp", None, "mp"), P("dp", None), rows, rows, shares, shares),
        out_specs=(rows, rows, rows, shares, shares),
        check_vma=False,
    )
```

```python
import functools
import math

import jax
import jax.numpy as jnp
from jax import lax
from jax.experimental import pallas as pl
from jax.experimental.pallas import tpu as pltpu
from jax.sharding import PartitionSpec as P

MESH = pl.DeviceIdType.MESH
BF16, F32 = jnp.bfloat16, jnp.float32

D = 3584
R = 256
ROWS = 104
VISION = 24
SHARE = 16
PIECES = 4
PIECE = D // PIECES
HANDED = 2
HAND = 3 * PIECES
NX, NZ = 4, 4
SPLIT = 1024

N_GATHER = 16
N_REDUCE = 12

NT = (((1,), (1,)), ((), ()))
TN = (((0,), (0,)), ((), ()))

SCALE = math.sqrt(2 / math.pi)


def gelu(v):
    return 0.5 * v * (1.0 + jnp.tanh(SCALE * (v + 0.044715 * (v * v * v))))


def gelu_slope(v):
    t = jnp.tanh(SCALE * (v + 0.044715 * (v * v * v)))
    return 0.5 * (1.0 + t) + 0.5 * v * (1.0 - t * t) * (SCALE * (1.0 + 3 * 0.044715 * (v * v)))


def kernel(
    section_ref, vision_ref, alternate_ref, grad_ref, parked_ref, wd_ref, wu_ref,
    o_section, o_parked, o_input_grad, o_up, o_down,
    sec, vis, alt, grad, fwd, bwd, out, weights, parts,
    pre_out, pre_in, bwd_pre, act, slope_act, act_t, grad_t,
    hand, stop, opp_up, opp_dn, from_up, from_dn, opp2_up, opp2_dn, from2_up, from2_dn, sums,
    local_sem, g_send, g_recv, r_send, r_recv, m_send, m_recv, y_send, y_recv,
):
    section = lax.axis_index("section")
    dp = lax.axis_index("dp")
    mp = lax.axis_index("mp")
    x, z = lax.div(dp, NZ), lax.rem(dp, NZ)

    def at(value, count):
        return lax.rem(value + count, count)

    def chunk(xi, zi):
        return at(xi, NX) * NZ + at(zi, NZ)

    mirror = {"section": 15 - section}
    following = {"section": lax.rem(section + 1, 16)}
    preceding = {"section": lax.rem(section + 15, 16)}
    other = {"mp": 1 - mp}
    right, left = {"dp": chunk(x + 1, z)}, {"dp": chunk(x - 1, z)}
    plus, minus = {"dp": chunk(x, z + 1)}, {"dp": chunk(x, z - 1)}

    pending = []

    def remote(src, dst, send, recv, to):
        copy = pltpu.make_async_remote_copy(
            src_ref=src, dst_ref=dst, send_sem=send, recv_sem=recv,
            device_id=to, device_id_type=MESH,
        )
        return copy

    def go(copy):
        copy.start()
        pending.append(copy)

    w_refs = (wd_ref, wu_ref)
    loads = [
        pltpu.make_async_copy(section_ref, sec, local_sem.at[0]),
        pltpu.make_async_copy(vision_ref, vis, local_sem.at[1]),
        pltpu.make_async_copy(alternate_ref, alt, local_sem.at[2]),
        pltpu.make_async_copy(grad_ref, grad, local_sem.at[3]),
        pltpu.make_async_copy(wd_ref, weights.at[0, x, z], local_sem.at[4]),
        pltpu.make_async_copy(wu_ref, weights.at[1, x, z], local_sem.at[5]),
    ]
    for load in loads:
        load.start()

    y, core = lax.div(section, 2), lax.rem(section, 2)
    turn = lax.rem(y, 4)
    near = jnp.logical_or(turn == 0, turn == 3)
    far = jnp.logical_not(near)
    detours, stops, ends = turn == 2, turn == 0, turn == 1
    next_chip = {"section": lax.rem(section + 2, 16)}
    last_chip = {"section": lax.rem(section + 14, 16)}
    stop_at = {"section": lax.rem(section + 12, 16)}
    stop_from = {"section": lax.rem(section + 4, 16)}
    stop_to = {"section": lax.rem(y + 5, 8) * 2 + 1 - core}
    end_from = {"section": lax.rem(y + 3, 8) * 2 + 1 - core}

    barrier = pltpu.get_barrier_semaphore()

    def greet(*partners):
        for partner in partners:
            pl.semaphore_signal(barrier, inc=1, device_id=partner, device_id_type=MESH)

    greet(mirror, following, preceding, other, right, left, plus, minus)
    pl.when(detours)(lambda: greet(stop_at))
    pl.when(stops)(lambda: greet(stop_from, stop_to))
    pl.when(ends)(lambda: greet(end_from))
    pl.when(core == 0)(lambda: greet(next_chip, last_chip))
    extra = jnp.where(stops, 2, jnp.where(turn == 3, 0, 1))
    pl.semaphore_wait(barrier, 8 + extra + 2 * (1 - core))

    def piece(i):
        return pl.ds(i * PIECE, PIECE)

    def y_piece(src, dst, index, i, to):
        return remote(
            src.at[:, piece(i)], dst.at[:, piece(i)], y_send.at[index], y_recv.at[index], to
        )

    parked_copies = [y_piece(parked_ref, bwd, i, i, mirror) for i in range(PIECES)]
    forward_copies = [y_piece(fwd, o_parked, PIECES + i, i, mirror) for i in range(PIECES)]
    shift_copies = [y_piece(out, o_section, 2 * PIECES + i, i, following) for i in range(PIECES)]
    for copy in parked_copies:
        go(copy)

    def send_forward(pieces, when):
        @pl.when(when)
        def _():
            for i in pieces:
                forward_copies[i].start()

    hand_copies, pass_copies = {}, {}
    for i in range(HANDED, PIECES):
        held = hand.at[:, pl.ds((i - HANDED) * PIECE, PIECE)]
        hand_copies[i] = remote(
            out.at[:, piece(i)], held, y_send.at[HAND + i], y_recv.at[HAND + i], preceding
        )
        pass_copies[i] = remote(
            held, o_section.at[:, piece(i)],
            y_send.at[HAND + i], y_recv.at[2 * PIECES + i], next_chip,
        )

    last = PIECES - 1
    detour_in = remote(
        fwd.at[:, piece(last)], stop, y_send.at[3 * PIECES], y_recv.at[3 * PIECES], stop_at
    )
    detour_out = remote(
        stop, o_parked.at[:, piece(last)],
        y_send.at[3 * PIECES + 1], y_recv.at[PIECES + last], stop_to,
    )

    class Gather:
        def __init__(self, number, w, start, stop, x_first):
            self.base, self.w, self.start, self.stop = number * N_GATHER, w, start, stop
            self.x_first = x_first
            self.a, self.b = (x, z) if x_first else (z, x)
            xs, zs = (right, left), (plus, minus)
            (self.up, self.dn), (self.up2, self.dn2) = (xs, zs) if x_first else (zs, xs)
            middle = (start + stop) // 2
            self.all = pl.ds(start, stop - start)
            self.low, self.high = pl.ds(start, middle - start), pl.ds(middle, stop - middle)

        def copy(self, m, to, a=0, b=0, cols=None):
            cols = self.all if cols is None else cols
            a, b = at(self.a + a, 4), at(self.b + b, 4)
            xi, zi = (a, b) if self.x_first else (b, a)
            place = weights.at[self.w, xi, zi, :, cols]
            index = self.base + m
            return remote(place, place, g_send.at[index], g_recv.at[index], to)

        def start1(self):
            go(self.copy(0, self.up))
            go(self.copy(1, self.dn))

        def start2(self, k):
            go(self.copy(4 + k, self.up2, a=k))
            go(self.copy(8 + k, self.dn2, a=k))

        def near1(self, side):
            self.copy(side, (self.up, self.dn)[side]).wait_recv()
            if side == 0:
                go(self.copy(2, self.up, a=-1, cols=self.low))
                self.start2(3)
            else:
                go(self.copy(3, self.dn, a=1, cols=self.high))
                self.start2(1)

        def far1(self):
            self.copy(2, self.up, cols=self.low).wait_recv()
            self.copy(3, self.dn, cols=self.high).wait_recv()
            self.start2(2)

        def near2(self, k, side):
            self.copy(4 + 4 * side + k, (self.up2, self.dn2)[side]).wait_recv()
            if k % 2 == 0 and side == 0:
                go(self.copy(12 + k // 2, self.up2, a=k, b=-1))
            if k % 2 == 1 and side == 1:
                go(self.copy(14 + k // 2, self.dn2, a=k, b=1))

        def far2(self, k):
            if k % 2 == 0:
                self.copy(12 + k // 2, self.up2).wait_recv()
            else:
                self.copy(14 + k // 2, self.dn2).wait_recv()

    down = Gather(0, 0, SPLIT, D, False)
    up = Gather(1, 1, SPLIT, D, False)
    both = Gather(2, slice(None), 0, SPLIT, True)

    def exchange(slot):
        return remote(
            pre_out.at[slot], pre_in.at[slot], m_send.at[slot], m_recv.at[slot], other
        )

    def weight(w, cols):
        block = weights[w, :, :, :, cols]
        return block.reshape(R, block.shape[-1])

    def partial(slot, rows, w):
        total = jnp.zeros((ROWS, R), F32)
        for i in range(PIECES):
            total += lax.dot_general(
                rows[:, piece(i)], weight(w, piece(i)), NT, preferred_element_type=F32
            )
        send_partial(slot, total)

    def send_partial(slot, total):
        pre_out[slot] = total.astype(BF16)
        go(exchange(slot))

    def summed(slot):
        exchange(slot).wait_recv()
        return pre_out[slot].astype(F32) + pre_in[slot].astype(F32)

    for load in loads[4:]:
        load.wait()
    down.start1()
    down.start2(0)
    both.start1()
    both.start2(0)
    up.start2(0)
    up.start1()

    for load in loads[:3]:
        load.wait()
    picks = jnp.where(section == 0, alt[...], -1)
    chosen_t = (lax.broadcasted_iota(jnp.int32, (VISION, ROWS), 0) == picks).astype(BF16)
    hit = lax.dot_general(
        chosen_t, jnp.ones((VISION, PIECE), BF16), TN, preferred_element_type=F32
    )

    for i in range(PIECES):
        cols = piece(i)
        chosen = lax.dot_general(chosen_t, vis[:, cols], TN, preferred_element_type=F32)
        fwd[:, cols] = jnp.where(hit > 0.5, chosen, sec[:, cols].astype(F32)).astype(BF16)
    pl.when(detours)(detour_in.start)

    def backward_rows():
        total = jnp.zeros((ROWS, R), F32)
        for i in range(PIECES):
            parked_copies[i].wait_recv()
            send_forward([i], near)
            cols = piece(i)
            total += lax.dot_general(
                bwd[:, cols], weight(0, cols), NT, preferred_element_type=F32
            )
        send_partial(2, total)

        @pl.when(stops)
        def _():
            detour_in.wait_recv()
            detour_out.start()

    both.near1(0)
    both.near1(1)
    down.near2(0, 0)
    down.near2(0, 1)
    up.near2(0, 0)
    up.near2(0, 1)
    both.far1()
    down.far2(0)
    up.far2(0)
    both.near2(0, 0)
    both.near2(0, 1)
    down.near1(0)
    down.near1(1)
    up.near1(1)
    up.near1(0)
    down.near2(3, 0)
    down.near2(3, 1)
    down.near2(1, 0)
    down.near2(1, 1)
    both.near2(3, 1)
    both.near2(1, 1)
    up.near2(1, 0)
    up.near2(3, 0)
    both.near2(2, 1)
    both.near2(3, 0)
    both.near2(1, 0)
    up.near2(1, 1)
    up.near2(3, 1)
    down.far1()
    both.near2(2, 0)
    up.far1()
    down.far2(3)
    both.far2(0)
    down.far2(1)
    down.near2(2, 0)
    both.far2(3)
    both.far2(1)
    both.far2(2)
    up.near2(2, 0)
    up.far2(1)
    down.far2(2)
    up.far2(3)
    down.near2(2, 1)
    backward_rows()
    up.near2(2, 1)
    up.far2(2)
    loads[3].wait()
    partial(1, grad, 1)
    partial(0, fwd, 0)

    def backward_act():
        bwd_pre[...] = summed(2)
        act_t[...] = gelu(bwd_pre[...]).astype(BF16).T

    def slopes():
        pre_grad = (summed(1) * gelu_slope(bwd_pre[...])).astype(BF16)
        slope_act[...] = pre_grad
        grad_t[...] = pre_grad.T

    def outputs(i):
        cols = piece(i)
        product = jnp.dot(act[...], weight(1, cols), preferred_element_type=F32)
        out[:, cols] = (fwd[:, cols].astype(F32) + product).astype(BF16)
        if i < HANDED:
            go(shift_copies[i])
        else:
            pl.when(core == 0)(shift_copies[i].start)
            pl.when(core == 1)(hand_copies[i].start)

    def pass_on():
        @pl.when(core == 0)
        def _():
            for i in range(HANDED, PIECES):
                hand_copies[i].wait_recv()
                pass_copies[i].start()

    def add_into(total, term):
        total[...] = (total[...].astype(F32) + term[...].astype(F32)).astype(BF16)

    class Reduce:
        def __init__(self, number, w, start, stop, x_first):
            self.base, self.w, self.start, self.stop = number * N_REDUCE, w, start, stop
            self.x_first = x_first
            self.a, self.b = (x, z) if x_first else (z, x)
            xs, zs = (right, left), (plus, minus)
            (self.up, self.dn), (self.up2, self.dn2) = (xs, zs) if x_first else (zs, xs)
            middle = (start + stop) // 2
            self.all = pl.ds(start, stop - start)
            self.low, self.high = pl.ds(start, middle - start), pl.ds(middle, stop - middle)

        def block(self, a, b0, count):
            a = at(self.a + a, 4)
            if self.x_first:
                return parts.at[self.w, a, pl.ds(b0, count), :, self.all]
            return parts.at[self.w, pl.ds(b0, count), a, :, self.all]

        def term(self, ref, b0, count):
            return ref.at[self.w, pl.ds(b0, count), :, self.all]

        def total(self, b, cols):
            return sums.at[self.w, at(self.b + b, 4), :, cols]

        def copy(self, m):
            w = self.w
            src, dst, to = (
                lambda: (self.block(2, 0, 2), self.term(opp_up, 0, 2), self.dn),
                lambda: (self.block(2, 2, 2), self.term(opp_dn, 0, 2), self.up),
                lambda: (self.block(-1, 2, 2), self.term(from_up, 2, 2), self.dn),
                lambda: (self.block(1, 0, 2), self.term(from_dn, 0, 2), self.up),
                lambda: (self.block(-1, 0, 2), self.term(from_up, 0, 2), self.dn),
                lambda: (self.block(1, 2, 2), self.term(from_dn, 2, 2), self.up),
                lambda: (self.total(2, self.low), opp2_up.at[w, :, self.low], self.dn2),
                lambda: (self.total(2, self.high), opp2_dn.at[w, :, self.high], self.up2),
                lambda: (self.total(-1, self.high), from2_up.at[w, :, self.high], self.dn2),
                lambda: (self.total(1, self.low), from2_dn.at[w, :, self.low], self.up2),
                lambda: (self.total(-1, self.low), from2_up.at[w, :, self.low], self.dn2),
                lambda: (self.total(1, self.high), from2_dn.at[w, :, self.high], self.up2),
            )[m]()
            index = self.base + m
            return remote(src, dst, r_send.at[index], r_recv.at[index], to)

        def send_far(self):
            lhs, rhs = ((act_t, grad), (grad_t, bwd))[self.w]
            steps = -(-(self.stop - self.start) // 640)
            width = (self.stop - self.start) // steps
            for i in range(steps):
                cols = pl.ds(self.start + i * width, width)
                product = jnp.dot(lhs[...], rhs[:, cols], preferred_element_type=F32)
                parts[self.w, :, :, :, cols] = product.astype(BF16).reshape(NX, NZ, SHARE, width)
            go(self.copy(0))
            go(self.copy(1))

        def send_near(self):
            go(self.copy(2))
            go(self.copy(3))

        def relay(self, side):
            self.copy(side).wait_recv()
            if side == 0:
                add_into(self.block(-1, 0, 2), self.term(opp_up, 0, 2))
            else:
                add_into(self.block(1, 2, 2), self.term(opp_dn, 0, 2))
            go(self.copy(4 + side))

        def fold(self):
            for m in (2, 3, 4, 5):
                self.copy(m).wait_recv()
            self.term(sums, 0, 4)[...] = (
                self.block(0, 0, 4)[...].astype(F32)
                + self.term(from_up, 0, 4)[...].astype(F32)
                + self.term(from_dn, 0, 4)[...].astype(F32)
            ).astype(BF16)
            for m in (6, 7, 8, 9):
                go(self.copy(m))

        def relay2(self, side):
            w = self.w
            self.copy(6 + side).wait_recv()
            if side == 0:
                add_into(self.total(-1, self.low), opp2_up.at[w, :, self.low])
            else:
                add_into(self.total(1, self.high), opp2_dn.at[w, :, self.high])
            go(self.copy(10 + side))

        def finish(self):
            w, cols = self.w, self.all
            for m in (8, 9, 10, 11):
                self.copy(m).wait_recv()
            total = (
                parts[w, x, z, :, cols].astype(F32)
                + from_up[w, self.b, :, cols].astype(F32)
                + from_dn[w, self.b, :, cols].astype(F32)
                + from2_up[w, :, cols].astype(F32)
                + from2_dn[w, :, cols].astype(F32)
            )
            (o_up, o_down)[w][:, cols] = (total * (1.0 / 16)).astype(BF16)

    def input_grad(i):
        cols = piece(i)
        product = jnp.dot(slope_act[...], weight(0, cols), preferred_element_type=F32)
        o_input_grad[:, cols] = (grad[:, cols].astype(F32) + product).astype(BF16)

    cut = (SPLIT + D) // 2
    u0, u1 = Reduce(0, 0, SPLIT, cut, True), Reduce(1, 0, cut, D, True)
    d0, d1 = Reduce(2, 1, SPLIT, cut, True), Reduce(3, 1, cut, D, True)
    uz, dz = Reduce(4, 0, 0, SPLIT, False), Reduce(5, 1, 0, SPLIT, False)
    backward_act()
    u0.send_far()
    slopes()
    u0.send_near()
    uz.send_far()
    u1.send_far()
    uz.send_near()
    u1.send_near()
    dz.send_far()
    d0.send_far()
    u0.relay(0)
    u0.relay(1)
    dz.send_near()
    d0.send_near()
    d1.send_far()
    d1.send_near()
    act[...] = gelu(summed(0)).astype(BF16)
    outputs(0)
    outputs(1)
    outputs(2)
    outputs(3)
    send_forward(range(last), far)
    send_forward([last], ends)
    uz.relay(0)
    uz.relay(1)
    input_grad(0)
    input_grad(1)
    input_grad(2)
    input_grad(3)
    pass_on()
    u1.relay(1)
    u1.relay(0)
    dz.relay(0)
    dz.relay(1)
    d0.relay(0)
    d0.relay(1)
    u0.fold()
    uz.fold()
    d1.relay(0)
    d1.relay(1)
    u1.fold()
    uz.relay2(1)
    uz.relay2(0)
    u0.relay2(0)
    u0.relay2(1)
    dz.fold()
    d0.fold()
    uz.finish()
    u1.relay2(0)
    u1.relay2(1)
    d1.fold()
    dz.relay2(0)
    dz.relay2(1)
    u0.finish()
    d0.relay2(1)
    d0.relay2(0)
    dz.finish()
    u1.finish()
    d1.relay2(0)
    d1.relay2(1)
    d0.finish()
    d1.finish()

    for copy in forward_copies + shift_copies:
        copy.wait_recv()
    for copy in pending + forward_copies[:last]:
        copy.wait_send()
    pl.when(jnp.logical_not(detours))(forward_copies[last].wait_send)
    pl.when(detours)(detour_in.wait_send)
    for i in range(HANDED, PIECES):
        pl.when(core == 0)(shift_copies[i].wait_send)
        pl.when(core == 0)(pass_copies[i].wait_send)
        pl.when(core == 1)(hand_copies[i].wait_send)
    pl.when(stops)(detour_out.wait_send)


def write_out(*refs):
    copies = [
        pltpu.make_async_copy(refs[i], refs[5 + i], refs[10].at[i]) for i in range(5)
    ]
    for copy in copies:
        copy.start()
    for copy in copies:
        copy.wait()


def local(section_in, vision_rows, alternate, grad_in, parked, w_down, w_up):
    rows = jax.ShapeDtypeStruct((ROWS, D), BF16)
    shares = jax.ShapeDtypeStruct((SHARE, D), BF16)
    dma = pltpu.SemaphoreType.DMA
    outs = pl.pallas_call(
        kernel,
        out_shape=(pltpu.VMEM((ROWS, D), BF16),) * 3 + (pltpu.VMEM((SHARE, D), BF16),) * 2,
        in_specs=[pl.BlockSpec(memory_space=pltpu.HBM)] * 7,
        out_specs=[pl.BlockSpec(memory_space=pltpu.VMEM)] * 5,
        scratch_shapes=[
            pltpu.VMEM((ROWS, D), BF16),
            pltpu.VMEM((VISION, D), BF16),
            pltpu.VMEM((1, ROWS), jnp.int32),
            pltpu.VMEM((ROWS, D), BF16),
            pltpu.VMEM((ROWS, D), BF16),
            pltpu.VMEM((ROWS, D), BF16),
            pltpu.VMEM((ROWS, D), BF16),
            pltpu.VMEM((2, NX, NZ, SHARE, D), BF16),
            pltpu.VMEM((2, NX, NZ, SHARE, D), BF16),
            pltpu.VMEM((3, ROWS, R), BF16),
            pltpu.VMEM((3, ROWS, R), BF16),
            pltpu.VMEM((ROWS, R), F32),
            pltpu.VMEM((ROWS, R), BF16),
            pltpu.VMEM((ROWS, R), BF16),
            pltpu.VMEM((R, ROWS), BF16),
            pltpu.VMEM((R, ROWS), BF16),
            pltpu.VMEM((ROWS, (PIECES - HANDED) * PIECE), BF16),
            pltpu.VMEM((ROWS, PIECE), BF16),
            pltpu.VMEM((2, 2, SHARE, D), BF16),
            pltpu.VMEM((2, 2, SHARE, D), BF16),
            pltpu.VMEM((2, 4, SHARE, D), BF16),
            pltpu.VMEM((2, 4, SHARE, D), BF16),
            pltpu.VMEM((2, SHARE, D), BF16),
            pltpu.VMEM((2, SHARE, D), BF16),
            pltpu.VMEM((2, SHARE, D), BF16),
            pltpu.VMEM((2, SHARE, D), BF16),
            pltpu.VMEM((2, 4, SHARE, D), BF16),
            dma((6,)),
            dma((3 * N_GATHER,)),
            dma((3 * N_GATHER,)),
            dma((6 * N_REDUCE,)),
            dma((6 * N_REDUCE,)),
            dma((3,)),
            dma((3,)),
            dma((4 * PIECES,)),
            dma((4 * PIECES,)),
        ],
        compiler_params=pltpu.CompilerParams(
            collective_id=0, has_side_effects=True, vmem_limit_bytes=40 * 2**20
        ),
        cost_estimate=pl.CostEstimate(
            flops=14 * ROWS * D * R, bytes_accessed=12 * ROWS * D, transcendentals=3 * ROWS * R
        ),
        name="relay_tick",
    )(*(
        pltpu.with_memory_space_constraint(operand, pltpu.HBM)
        for operand in (
            section_in[0, 0], vision_rows[0], alternate, grad_in[0, 0], parked[0, 0],
            w_down[0], w_up[0],
        )
    ))
    received, stash, input_grad, up_grad, down_grad = pl.pallas_call(
        write_out,
        out_shape=(rows, rows, rows, shares, shares),
        in_specs=[pl.BlockSpec(memory_space=pltpu.VMEM)] * 5,
        out_specs=[pl.BlockSpec(memory_space=pltpu.HBM)] * 5,
        scratch_shapes=[dma((5,))],
        name="write_out",
    )(*(pltpu.with_memory_space_constraint(out, pltpu.VMEM) for out in outs))
    return (
        received[None, None],
        stash[None, None],
        input_grad[None, None],
        up_grad[None],
        down_grad[None],
    )


def solution(mesh):
    rows = P("section", "dp", None, "mp")
    shares = P("section", "dp", "mp")
    return jax.shard_map(
        local,
        mesh=mesh,
        in_specs=(rows, P("dp", None, "mp"), P("dp", None), rows, rows, shares, shares),
        out_specs=(rows, rows, rows, shares, shares),
        check_vma=False,
    )
```

```python
import functools
import math

import jax
import jax.numpy as jnp
from jax import lax
from jax.experimental import pallas as pl
from jax.experimental.pallas import tpu as pltpu
from jax.sharding import PartitionSpec as P

MESH = pl.DeviceIdType.MESH
BF16, F32 = jnp.bfloat16, jnp.float32

D = 3584
R = 256
ROWS = 104
VISION = 24
SHARE = 16
PIECES = 4
PIECE = D // PIECES
CUT = 512
HANDED = 2
HAND = 3 * PIECES
NX, NZ = 4, 4
SPLIT = 1024

N_GATHER = 16
N_REDUCE = 12

NT = (((1,), (1,)), ((), ()))
TN = (((0,), (0,)), ((), ()))

SCALE = math.sqrt(2 / math.pi)


def gelu(v):
    return 0.5 * v * (1.0 + jnp.tanh(SCALE * (v + 0.044715 * (v * v * v))))


def gelu_slope(v):
    t = jnp.tanh(SCALE * (v + 0.044715 * (v * v * v)))
    return 0.5 * (1.0 + t) + 0.5 * v * (1.0 - t * t) * (SCALE * (1.0 + 3 * 0.044715 * (v * v)))


def kernel(
    section_ref, vision_ref, alternate_ref, grad_ref, parked_ref, wd_ref, wu_ref,
    o_section, o_parked, o_input_grad, o_up, o_down,
    sec, vis, alt, grad, fwd, bwd, out, weights, parts,
    pre_out, pre_in, bwd_pre, act, slope_act, act_ts, grad_t, grads, by_right, by_left,
    hand, stop, opp_up, opp_dn, from_up, from_dn, opp2_up, opp2_dn, from2_up, from2_dn, sums,
    u_parts, u_opp_up, u_opp_dn, u_from_up, u_from_dn, ready,
    local_sem, g_send, g_recv, r_send, r_recv, m_send, m_recv, y_send, y_recv, x_send, x_recv,
):
    section = lax.axis_index("section")
    dp = lax.axis_index("dp")
    mp = lax.axis_index("mp")
    x, z = lax.div(dp, NZ), lax.rem(dp, NZ)

    def at(value, count):
        return lax.rem(value + count, count)

    def chunk(xi, zi):
        return at(xi, NX) * NZ + at(zi, NZ)

    mirror = {"section": 15 - section}
    following = {"section": lax.rem(section + 1, 16)}
    preceding = {"section": lax.rem(section + 15, 16)}
    other = {"mp": 1 - mp}
    right, left = {"dp": chunk(x + 1, z)}, {"dp": chunk(x - 1, z)}
    opposite = {"dp": chunk(x + 2, z)}
    plus, minus = {"dp": chunk(x, z + 1)}, {"dp": chunk(x, z - 1)}

    pending = []

    def remote(src, dst, send, recv, to):
        copy = pltpu.make_async_remote_copy(
            src_ref=src, dst_ref=dst, send_sem=send, recv_sem=recv,
            device_id=to, device_id_type=MESH,
        )
        return copy

    def go(copy):
        copy.start()
        pending.append(copy)

    w_refs = (wd_ref, wu_ref)
    loads = [
        pltpu.make_async_copy(section_ref, sec, local_sem.at[0]),
        pltpu.make_async_copy(vision_ref, vis, local_sem.at[1]),
        pltpu.make_async_copy(alternate_ref, alt, local_sem.at[2]),
        pltpu.make_async_copy(grad_ref, grad, local_sem.at[3]),
        pltpu.make_async_copy(wd_ref, weights.at[0, x, z], local_sem.at[4]),
        pltpu.make_async_copy(wu_ref, weights.at[1, x, z], local_sem.at[5]),
    ]
    for load in loads:
        load.start()

    y, core = lax.div(section, 2), lax.rem(section, 2)
    turn = lax.rem(y, 4)
    near = jnp.logical_or(turn == 0, turn == 3)
    far = jnp.logical_not(near)
    detours, stops, ends = turn == 2, turn == 0, turn == 1
    next_chip = {"section": lax.rem(section + 2, 16)}
    last_chip = {"section": lax.rem(section + 14, 16)}
    stop_at = {"section": lax.rem(section + 12, 16)}
    stop_from = {"section": lax.rem(section + 4, 16)}
    stop_to = {"section": lax.rem(y + 5, 8) * 2 + 1 - core}
    end_from = {"section": lax.rem(y + 3, 8) * 2 + 1 - core}

    barrier = pltpu.get_barrier_semaphore()

    def greet(*partners):
        for partner in partners:
            pl.semaphore_signal(barrier, inc=1, device_id=partner, device_id_type=MESH)

    greet(mirror, following, preceding, other, right, left, opposite, plus, minus)
    pl.when(detours)(lambda: greet(stop_at))
    pl.when(stops)(lambda: greet(stop_from, stop_to))
    pl.when(ends)(lambda: greet(end_from))
    pl.when(core == 0)(lambda: greet(next_chip, last_chip))
    extra = jnp.where(stops, 2, jnp.where(turn == 3, 0, 1))
    pl.semaphore_wait(barrier, 9 + extra + 2 * (1 - core))

    def piece(i):
        return pl.ds(i * PIECE, PIECE)

    def y_piece(src, dst, index, i, to):
        return remote(
            src.at[:, piece(i)], dst.at[:, piece(i)], y_send.at[index], y_recv.at[index], to
        )

    parked_copies = [y_piece(parked_ref, bwd, i, i, mirror) for i in range(PIECES)]
    forward_copies = [y_piece(fwd, o_parked, PIECES + i, i, mirror) for i in range(PIECES)]
    shift_copies = [y_piece(out, o_section, 2 * PIECES + i, i, following) for i in range(PIECES)]
    for copy in parked_copies:
        go(copy)

    def send_forward(pieces, when):
        @pl.when(when)
        def _():
            for i in pieces:
                forward_copies[i].start()

    hand_copies, pass_copies = {}, {}
    for i in range(HANDED, PIECES):
        held = hand.at[:, pl.ds((i - HANDED) * PIECE, PIECE)]
        hand_copies[i] = remote(
            out.at[:, piece(i)], held, y_send.at[HAND + i], y_recv.at[HAND + i], preceding
        )
        pass_copies[i] = remote(
            held, o_section.at[:, piece(i)],
            y_send.at[HAND + i], y_recv.at[2 * PIECES + i], next_chip,
        )

    last = PIECES - 1
    detour_in = remote(
        fwd.at[:, piece(last)], stop, y_send.at[3 * PIECES], y_recv.at[3 * PIECES], stop_at
    )
    detour_out = remote(
        stop, o_parked.at[:, piece(last)],
        y_send.at[3 * PIECES + 1], y_recv.at[PIECES + last], stop_to,
    )

    class Gather:
        def __init__(self, number, w, start, stop, x_first):
            self.base, self.w, self.start, self.stop = number * N_GATHER, w, start, stop
            self.x_first = x_first
            self.a, self.b = (x, z) if x_first else (z, x)
            xs, zs = (right, left), (plus, minus)
            (self.up, self.dn), (self.up2, self.dn2) = (xs, zs) if x_first else (zs, xs)
            middle = (start + stop) // 2
            self.all = pl.ds(start, stop - start)
            self.low, self.high = pl.ds(start, middle - start), pl.ds(middle, stop - middle)

        def copy(self, m, to, a=0, b=0, cols=None):
            cols = self.all if cols is None else cols
            a, b = at(self.a + a, 4), at(self.b + b, 4)
            xi, zi = (a, b) if self.x_first else (b, a)
            place = weights.at[self.w, xi, zi, :, cols]
            index = self.base + m
            return remote(place, place, g_send.at[index], g_recv.at[index], to)

        def start1(self):
            go(self.copy(0, self.up))
            go(self.copy(1, self.dn))

        def start2(self, k):
            go(self.copy(4 + k, self.up2, a=k))
            go(self.copy(8 + k, self.dn2, a=k))

        def near1(self, side):
            self.copy(side, (self.up, self.dn)[side]).wait_recv()
            if side == 0:
                go(self.copy(2, self.up, a=-1, cols=self.low))
                self.start2(3)
            else:
                go(self.copy(3, self.dn, a=1, cols=self.high))
                self.start2(1)

        def far1(self):
            self.copy(2, self.up, cols=self.low).wait_recv()
            self.copy(3, self.dn, cols=self.high).wait_recv()
            self.start2(2)

        def near2(self, k, side):
            self.copy(4 + 4 * side + k, (self.up2, self.dn2)[side]).wait_recv()
            if k % 2 == 0 and side == 0:
                go(self.copy(12 + k // 2, self.up2, a=k, b=-1))
            if k % 2 == 1 and side == 1:
                go(self.copy(14 + k // 2, self.dn2, a=k, b=1))

        def far2(self, k):
            if k % 2 == 0:
                self.copy(12 + k // 2, self.up2).wait_recv()
            else:
                self.copy(14 + k // 2, self.dn2).wait_recv()

    down = Gather(0, 0, SPLIT, D, False)
    up = Gather(1, 1, SPLIT, D, False)
    both = Gather(2, slice(None), 0, SPLIT, True)

    def exchange(slot):
        return remote(
            pre_out.at[slot], pre_in.at[slot], m_send.at[slot], m_recv.at[slot], other
        )

    def weight(w, cols):
        block = weights[w, :, :, :, cols]
        return block.reshape(R, block.shape[-1])

    def partial(slot, rows, w):
        total = jnp.zeros((ROWS, R), F32)
        for i in range(PIECES):
            total += lax.dot_general(
                rows[:, piece(i)], weight(w, piece(i)), NT, preferred_element_type=F32
            )
        send_partial(slot, total)

    def send_partial(slot, total):
        pre_out[slot] = total.astype(BF16)
        go(exchange(slot))

    def summed(slot):
        exchange(slot).wait_recv()
        return pre_out[slot].astype(F32) + pre_in[slot].astype(F32)

    for load in loads[4:]:
        load.wait()
    def choose_rows():
        for load in loads[:3]:
            load.wait()
        picks = jnp.where(section == 0, alt[...], -1)
        chosen_t = (lax.broadcasted_iota(jnp.int32, (VISION, ROWS), 0) == picks).astype(BF16)
        hit = lax.dot_general(
            chosen_t, jnp.ones((VISION, PIECE), BF16), TN, preferred_element_type=F32
        )

        for i in range(PIECES):
            cols = piece(i)
            chosen = lax.dot_general(chosen_t, vis[:, cols], TN, preferred_element_type=F32)
            fwd[:, cols] = jnp.where(hit > 0.5, chosen, sec[:, cols].astype(F32)).astype(BF16)
        pl.when(detours)(detour_in.start)

        def backward_rows():
            total = jnp.zeros((ROWS, R), F32)
            for i in range(PIECES):
                parked_copies[i].wait_recv()
                send_forward([i], near)
                cols = piece(i)
                total += lax.dot_general(
                    bwd[:, cols], weight(0, cols), NT, preferred_element_type=F32
                )
            send_partial(2, total)

            @pl.when(stops)
            def _():
                detour_in.wait_recv()
                detour_out.start()

    def quarter(k, first=0, size=PIECE):
        return pl.ds(pl.multiple_of(at(x + k, NX) * PIECE + first, 128), size)

    def x_copy(m, src, dst, to):
        return remote(src, dst, x_send.at[m], x_recv.at[m], to)

    lows, highs = pl.ds(0, CUT), pl.ds(CUT, PIECE - CUT)
    from_x = [at(x + k, NX) for k in range(-1, 2)]
    row_copies = [
        x_copy(0, grad.at[:, quarter(1)], grads.at[x], right),
        x_copy(1, grad.at[:, quarter(-1)], grads.at[x], left),
        x_copy(2, grad.at[:, quarter(2, 0, CUT)], by_right, right),
        x_copy(3, grad.at[:, quarter(2, CUT, PIECE - CUT)], by_left, left),
        x_copy(4, by_right, grads.at[from_x[0], :, lows], right),
        x_copy(5, by_left, grads.at[from_x[2], :, highs], left),
    ]
    act_copies = [
        x_copy(6, act_ts.at[x], act_ts.at[x], right),
        x_copy(7, act_ts.at[x], act_ts.at[x], left),
        x_copy(8, act_ts.at[from_x[0]], act_ts.at[from_x[0]], right),
    ]

    def rows_far():
        go(row_copies[2])
        go(row_copies[3])

    def rows_near():
        go(row_copies[0])
        go(row_copies[1])
        grads[x] = grad[:, quarter(0)]

    def rows_relay(side):
        row_copies[2 + side].wait_recv()
        go(row_copies[4 + side])

    def rows_done():
        for m in (0, 1, 4, 5):
            row_copies[m].wait_recv()

    def act_send():
        go(act_copies[0])
        go(act_copies[1])

    def act_relay():
        act_copies[0].wait_recv()
        go(act_copies[2])

    def act_done():
        act_copies[1].wait_recv()
        act_copies[2].wait_recv()

    def backward_rows():
        total = jnp.zeros((ROWS, R), F32)
        for i in range(PIECES):
            parked_copies[i].wait_recv()
            send_forward([i], near)
            cols = piece(i)
            total += lax.dot_general(
                bwd[:, cols], weight(0, cols), NT, preferred_element_type=F32
            )
        send_partial(2, total)

        @pl.when(stops)
        def _():
            detour_in.wait_recv()
            detour_out.start()

    def backward_act():
        bwd_pre[...] = summed(2)
        act_ts[x] = gelu(bwd_pre[...]).astype(BF16).T

    def slopes():
        pre_grad = (summed(1) * gelu_slope(bwd_pre[...])).astype(BF16)
        slope_act[...] = pre_grad
        grad_t[...] = pre_grad.T

    def outputs(i):
        cols = piece(i)
        product = jnp.dot(act[...], weight(1, cols), preferred_element_type=F32)
        out[:, cols] = (fwd[:, cols].astype(F32) + product).astype(BF16)
        if i < HANDED:
            go(shift_copies[i])
        else:
            pl.when(core == 0)(shift_copies[i].start)
            pl.when(core == 1)(hand_copies[i].start)

    def pass_on():
        @pl.when(core == 0)
        def _():
            for i in range(HANDED, PIECES):
                hand_copies[i].wait_recv()
                pass_copies[i].start()

    def add_into(total, term):
        total[...] = (total[...].astype(F32) + term[...].astype(F32)).astype(BF16)

    class Reduce:
        def __init__(self, number, place, start, stop, x_first):
            self.base, self.start, self.stop = number * N_REDUCE, start, stop
            self.parts, self.opp_up, self.opp_dn, self.from_up, self.from_dn = place
            self.x_first = x_first
            self.a, self.b = (x, z) if x_first else (z, x)
            xs, zs = (right, left), (plus, minus)
            (self.up, self.dn), (self.up2, self.dn2) = (xs, zs) if x_first else (zs, xs)
            middle = (start + stop) // 2
            self.all = pl.ds(start, stop - start)
            self.low, self.high = pl.ds(start, middle - start), pl.ds(middle, stop - middle)

        def block(self, a, b0, count):
            a = at(self.a + a, 4)
            if self.x_first:
                return self.parts.at[a, pl.ds(b0, count), :, self.all]
            return self.parts.at[pl.ds(b0, count), a, :, self.all]

        def term(self, ref, b0, count):
            return ref.at[pl.ds(b0, count), :, self.all]

        def total(self, b, cols):
            return sums.at[at(self.b + b, 4), :, cols]

        def copy(self, m):
            src, dst, to = (
                lambda: (self.block(2, 0, 2), self.term(self.opp_up, 0, 2), self.dn),
                lambda: (self.block(2, 2, 2), self.term(self.opp_dn, 0, 2), self.up),
                lambda: (self.block(-1, 2, 2), self.term(self.from_up, 2, 2), self.dn),
                lambda: (self.block(1, 0, 2), self.term(self.from_dn, 0, 2), self.up),
                lambda: (self.block(-1, 0, 2), self.term(self.from_up, 0, 2), self.dn),
                lambda: (self.block(1, 2, 2), self.term(self.from_dn, 2, 2), self.up),
                lambda: (self.total(2, self.low), opp2_up.at[:, self.low], self.dn2),
                lambda: (self.total(2, self.high), opp2_dn.at[:, self.high], self.up2),
                lambda: (self.total(-1, self.high), from2_up.at[:, self.high], self.dn2),
                lambda: (self.total(1, self.low), from2_dn.at[:, self.low], self.up2),
                lambda: (self.total(-1, self.low), from2_up.at[:, self.low], self.dn2),
                lambda: (self.total(1, self.high), from2_dn.at[:, self.high], self.up2),
            )[m]()
            return self.message(m, src, dst, to)

        def message(self, m, src, dst, to):
            index = self.base + m
            return remote(src, dst, r_send.at[index], r_recv.at[index], to)

        def send_far(self):
            steps = -(-(self.stop - self.start) // 640)
            width = (self.stop - self.start) // steps
            for i in range(steps):
                cols = pl.ds(self.start + i * width, width)
                product = jnp.dot(grad_t[...], bwd[:, cols], preferred_element_type=F32)
                parts[:, :, :, cols] = product.astype(BF16).reshape(NX, NZ, SHARE, width)
            go(self.copy(0))
            go(self.copy(1))

        def send_near(self):
            go(self.copy(2))
            go(self.copy(3))

        def relay(self, side):
            self.copy(side).wait_recv()
            if side == 0:
                add_into(self.block(-1, 0, 2), self.term(self.opp_up, 0, 2))
            else:
                add_into(self.block(1, 2, 2), self.term(self.opp_dn, 0, 2))
            go(self.copy(4 + side))

        def folded(self):
            for m in (2, 3, 4, 5):
                self.copy(m).wait_recv()
            return (
                self.block(0, 0, 4)[...].astype(F32)
                + self.term(self.from_up, 0, 4)[...].astype(F32)
                + self.term(self.from_dn, 0, 4)[...].astype(F32)
            )

        def fold(self):
            self.term(sums, 0, 4)[...] = self.folded().astype(BF16)
            for m in (6, 7, 8, 9):
                go(self.copy(m))

        def relay2(self, side):
            self.copy(6 + side).wait_recv()
            if side == 0:
                add_into(self.total(-1, self.low), opp2_up.at[:, self.low])
            else:
                add_into(self.total(1, self.high), opp2_dn.at[:, self.high])
            go(self.copy(10 + side))

        def finish(self):
            cols = self.all
            for m in (8, 9, 10, 11):
                self.copy(m).wait_recv()
            total = (
                parts[x, z, :, cols].astype(F32)
                + from_up[self.b, :, cols].astype(F32)
                + from_dn[self.b, :, cols].astype(F32)
                + from2_up[:, cols].astype(F32)
                + from2_dn[:, cols].astype(F32)
            )
            o_down[:, cols] = (total * (1.0 / 16)).astype(BF16)

    class ReduceUp(Reduce):
        def send_far(self):
            for cols in (lows, highs):
                product = jnp.zeros((R, cols.size), F32)
                for i in range(NX):
                    product += jnp.dot(
                        act_ts[i], grads[i, :, cols], preferred_element_type=F32
                    )
                u_parts[:, :, :, cols] = product.astype(BF16).reshape(NX, NZ, SHARE, cols.size)
            go(self.copy(0))
            go(self.copy(1))

        def owner(self, m):
            k, to = ((1, right), (-1, left), (2, opposite))[m]
            return self.message(6 + m, ready.at[at(x + k, NX)], o_up.at[:, quarter(0)], to)

        def fold(self):
            ready[...] = (self.folded() * (1.0 / 16)).astype(BF16)
            for m in (2, 0, 1):
                go(self.owner(m))
            o_up[:, quarter(0)] = ready[x]

        def finish(self):
            for m in range(3):
                self.owner(m).wait_recv()

    def input_grad(i):
        cols = piece(i)
        product = jnp.dot(slope_act[...], weight(0, cols), preferred_element_type=F32)
        o_input_grad[:, cols] = (grad[:, cols].astype(F32) + product).astype(BF16)

    down_place = (parts, opp_up, opp_dn, from_up, from_dn)
    up_place = (u_parts, u_opp_up, u_opp_dn, u_from_up, u_from_dn)
    d0, d1 = Reduce(0, down_place, 512, 2048, True), Reduce(1, down_place, 2048, D, True)
    dz = Reduce(2, down_place, 0, 512, False)
    u0 = ReduceUp(3, up_place, 0, PIECE, False)

    both.start1()
    down.start2(0)
    down.start1()
    up.start2(0)
    both.start2(0)
    up.start1()
    loads[3].wait()
    rows_far()
    rows_near()
    choose_rows()
    both.near1(0)
    both.near1(1)
    down.near2(0, 0)
    down.near2(0, 1)
    up.near2(0, 0)
    up.near2(0, 1)
    rows_relay(1)
    both.far1()
    both.near2(0, 0)
    both.near2(0, 1)
    rows_relay(0)
    down.near1(0)
    down.near1(1)
    up.near1(1)
    up.near1(0)
    down.far2(0)
    down.near2(3, 1)
    up.far2(0)
    down.near2(1, 1)
    both.near2(3, 1)
    both.near2(1, 1)
    up.near2(1, 1)
    up.near2(3, 1)
    both.near2(3, 0)
    both.near2(1, 0)
    both.near2(2, 1)
    down.far1()
    down.near2(3, 0)
    down.near2(1, 0)
    up.far1()
    rows_done()
    up.near2(1, 0)
    up.near2(3, 0)
    both.near2(2, 0)
    both.far2(0)
    down.far2(3)
    down.far2(1)
    down.near2(2, 0)
    both.far2(3)
    both.far2(1)
    up.near2(2, 0)
    both.far2(2)
    up.far2(1)
    up.far2(3)
    down.near2(2, 1)
    up.near2(2, 1)
    down.far2(2)
    backward_rows()
    partial(0, fwd, 0)
    up.far2(2)
    partial(1, grad, 1)
    backward_act()
    act_send()
    act[...] = gelu(summed(0)).astype(BF16)
    outputs(0)
    outputs(1)
    outputs(2)
    slopes()
    dz.send_far()
    act_relay()
    dz.send_near()
    d0.send_far()
    d1.send_far()
    d0.send_near()
    d1.send_near()
    outputs(3)
    send_forward(range(last), far)
    send_forward([last], ends)
    act_done()
    u0.send_far()
    dz.relay(1)
    dz.relay(0)
    u0.send_near()
    input_grad(0)
    input_grad(1)
    pass_on()
    input_grad(2)
    d0.relay(0)
    input_grad(3)
    d0.relay(1)
    d1.relay(1)
    d1.relay(0)
    dz.fold()
    u0.relay(0)
    u0.relay(1)
    d0.fold()
    dz.relay2(0)
    dz.relay2(1)
    d1.fold()
    dz.finish()
    d0.relay2(0)
    d0.relay2(1)
    u0.fold()
    d1.relay2(0)
    d1.relay2(1)
    d0.finish()
    u0.finish()
    d1.finish()

    for copy in forward_copies + shift_copies:
        copy.wait_recv()
    for copy in pending + forward_copies[:last]:
        copy.wait_send()
    pl.when(jnp.logical_not(detours))(forward_copies[last].wait_send)
    pl.when(detours)(detour_in.wait_send)
    for i in range(HANDED, PIECES):
        pl.when(core == 0)(shift_copies[i].wait_send)
        pl.when(core == 0)(pass_copies[i].wait_send)
        pl.when(core == 1)(hand_copies[i].wait_send)
    pl.when(stops)(detour_out.wait_send)


def write_out(*refs):
    copies = [
        pltpu.make_async_copy(refs[i], refs[5 + i], refs[10].at[i]) for i in range(5)
    ]
    for copy in copies:
        copy.start()
    for copy in copies:
        copy.wait()


def local(section_in, vision_rows, alternate, grad_in, parked, w_down, w_up):
    rows = jax.ShapeDtypeStruct((ROWS, D), BF16)
    shares = jax.ShapeDtypeStruct((SHARE, D), BF16)
    dma = pltpu.SemaphoreType.DMA
    outs = pl.pallas_call(
        kernel,
        out_shape=(pltpu.VMEM((ROWS, D), BF16),) * 3 + (pltpu.VMEM((SHARE, D), BF16),) * 2,
        in_specs=[pl.BlockSpec(memory_space=pltpu.HBM)] * 7,
        out_specs=[pl.BlockSpec(memory_space=pltpu.VMEM)] * 5,
        scratch_shapes=[
            pltpu.VMEM((ROWS, D), BF16),
            pltpu.VMEM((VISION, D), BF16),
            pltpu.VMEM((1, ROWS), jnp.int32),
            pltpu.VMEM((ROWS, D), BF16),
            pltpu.VMEM((ROWS, D), BF16),
            pltpu.VMEM((ROWS, D), BF16),
            pltpu.VMEM((ROWS, D), BF16),
            pltpu.VMEM((2, NX, NZ, SHARE, D), BF16),
            pltpu.VMEM((NX, NZ, SHARE, D), BF16),
            pltpu.VMEM((3, ROWS, R), BF16),
            pltpu.VMEM((3, ROWS, R), BF16),
            pltpu.VMEM((ROWS, R), F32),
            pltpu.VMEM((ROWS, R), BF16),
            pltpu.VMEM((ROWS, R), BF16),
            pltpu.VMEM((NX, R, ROWS), BF16),
            pltpu.VMEM((R, ROWS), BF16),
            pltpu.VMEM((NX, ROWS, PIECE), BF16),
            pltpu.VMEM((ROWS, CUT), BF16),
            pltpu.VMEM((ROWS, PIECE - CUT), BF16),
            pltpu.VMEM((ROWS, (PIECES - HANDED) * PIECE), BF16),
            pltpu.VMEM((ROWS, PIECE), BF16),
            pltpu.VMEM((2, SHARE, D), BF16),
            pltpu.VMEM((2, SHARE, D), BF16),
            pltpu.VMEM((4, SHARE, D), BF16),
            pltpu.VMEM((4, SHARE, D), BF16),
            pltpu.VMEM((SHARE, D), BF16),
            pltpu.VMEM((SHARE, D), BF16),
            pltpu.VMEM((SHARE, D), BF16),
            pltpu.VMEM((SHARE, D), BF16),
            pltpu.VMEM((4, SHARE, D), BF16),
            pltpu.VMEM((NX, NZ, SHARE, PIECE), BF16),
            pltpu.VMEM((2, SHARE, PIECE), BF16),
            pltpu.VMEM((2, SHARE, PIECE), BF16),
            pltpu.VMEM((4, SHARE, PIECE), BF16),
            pltpu.VMEM((4, SHARE, PIECE), BF16),
            pltpu.VMEM((4, SHARE, PIECE), BF16),
            dma((6,)),
            dma((3 * N_GATHER,)),
            dma((3 * N_GATHER,)),
            dma((4 * N_REDUCE,)),
            dma((4 * N_REDUCE,)),
            dma((3,)),
            dma((3,)),
            dma((4 * PIECES,)),
            dma((4 * PIECES,)),
            dma((9,)),
            dma((9,)),
        ],
        compiler_params=pltpu.CompilerParams(
            collective_id=0, has_side_effects=True, vmem_limit_bytes=40 * 2**20
        ),
        cost_estimate=pl.CostEstimate(
            flops=14 * ROWS * D * R, bytes_accessed=12 * ROWS * D, transcendentals=3 * ROWS * R
        ),
        name="relay_tick",
    )(*(
        pltpu.with_memory_space_constraint(operand, pltpu.HBM)
        for operand in (
            section_in[0, 0], vision_rows[0], alternate, grad_in[0, 0], parked[0, 0],
            w_down[0], w_up[0],
        )
    ))
    received, stash, input_grad, up_grad, down_grad = pl.pallas_call(
        write_out,
        out_shape=(rows, rows, rows, shares, shares),
        in_specs=[pl.BlockSpec(memory_space=pltpu.VMEM)] * 5,
        out_specs=[pl.BlockSpec(memory_space=pltpu.HBM)] * 5,
        scratch_shapes=[dma((5,))],
        name="write_out",
    )(*(pltpu.with_memory_space_constraint(out, pltpu.VMEM) for out in outs))
    return (
        received[None, None],
        stash[None, None],
        input_grad[None, None],
        up_grad[None],
        down_grad[None],
    )


def solution(mesh):
    rows = P("section", "dp", None, "mp")
    shares = P("section", "dp", "mp")
    return jax.shard_map(
        local,
        mesh=mesh,
        in_specs=(rows, P("dp", None, "mp"), P("dp", None), rows, rows, shares, shares),
        out_specs=(rows, rows, rows, shares, shares),
        check_vma=False,
    )
```

```python
import functools
import math

import jax
import jax.numpy as jnp
from jax import lax
from jax.experimental import pallas as pl
from jax.experimental.pallas import tpu as pltpu
from jax.sharding import PartitionSpec as P

MESH = pl.DeviceIdType.MESH
BF16, F32 = jnp.bfloat16, jnp.float32

D = 3584
R = 256
ROWS = 104
VISION = 24
SHARE = 16
PIECES = 4
PIECE = D // PIECES
CUT = 512
HANDED = 2
HAND = 3 * PIECES
NX, NZ = 4, 4
SPLIT = 1024

N_GATHER = 16
N_REDUCE = 12

NT = (((1,), (1,)), ((), ()))
TN = (((0,), (0,)), ((), ()))

SCALE = math.sqrt(2 / math.pi)


def gelu(v):
    return 0.5 * v * (1.0 + jnp.tanh(SCALE * (v + 0.044715 * (v * v * v))))


def gelu_slope(v):
    t = jnp.tanh(SCALE * (v + 0.044715 * (v * v * v)))
    return 0.5 * (1.0 + t) + 0.5 * v * (1.0 - t * t) * (SCALE * (1.0 + 3 * 0.044715 * (v * v)))


def kernel(
    section_ref, vision_ref, alternate_ref, grad_ref, parked_ref, wd_ref, wu_ref,
    o_section, o_parked, o_input_grad, o_up, o_down,
    sec, vis, alt, grad, fwd, bwd, out, weights, parts,
    pre_out, pre_in, bwd_pre, act, slope_act, act_ts, grad_t, grads, by_right, by_left,
    hand, stop, opp_up, opp_dn, from_up, from_dn, opp2_up, opp2_dn, from2_up, from2_dn, sums,
    u_parts, u_opp_up, u_opp_dn, u_from_up, u_from_dn, ready,
    local_sem, g_send, g_recv, r_send, r_recv, m_send, m_recv, y_send, y_recv, x_send, x_recv, y_go, xz_go,
):
    section = lax.axis_index("section")
    dp = lax.axis_index("dp")
    mp = lax.axis_index("mp")
    x, z = lax.div(dp, NZ), lax.rem(dp, NZ)

    def at(value, count):
        return lax.rem(value + count, count)

    def chunk(xi, zi):
        return at(xi, NX) * NZ + at(zi, NZ)

    mirror = {"section": 15 - section}
    following = {"section": lax.rem(section + 1, 16)}
    preceding = {"section": lax.rem(section + 15, 16)}
    other = {"mp": 1 - mp}
    right, left = {"dp": chunk(x + 1, z)}, {"dp": chunk(x - 1, z)}
    opposite = {"dp": chunk(x + 2, z)}
    plus, minus = {"dp": chunk(x, z + 1)}, {"dp": chunk(x, z - 1)}

    pending = []

    def remote(src, dst, send, recv, to):
        copy = pltpu.make_async_remote_copy(
            src_ref=src, dst_ref=dst, send_sem=send, recv_sem=recv,
            device_id=to, device_id_type=MESH,
        )
        return copy

    def go(copy):
        copy.start()
        pending.append(copy)

    w_refs = (wd_ref, wu_ref)
    loads = [
        pltpu.make_async_copy(section_ref, sec, local_sem.at[0]),
        pltpu.make_async_copy(vision_ref, vis, local_sem.at[1]),
        pltpu.make_async_copy(alternate_ref, alt, local_sem.at[2]),
        pltpu.make_async_copy(grad_ref, grad, local_sem.at[3]),
        pltpu.make_async_copy(wd_ref, weights.at[0, x, z], local_sem.at[4]),
        pltpu.make_async_copy(wu_ref, weights.at[1, x, z], local_sem.at[5]),
    ]
    y, core = lax.div(section, 2), lax.rem(section, 2)
    turn = lax.rem(y, 4)
    near = jnp.logical_or(turn == 0, turn == 3)
    far = jnp.logical_not(near)
    detours, stops, ends = turn == 2, turn == 0, turn == 1
    next_chip = {"section": lax.rem(section + 2, 16)}
    stop_at = {"section": lax.rem(section + 12, 16)}
    stop_to = {"section": lax.rem(y + 5, 8) * 2 + 1 - core}

    barrier = pltpu.get_barrier_semaphore()

    def greet(*partners):
        for partner in partners:
            pl.semaphore_signal(barrier, inc=1, device_id=partner, device_id_type=MESH)

    def chip_y(value):
        return {"section": 2 * lax.rem(value + 8, 8)}

    mate = {"section": section + 1 - 2 * core}
    greet(mate, chip_y(7 - y), chip_y(y + 1), chip_y(y - 1))
    pl.when(detours)(lambda: greet(chip_y(y - 2)))
    pl.when(stops)(lambda: greet(chip_y(y + 2), chip_y(y + 5)))
    pl.when(ends)(lambda: greet(chip_y(y + 3)))
    greet(*({**to, "section": 2 * y + 1} for to in (right, left, opposite, plus, minus, other)))
    for load in loads:
        load.start()
    extra = jnp.where(stops, 2, jnp.where(turn == 3, 0, 1))

    @pl.when(core == 0)
    def _():
        pl.semaphore_wait(barrier, 7 + 2 * extra)
        pl.semaphore_signal(y_go, inc=1, device_id=mate, device_id_type=MESH)

    @pl.when(core == 1)
    def _():
        pl.semaphore_wait(y_go, 1)

    def piece(i):
        return pl.ds(i * PIECE, PIECE)

    def y_piece(src, dst, index, i, to):
        return remote(
            src.at[:, piece(i)], dst.at[:, piece(i)], y_send.at[index], y_recv.at[index], to
        )

    parked_copies = [y_piece(parked_ref, bwd, i, i, mirror) for i in range(PIECES)]
    forward_copies = [y_piece(fwd, o_parked, PIECES + i, i, mirror) for i in range(PIECES)]
    shift_copies = [y_piece(out, o_section, 2 * PIECES + i, i, following) for i in range(PIECES)]
    for copy in parked_copies:
        go(copy)

    @pl.when(core == 1)
    def _():
        pl.semaphore_wait(barrier, 13)
        pl.semaphore_signal(xz_go, inc=1, device_id=mate, device_id_type=MESH)

    @pl.when(core == 0)
    def _():
        pl.semaphore_wait(xz_go, 1)

    def send_forward(pieces, when):
        @pl.when(when)
        def _():
            for i in pieces:
                forward_copies[i].start()

    hand_copies, pass_copies = {}, {}
    for i in range(HANDED, PIECES):
        held = hand.at[:, pl.ds((i - HANDED) * PIECE, PIECE)]
        hand_copies[i] = remote(
            out.at[:, piece(i)], held, y_send.at[HAND + i], y_recv.at[HAND + i], preceding
        )
        pass_copies[i] = remote(
            held, o_section.at[:, piece(i)],
            y_send.at[HAND + i], y_recv.at[2 * PIECES + i], next_chip,
        )

    last = PIECES - 1
    detour_in = remote(
        fwd.at[:, piece(last)], stop, y_send.at[3 * PIECES], y_recv.at[3 * PIECES], stop_at
    )
    detour_out = remote(
        stop, o_parked.at[:, piece(last)],
        y_send.at[3 * PIECES + 1], y_recv.at[PIECES + last], stop_to,
    )

    class Gather:
        def __init__(self, number, w, start, stop, x_first):
            self.base, self.w, self.start, self.stop = number * N_GATHER, w, start, stop
            self.x_first = x_first
            self.a, self.b = (x, z) if x_first else (z, x)
            xs, zs = (right, left), (plus, minus)
            (self.up, self.dn), (self.up2, self.dn2) = (xs, zs) if x_first else (zs, xs)
            middle = (start + stop) // 2
            self.all = pl.ds(start, stop - start)
            self.low, self.high = pl.ds(start, middle - start), pl.ds(middle, stop - middle)

        def copy(self, m, to, a=0, b=0, cols=None):
            cols = self.all if cols is None else cols
            a, b = at(self.a + a, 4), at(self.b + b, 4)
            xi, zi = (a, b) if self.x_first else (b, a)
            place = weights.at[self.w, xi, zi, :, cols]
            index = self.base + m
            return remote(place, place, g_send.at[index], g_recv.at[index], to)

        def start1(self):
            go(self.copy(0, self.up))
            go(self.copy(1, self.dn))

        def start2(self, k):
            go(self.copy(4 + k, self.up2, a=k))
            go(self.copy(8 + k, self.dn2, a=k))

        def near1(self, side):
            self.copy(side, (self.up, self.dn)[side]).wait_recv()
            if side == 0:
                go(self.copy(2, self.up, a=-1, cols=self.low))
                self.start2(3)
            else:
                go(self.copy(3, self.dn, a=1, cols=self.high))
                self.start2(1)

        def far1(self):
            self.copy(2, self.up, cols=self.low).wait_recv()
            self.copy(3, self.dn, cols=self.high).wait_recv()
            self.start2(2)

        def near2(self, k, side):
            self.copy(4 + 4 * side + k, (self.up2, self.dn2)[side]).wait_recv()
            if k % 2 == 0 and side == 0:
                go(self.copy(12 + k // 2, self.up2, a=k, b=-1))
            if k % 2 == 1 and side == 1:
                go(self.copy(14 + k // 2, self.dn2, a=k, b=1))

        def far2(self, k):
            if k % 2 == 0:
                self.copy(12 + k // 2, self.up2).wait_recv()
            else:
                self.copy(14 + k // 2, self.dn2).wait_recv()

    down = Gather(0, 0, SPLIT, D, False)
    up = Gather(1, 1, SPLIT, D, False)
    both = Gather(2, slice(None), 0, SPLIT, True)

    def exchange(slot):
        return remote(
            pre_out.at[slot], pre_in.at[slot], m_send.at[slot], m_recv.at[slot], other
        )

    def weight(w, cols):
        block = weights[w, :, :, :, cols]
        return block.reshape(R, block.shape[-1])

    def partial(slot, rows, w):
        total = jnp.zeros((ROWS, R), F32)
        for i in range(PIECES):
            total += lax.dot_general(
                rows[:, piece(i)], weight(w, piece(i)), NT, preferred_element_type=F32
            )
        send_partial(slot, total)

    def send_partial(slot, total):
        pre_out[slot] = total.astype(BF16)
        go(exchange(slot))

    def summed(slot):
        exchange(slot).wait_recv()
        return pre_out[slot].astype(F32) + pre_in[slot].astype(F32)

    for load in loads[4:]:
        load.wait()
    def choose_rows():
        for load in loads[:3]:
            load.wait()
        picks = jnp.where(section == 0, alt[...], -1)
        chosen_t = (lax.broadcasted_iota(jnp.int32, (VISION, ROWS), 0) == picks).astype(BF16)
        hit = lax.dot_general(
            chosen_t, jnp.ones((VISION, PIECE), BF16), TN, preferred_element_type=F32
        )

        for i in range(PIECES):
            cols = piece(i)
            chosen = lax.dot_general(chosen_t, vis[:, cols], TN, preferred_element_type=F32)
            fwd[:, cols] = jnp.where(hit > 0.5, chosen, sec[:, cols].astype(F32)).astype(BF16)
        pl.when(detours)(detour_in.start)
        send_forward(range(PIECES), near)

    def quarter(k, first=0, size=PIECE):
        return pl.ds(pl.multiple_of(at(x + k, NX) * PIECE + first, 128), size)

    def x_copy(m, src, dst, to):
        return remote(src, dst, x_send.at[m], x_recv.at[m], to)

    lows, highs = pl.ds(0, CUT), pl.ds(CUT, PIECE - CUT)
    from_x = [at(x + k, NX) for k in range(-1, 2)]
    row_copies = [
        x_copy(0, grad.at[:, quarter(1)], grads.at[x], right),
        x_copy(1, grad.at[:, quarter(-1)], grads.at[x], left),
        x_copy(2, grad.at[:, quarter(2, 0, CUT)], by_right, right),
        x_copy(3, grad.at[:, quarter(2, CUT, PIECE - CUT)], by_left, left),
        x_copy(4, by_right, grads.at[from_x[0], :, lows], right),
        x_copy(5, by_left, grads.at[from_x[2], :, highs], left),
    ]
    act_copies = [
        x_copy(6, act_ts.at[x], act_ts.at[x], right),
        x_copy(7, act_ts.at[x], act_ts.at[x], left),
        x_copy(8, act_ts.at[from_x[0]], act_ts.at[from_x[0]], right),
    ]

    def rows_far():
        go(row_copies[2])
        go(row_copies[3])

    def rows_near():
        go(row_copies[0])
        go(row_copies[1])
        grads[x] = grad[:, quarter(0)]

    def rows_relay(side):
        row_copies[2 + side].wait_recv()
        go(row_copies[4 + side])

    def rows_done():
        for m in (0, 1, 4, 5):
            row_copies[m].wait_recv()

    def act_send():
        go(act_copies[0])
        go(act_copies[1])

    def act_relay():
        act_copies[0].wait_recv()
        go(act_copies[2])

    def act_done():
        act_copies[1].wait_recv()
        act_copies[2].wait_recv()

    def backward_rows():
        total = jnp.zeros((ROWS, R), F32)
        for i in range(PIECES):
            parked_copies[i].wait_recv()
            cols = piece(i)
            total += lax.dot_general(
                bwd[:, cols], weight(0, cols), NT, preferred_element_type=F32
            )
        send_partial(2, total)

        @pl.when(stops)
        def _():
            detour_in.wait_recv()
            detour_out.start()

    def backward_act():
        bwd_pre[...] = summed(2)
        act_ts[x] = gelu(bwd_pre[...]).astype(BF16).T

    def slopes():
        pre_grad = (summed(1) * gelu_slope(bwd_pre[...])).astype(BF16)
        slope_act[...] = pre_grad
        grad_t[...] = pre_grad.T

    def outputs(i):
        cols = piece(i)
        product = jnp.dot(act[...], weight(1, cols), preferred_element_type=F32)
        out[:, cols] = (fwd[:, cols].astype(F32) + product).astype(BF16)
        if i < HANDED:
            go(shift_copies[i])
        else:
            pl.when(core == 0)(shift_copies[i].start)
            pl.when(core == 1)(hand_copies[i].start)

    def pass_on():
        @pl.when(core == 0)
        def _():
            for i in range(HANDED, PIECES):
                hand_copies[i].wait_recv()
                pass_copies[i].start()

    def add_into(total, term):
        total[...] = (total[...].astype(F32) + term[...].astype(F32)).astype(BF16)

    class Reduce:
        def __init__(self, number, place, start, stop, x_first):
            self.base, self.start, self.stop = number * N_REDUCE, start, stop
            self.parts, self.opp_up, self.opp_dn, self.from_up, self.from_dn = place
            self.x_first = x_first
            self.a, self.b = (x, z) if x_first else (z, x)
            xs, zs = (right, left), (plus, minus)
            (self.up, self.dn), (self.up2, self.dn2) = (xs, zs) if x_first else (zs, xs)
            middle = (start + stop) // 2
            self.all = pl.ds(start, stop - start)
            self.low, self.high = pl.ds(start, middle - start), pl.ds(middle, stop - middle)

        def block(self, a, b0, count):
            a = at(self.a + a, 4)
            if self.x_first:
                return self.parts.at[a, pl.ds(b0, count), :, self.all]
            return self.parts.at[pl.ds(b0, count), a, :, self.all]

        def term(self, ref, b0, count):
            return ref.at[pl.ds(b0, count), :, self.all]

        def total(self, b, cols):
            return sums.at[at(self.b + b, 4), :, cols]

        def copy(self, m):
            src, dst, to = (
                lambda: (self.block(2, 0, 2), self.term(self.opp_up, 0, 2), self.dn),
                lambda: (self.block(2, 2, 2), self.term(self.opp_dn, 0, 2), self.up),
                lambda: (self.block(-1, 2, 2), self.term(self.from_up, 2, 2), self.dn),
                lambda: (self.block(1, 0, 2), self.term(self.from_dn, 0, 2), self.up),
                lambda: (self.block(-1, 0, 2), self.term(self.from_up, 0, 2), self.dn),
                lambda: (self.block(1, 2, 2), self.term(self.from_dn, 2, 2), self.up),
                lambda: (self.total(2, self.low), opp2_up.at[:, self.low], self.dn2),
                lambda: (self.total(2, self.high), opp2_dn.at[:, self.high], self.up2),
                lambda: (self.total(-1, self.high), from2_up.at[:, self.high], self.dn2),
                lambda: (self.total(1, self.low), from2_dn.at[:, self.low], self.up2),
                lambda: (self.total(-1, self.low), from2_up.at[:, self.low], self.dn2),
                lambda: (self.total(1, self.high), from2_dn.at[:, self.high], self.up2),
            )[m]()
            return self.message(m, src, dst, to)

        def message(self, m, src, dst, to):
            index = self.base + m
            return remote(src, dst, r_send.at[index], r_recv.at[index], to)

        def send_far(self):
            steps = -(-(self.stop - self.start) // 640)
            width = (self.stop - self.start) // steps
            for i in range(steps):
                cols = pl.ds(self.start + i * width, width)
                product = jnp.dot(grad_t[...], bwd[:, cols], preferred_element_type=F32)
                parts[:, :, :, cols] = product.astype(BF16).reshape(NX, NZ, SHARE, width)
            go(self.copy(0))
            go(self.copy(1))

        def send_near(self):
            go(self.copy(2))
            go(self.copy(3))

        def relay(self, side):
            self.copy(side).wait_recv()
            if side == 0:
                add_into(self.block(-1, 0, 2), self.term(self.opp_up, 0, 2))
            else:
                add_into(self.block(1, 2, 2), self.term(self.opp_dn, 0, 2))
            go(self.copy(4 + side))

        def folded(self):
            for m in (2, 3, 4, 5):
                self.copy(m).wait_recv()
            return (
                self.block(0, 0, 4)[...].astype(F32)
                + self.term(self.from_up, 0, 4)[...].astype(F32)
                + self.term(self.from_dn, 0, 4)[...].astype(F32)
            )

        def fold(self):
            self.term(sums, 0, 4)[...] = self.folded().astype(BF16)
            for m in (6, 7, 8, 9):
                go(self.copy(m))

        def relay2(self, side):
            self.copy(6 + side).wait_recv()
            if side == 0:
                add_into(self.total(-1, self.low), opp2_up.at[:, self.low])
            else:
                add_into(self.total(1, self.high), opp2_dn.at[:, self.high])
            go(self.copy(10 + side))

        def finish(self):
            cols = self.all
            for m in (8, 9, 10, 11):
                self.copy(m).wait_recv()
            total = (
                parts[x, z, :, cols].astype(F32)
                + from_up[self.b, :, cols].astype(F32)
                + from_dn[self.b, :, cols].astype(F32)
                + from2_up[:, cols].astype(F32)
                + from2_dn[:, cols].astype(F32)
            )
            o_down[:, cols] = (total * (1.0 / 16)).astype(BF16)

    class ReduceUp(Reduce):
        def send_far(self):
            for cols in (lows, highs):
                product = jnp.zeros((R, cols.size), F32)
                for i in range(NX):
                    product += jnp.dot(
                        act_ts[i], grads[i, :, cols], preferred_element_type=F32
                    )
                u_parts[:, :, :, cols] = product.astype(BF16).reshape(NX, NZ, SHARE, cols.size)
            go(self.copy(0))
            go(self.copy(1))

        def owner(self, m):
            k, to = ((1, right), (-1, left), (2, opposite))[m]
            return self.message(6 + m, ready.at[at(x + k, NX)], o_up.at[:, quarter(0)], to)

        def fold(self):
            ready[...] = (self.folded() * (1.0 / 16)).astype(BF16)
            for m in (2, 0, 1):
                go(self.owner(m))
            o_up[:, quarter(0)] = ready[x]

        def finish(self):
            for m in range(3):
                self.owner(m).wait_recv()

    def input_grad(i):
        cols = piece(i)
        product = jnp.dot(slope_act[...], weight(0, cols), preferred_element_type=F32)
        o_input_grad[:, cols] = (grad[:, cols].astype(F32) + product).astype(BF16)

    down_place = (parts, opp_up, opp_dn, from_up, from_dn)
    up_place = (u_parts, u_opp_up, u_opp_dn, u_from_up, u_from_dn)
    d0, d1 = Reduce(0, down_place, 512, 2048, True), Reduce(1, down_place, 2048, D, True)
    dz = Reduce(2, down_place, 0, 512, False)
    u0 = ReduceUp(3, up_place, 0, PIECE, False)

    both.start1()
    down.start2(0)
    down.start1()
    up.start2(0)
    both.start2(0)
    up.start1()
    loads[3].wait()
    rows_far()
    rows_near()
    choose_rows()
    both.near1(0)
    both.near1(1)
    down.near2(0, 0)
    down.near2(0, 1)
    up.near2(0, 0)
    up.near2(0, 1)
    rows_relay(1)
    both.far1()
    both.near2(0, 0)
    both.near2(0, 1)
    rows_relay(0)
    down.near1(0)
    down.near1(1)
    up.near1(1)
    up.near1(0)
    down.far2(0)
    down.near2(3, 1)
    up.far2(0)
    down.near2(1, 1)
    both.near2(3, 1)
    both.near2(1, 1)
    up.near2(1, 1)
    up.near2(3, 1)
    both.near2(3, 0)
    both.near2(1, 0)
    both.near2(2, 1)
    down.far1()
    down.near2(3, 0)
    down.near2(1, 0)
    up.far1()
    rows_done()
    up.near2(1, 0)
    up.near2(3, 0)
    both.near2(2, 0)
    both.far2(0)
    down.far2(3)
    down.far2(1)
    down.near2(2, 0)
    both.far2(3)
    both.far2(1)
    up.near2(2, 0)
    both.far2(2)
    up.far2(1)
    up.far2(3)
    down.near2(2, 1)
    up.near2(2, 1)
    down.far2(2)
    backward_rows()
    partial(0, fwd, 0)
    up.far2(2)
    partial(1, grad, 1)
    backward_act()
    act_send()
    act[...] = gelu(summed(0)).astype(BF16)
    outputs(0)
    outputs(1)
    outputs(2)
    slopes()
    dz.send_far()
    act_relay()
    dz.send_near()
    d0.send_far()
    d1.send_far()
    d0.send_near()
    d1.send_near()
    outputs(3)
    send_forward(range(last), far)
    send_forward([last], ends)
    act_done()
    u0.send_far()
    dz.relay(1)
    dz.relay(0)
    u0.send_near()
    input_grad(0)
    input_grad(1)
    pass_on()
    input_grad(2)
    d0.relay(0)
    input_grad(3)
    d0.relay(1)
    d1.relay(1)
    d1.relay(0)
    dz.fold()
    u0.relay(0)
    u0.relay(1)
    d0.fold()
    dz.relay2(0)
    dz.relay2(1)
    d1.fold()
    dz.finish()
    d0.relay2(0)
    d0.relay2(1)
    u0.fold()
    d1.relay2(0)
    d1.relay2(1)
    d0.finish()
    u0.finish()
    d1.finish()

    for copy in forward_copies + shift_copies:
        copy.wait_recv()
    for copy in pending + forward_copies[:last]:
        copy.wait_send()
    pl.when(jnp.logical_not(detours))(forward_copies[last].wait_send)
    pl.when(detours)(detour_in.wait_send)
    for i in range(HANDED, PIECES):
        pl.when(core == 0)(shift_copies[i].wait_send)
        pl.when(core == 0)(pass_copies[i].wait_send)
        pl.when(core == 1)(hand_copies[i].wait_send)
    pl.when(stops)(detour_out.wait_send)


def write_out(*refs):
    copies = [
        pltpu.make_async_copy(refs[i], refs[5 + i], refs[10].at[i]) for i in range(5)
    ]
    for copy in copies:
        copy.start()
    for copy in copies:
        copy.wait()


def local(section_in, vision_rows, alternate, grad_in, parked, w_down, w_up):
    rows = jax.ShapeDtypeStruct((ROWS, D), BF16)
    shares = jax.ShapeDtypeStruct((SHARE, D), BF16)
    dma = pltpu.SemaphoreType.DMA
    outs = pl.pallas_call(
        kernel,
        out_shape=(pltpu.VMEM((ROWS, D), BF16),) * 3 + (pltpu.VMEM((SHARE, D), BF16),) * 2,
        in_specs=[pl.BlockSpec(memory_space=pltpu.HBM)] * 7,
        out_specs=[pl.BlockSpec(memory_space=pltpu.VMEM)] * 5,
        scratch_shapes=[
            pltpu.VMEM((ROWS, D), BF16),
            pltpu.VMEM((VISION, D), BF16),
            pltpu.VMEM((1, ROWS), jnp.int32),
            pltpu.VMEM((ROWS, D), BF16),
            pltpu.VMEM((ROWS, D), BF16),
            pltpu.VMEM((ROWS, D), BF16),
            pltpu.VMEM((ROWS, D), BF16),
            pltpu.VMEM((2, NX, NZ, SHARE, D), BF16),
            pltpu.VMEM((NX, NZ, SHARE, D), BF16),
            pltpu.VMEM((3, ROWS, R), BF16),
            pltpu.VMEM((3, ROWS, R), BF16),
            pltpu.VMEM((ROWS, R), F32),
            pltpu.VMEM((ROWS, R), BF16),
            pltpu.VMEM((ROWS, R), BF16),
            pltpu.VMEM((NX, R, ROWS), BF16),
            pltpu.VMEM((R, ROWS), BF16),
            pltpu.VMEM((NX, ROWS, PIECE), BF16),
            pltpu.VMEM((ROWS, CUT), BF16),
            pltpu.VMEM((ROWS, PIECE - CUT), BF16),
            pltpu.VMEM((ROWS, (PIECES - HANDED) * PIECE), BF16),
            pltpu.VMEM((ROWS, PIECE), BF16),
            pltpu.VMEM((2, SHARE, D), BF16),
            pltpu.VMEM((2, SHARE, D), BF16),
            pltpu.VMEM((4, SHARE, D), BF16),
            pltpu.VMEM((4, SHARE, D), BF16),
            pltpu.VMEM((SHARE, D), BF16),
            pltpu.VMEM((SHARE, D), BF16),
            pltpu.VMEM((SHARE, D), BF16),
            pltpu.VMEM((SHARE, D), BF16),
            pltpu.VMEM((4, SHARE, D), BF16),
            pltpu.VMEM((NX, NZ, SHARE, PIECE), BF16),
            pltpu.VMEM((2, SHARE, PIECE), BF16),
            pltpu.VMEM((2, SHARE, PIECE), BF16),
            pltpu.VMEM((4, SHARE, PIECE), BF16),
            pltpu.VMEM((4, SHARE, PIECE), BF16),
            pltpu.VMEM((4, SHARE, PIECE), BF16),
            dma((6,)),
            dma((3 * N_GATHER,)),
            dma((3 * N_GATHER,)),
            dma((4 * N_REDUCE,)),
            dma((4 * N_REDUCE,)),
            dma((3,)),
            dma((3,)),
            dma((4 * PIECES,)),
            dma((4 * PIECES,)),
            dma((9,)),
            dma((9,)),
            pltpu.SemaphoreType.REGULAR,
            pltpu.SemaphoreType.REGULAR,
        ],
        compiler_params=pltpu.CompilerParams(
            collective_id=0, has_side_effects=True, vmem_limit_bytes=40 * 2**20
        ),
        cost_estimate=pl.CostEstimate(
            flops=14 * ROWS * D * R, bytes_accessed=12 * ROWS * D, transcendentals=3 * ROWS * R
        ),
        name="relay_tick",
    )(*(
        pltpu.with_memory_space_constraint(operand, pltpu.HBM)
        for operand in (
            section_in[0, 0], vision_rows[0], alternate, grad_in[0, 0], parked[0, 0],
            w_down[0], w_up[0],
        )
    ))
    received, stash, input_grad, up_grad, down_grad = pl.pallas_call(
        write_out,
        out_shape=(rows, rows, rows, shares, shares),
        in_specs=[pl.BlockSpec(memory_space=pltpu.VMEM)] * 5,
        out_specs=[pl.BlockSpec(memory_space=pltpu.HBM)] * 5,
        scratch_shapes=[dma((5,))],
        name="write_out",
    )(*(pltpu.with_memory_space_constraint(out, pltpu.VMEM) for out in outs))
    return (
        received[None, None],
        stash[None, None],
        input_grad[None, None],
        up_grad[None],
        down_grad[None],
    )


def solution(mesh):
    rows = P("section", "dp", None, "mp")
    shares = P("section", "dp", "mp")
    return jax.shard_map(
        local,
        mesh=mesh,
        in_specs=(rows, P("dp", None, "mp"), P("dp", None), rows, rows, shares, shares),
        out_specs=(rows, rows, rows, shares, shares),
        check_vma=False,
    )
```

```python
import functools
import math

import jax
import jax.numpy as jnp
from jax import lax
from jax.experimental import pallas as pl
from jax.experimental.pallas import tpu as pltpu
from jax.sharding import PartitionSpec as P

MESH = pl.DeviceIdType.MESH
BF16, F32 = jnp.bfloat16, jnp.float32

D = 3584
R = 256
ROWS = 104
VISION = 24
SHARE = 16
PIECES = 4
PIECE = D // PIECES
CUT = 512
HANDED = 2
HAND = 3 * PIECES
NX, NZ = 4, 4
SPLIT = 1024

N_GATHER = 16
N_REDUCE = 12

NT = (((1,), (1,)), ((), ()))
TN = (((0,), (0,)), ((), ()))

SCALE = math.sqrt(2 / math.pi)


def gelu(v):
    return 0.5 * v * (1.0 + jnp.tanh(SCALE * (v + 0.044715 * (v * v * v))))


def gelu_slope(v):
    t = jnp.tanh(SCALE * (v + 0.044715 * (v * v * v)))
    return 0.5 * (1.0 + t) + 0.5 * v * (1.0 - t * t) * (SCALE * (1.0 + 3 * 0.044715 * (v * v)))


def kernel(
    section_ref, vision_ref, alternate_ref, grad_ref, parked_ref, wd_ref, wu_ref,
    o_section, o_parked, o_input_grad, o_up, o_down,
    sec, vis, alt, grad, fwd, bwd, out, weights, parts,
    pre_out, pre_in, bwd_pre, act, slope_act, act_ts, grad_t, grads, by_right, by_left,
    hand, stop, opp_up, opp_dn, from_up, from_dn, opp2_up, opp2_dn, from2_up, from2_dn, sums,
    u_parts, u_opp_up, u_opp_dn, u_from_up, u_from_dn, ready,
    local_sem, g_send, g_recv, r_send, r_recv, m_send, m_recv, y_send, y_recv, x_send, x_recv, y_go, xz_go,
):
    section = lax.axis_index("section")
    dp = lax.axis_index("dp")
    mp = lax.axis_index("mp")
    x, z = lax.div(dp, NZ), lax.rem(dp, NZ)

    def at(value, count):
        return lax.rem(value + count, count)

    def chunk(xi, zi):
        return at(xi, NX) * NZ + at(zi, NZ)

    mirror = {"section": 15 - section}
    following = {"section": lax.rem(section + 1, 16)}
    preceding = {"section": lax.rem(section + 15, 16)}
    other = {"mp": 1 - mp}
    right, left = {"dp": chunk(x + 1, z)}, {"dp": chunk(x - 1, z)}
    opposite = {"dp": chunk(x + 2, z)}
    plus, minus = {"dp": chunk(x, z + 1)}, {"dp": chunk(x, z - 1)}

    pending = []

    def remote(src, dst, send, recv, to):
        copy = pltpu.make_async_remote_copy(
            src_ref=src, dst_ref=dst, send_sem=send, recv_sem=recv,
            device_id=to, device_id_type=MESH,
        )
        return copy

    def go(copy):
        copy.start()
        pending.append(copy)

    w_refs = (wd_ref, wu_ref)
    loads = [
        pltpu.make_async_copy(section_ref, sec, local_sem.at[0]),
        pltpu.make_async_copy(vision_ref, vis, local_sem.at[1]),
        pltpu.make_async_copy(alternate_ref, alt, local_sem.at[2]),
        pltpu.make_async_copy(grad_ref, grad, local_sem.at[3]),
        pltpu.make_async_copy(wd_ref, weights.at[0, x, z], local_sem.at[4]),
        pltpu.make_async_copy(wu_ref, weights.at[1, x, z], local_sem.at[5]),
    ]
    y, core = lax.div(section, 2), lax.rem(section, 2)
    turn = lax.rem(y, 4)
    near = jnp.logical_or(turn == 0, turn == 3)
    far = jnp.logical_not(near)
    detours, stops, ends = turn == 2, turn == 0, turn == 1
    next_chip = {"section": lax.rem(section + 2, 16)}
    stop_at = {"section": lax.rem(section + 12, 16)}
    stop_to = {"section": lax.rem(y + 5, 8) * 2 + 1 - core}

    barrier = pltpu.get_barrier_semaphore()

    def greet(*partners):
        for partner in partners:
            pl.semaphore_signal(barrier, inc=1, device_id=partner, device_id_type=MESH)

    def chip_y(value):
        return {"section": 2 * lax.rem(value + 8, 8)}

    mate = {"section": section + 1 - 2 * core}
    greet(mate, chip_y(7 - y), chip_y(y + 1), chip_y(y - 1))
    pl.when(detours)(lambda: greet(chip_y(y - 2)))
    pl.when(stops)(lambda: greet(chip_y(y + 2), chip_y(y + 5)))
    pl.when(ends)(lambda: greet(chip_y(y + 3)))
    greet(*({**to, "section": 2 * y + 1} for to in (right, left, opposite, plus, minus, other)))
    for load in loads:
        load.start()
    extra = jnp.where(stops, 2, jnp.where(turn == 3, 0, 1))

    @pl.when(core == 0)
    def _():
        pl.semaphore_wait(barrier, 7 + 2 * extra)
        pl.semaphore_signal(y_go, inc=1, device_id=mate, device_id_type=MESH)

    @pl.when(core == 1)
    def _():
        pl.semaphore_wait(y_go, 1)

    def piece(i):
        return pl.ds(i * PIECE, PIECE)

    def y_piece(src, dst, index, i, to):
        return remote(
            src.at[:, piece(i)], dst.at[:, piece(i)], y_send.at[index], y_recv.at[index], to
        )

    parked_copies = [y_piece(parked_ref, bwd, i, i, mirror) for i in range(PIECES)]
    forward_copies = [y_piece(fwd, o_parked, PIECES + i, i, mirror) for i in range(PIECES)]
    shift_copies = [y_piece(out, o_section, 2 * PIECES + i, i, following) for i in range(PIECES)]
    for copy in parked_copies:
        go(copy)

    @pl.when(core == 1)
    def _():
        pl.semaphore_wait(barrier, 13)
        pl.semaphore_signal(xz_go, inc=1, device_id=mate, device_id_type=MESH)

    @pl.when(core == 0)
    def _():
        pl.semaphore_wait(xz_go, 1)

    def send_forward(pieces, when):
        @pl.when(when)
        def _():
            for i in pieces:
                forward_copies[i].start()

    hand_copies, pass_copies = {}, {}
    for i in range(HANDED, PIECES):
        held = hand.at[:, pl.ds((i - HANDED) * PIECE, PIECE)]
        hand_copies[i] = remote(
            out.at[:, piece(i)], held, y_send.at[HAND + i], y_recv.at[HAND + i], preceding
        )
        pass_copies[i] = remote(
            held, o_section.at[:, piece(i)],
            y_send.at[HAND + i], y_recv.at[2 * PIECES + i], next_chip,
        )

    last = PIECES - 1
    detour_in = remote(
        fwd.at[:, piece(last)], stop, y_send.at[3 * PIECES], y_recv.at[3 * PIECES], stop_at
    )
    detour_out = remote(
        stop, o_parked.at[:, piece(last)],
        y_send.at[3 * PIECES + 1], y_recv.at[PIECES + last], stop_to,
    )

    class Gather:
        def __init__(self, number, w, start, stop, x_first):
            self.base, self.w, self.start, self.stop = number * N_GATHER, w, start, stop
            self.x_first = x_first
            self.a, self.b = (x, z) if x_first else (z, x)
            xs, zs = (right, left), (plus, minus)
            (self.up, self.dn), (self.up2, self.dn2) = (xs, zs) if x_first else (zs, xs)
            middle = (start + stop) // 2
            self.all = pl.ds(start, stop - start)
            self.low, self.high = pl.ds(start, middle - start), pl.ds(middle, stop - middle)

        def copy(self, m, to, a=0, b=0, cols=None):
            cols = self.all if cols is None else cols
            a, b = at(self.a + a, 4), at(self.b + b, 4)
            xi, zi = (a, b) if self.x_first else (b, a)
            place = weights.at[self.w, xi, zi, :, cols]
            index = self.base + m
            return remote(place, place, g_send.at[index], g_recv.at[index], to)

        def start1(self):
            go(self.copy(0, self.up))
            go(self.copy(1, self.dn))

        def start2(self, k):
            go(self.copy(4 + k, self.up2, a=k))
            go(self.copy(8 + k, self.dn2, a=k))

        def near1(self, side):
            self.copy(side, (self.up, self.dn)[side]).wait_recv()
            if side == 0:
                go(self.copy(2, self.up, a=-1, cols=self.low))
                self.start2(3)
            else:
                go(self.copy(3, self.dn, a=1, cols=self.high))
                self.start2(1)

        def far1(self):
            self.copy(2, self.up, cols=self.low).wait_recv()
            self.copy(3, self.dn, cols=self.high).wait_recv()
            self.start2(2)

        def near2(self, k, side):
            self.copy(4 + 4 * side + k, (self.up2, self.dn2)[side]).wait_recv()
            if k % 2 == 0 and side == 0:
                go(self.copy(12 + k // 2, self.up2, a=k, b=-1))
            if k % 2 == 1 and side == 1:
                go(self.copy(14 + k // 2, self.dn2, a=k, b=1))

        def far2(self, k):
            if k % 2 == 0:
                self.copy(12 + k // 2, self.up2).wait_recv()
            else:
                self.copy(14 + k // 2, self.dn2).wait_recv()

    down = Gather(0, 0, SPLIT, D, False)
    up = Gather(1, 1, SPLIT, D, False)
    both = Gather(2, slice(None), 0, SPLIT, True)

    def exchange(slot):
        return remote(
            pre_out.at[slot], pre_in.at[slot], m_send.at[slot], m_recv.at[slot], other
        )

    def weight(w, cols):
        block = weights[w, :, :, :, cols]
        return block.reshape(R, block.shape[-1])

    def partial(slot, rows, w):
        total = jnp.zeros((ROWS, R), F32)
        for i in range(PIECES):
            total += lax.dot_general(
                rows[:, piece(i)], weight(w, piece(i)), NT, preferred_element_type=F32
            )
        send_partial(slot, total)

    def send_partial(slot, total):
        pre_out[slot] = total.astype(BF16)
        go(exchange(slot))

    def summed(slot):
        exchange(slot).wait_recv()
        return pre_out[slot].astype(F32) + pre_in[slot].astype(F32)

    for load in loads[4:]:
        load.wait()
    def choose_rows():
        for load in loads[:3]:
            load.wait()
        picks = jnp.where(section == 0, alt[...], -1)
        chosen_t = (lax.broadcasted_iota(jnp.int32, (VISION, ROWS), 0) == picks).astype(BF16)
        hit = lax.dot_general(
            chosen_t, jnp.ones((VISION, PIECE), BF16), TN, preferred_element_type=F32
        )

        for i in range(PIECES):
            cols = piece(i)
            chosen = lax.dot_general(chosen_t, vis[:, cols], TN, preferred_element_type=F32)
            fwd[:, cols] = jnp.where(hit > 0.5, chosen, sec[:, cols].astype(F32)).astype(BF16)
        pl.when(detours)(detour_in.start)
        send_forward(range(PIECES), near)

    def quarter(k, first=0, size=PIECE):
        return pl.ds(pl.multiple_of(at(x + k, NX) * PIECE + first, 128), size)

    def x_copy(m, src, dst, to):
        return remote(src, dst, x_send.at[m], x_recv.at[m], to)

    lows, highs = pl.ds(0, CUT), pl.ds(CUT, PIECE - CUT)
    from_x = [at(x + k, NX) for k in range(-1, 2)]
    row_copies = [
        x_copy(0, grad.at[:, quarter(1)], grads.at[x], right),
        x_copy(1, grad.at[:, quarter(-1)], grads.at[x], left),
        x_copy(2, grad.at[:, quarter(2, 0, CUT)], by_right, right),
        x_copy(3, grad.at[:, quarter(2, CUT, PIECE - CUT)], by_left, left),
        x_copy(4, by_right, grads.at[from_x[0], :, lows], right),
        x_copy(5, by_left, grads.at[from_x[2], :, highs], left),
    ]
    act_copies = [
        x_copy(6, act_ts.at[x], act_ts.at[x], right),
        x_copy(7, act_ts.at[x], act_ts.at[x], left),
        x_copy(8, act_ts.at[from_x[0]], act_ts.at[from_x[0]], right),
    ]

    def rows_far():
        go(row_copies[2])
        go(row_copies[3])

    def rows_near():
        go(row_copies[0])
        go(row_copies[1])
        grads[x] = grad[:, quarter(0)]

    def rows_relay(side):
        row_copies[2 + side].wait_recv()
        go(row_copies[4 + side])

    def rows_done():
        for m in (0, 1, 4, 5):
            row_copies[m].wait_recv()

    def act_send():
        go(act_copies[0])
        go(act_copies[1])

    def act_relay():
        act_copies[0].wait_recv()
        go(act_copies[2])

    def act_done():
        act_copies[1].wait_recv()
        act_copies[2].wait_recv()

    def backward_rows():
        total = jnp.zeros((ROWS, R), F32)
        for i in range(PIECES):
            parked_copies[i].wait_recv()
            cols = piece(i)
            total += lax.dot_general(
                bwd[:, cols], weight(0, cols), NT, preferred_element_type=F32
            )
        send_partial(2, total)

        @pl.when(stops)
        def _():
            detour_in.wait_recv()
            detour_out.start()

    def backward_act():
        bwd_pre[...] = summed(2)
        act_ts[x] = gelu(bwd_pre[...]).astype(BF16).T

    def slopes():
        pre_grad = (summed(1) * gelu_slope(bwd_pre[...])).astype(BF16)
        slope_act[...] = pre_grad
        grad_t[...] = pre_grad.T

    def outputs(i):
        cols = piece(i)
        product = jnp.dot(act[...], weight(1, cols), preferred_element_type=F32)
        out[:, cols] = (fwd[:, cols].astype(F32) + product).astype(BF16)
        if i < HANDED:
            go(shift_copies[i])
        else:
            pl.when(core == 0)(shift_copies[i].start)
            pl.when(core == 1)(hand_copies[i].start)

    def pass_on():
        @pl.when(core == 0)
        def _():
            for i in range(HANDED, PIECES):
                hand_copies[i].wait_recv()
                pass_copies[i].start()

    def add_into(total, term):
        total[...] = (total[...].astype(F32) + term[...].astype(F32)).astype(BF16)

    class Reduce:
        def __init__(self, number, place, start, stop, x_first):
            self.base, self.start, self.stop = number * N_REDUCE, start, stop
            self.parts, self.opp_up, self.opp_dn, self.from_up, self.from_dn = place
            self.x_first = x_first
            self.a, self.b = (x, z) if x_first else (z, x)
            xs, zs = (right, left), (plus, minus)
            (self.up, self.dn), (self.up2, self.dn2) = (xs, zs) if x_first else (zs, xs)
            middle = start + (stop - start + 128) // 256 * 128
            self.all = pl.ds(start, stop - start)
            self.low, self.high = pl.ds(start, middle - start), pl.ds(middle, stop - middle)

        def block(self, a, b0, count):
            a = at(self.a + a, 4)
            if self.x_first:
                return self.parts.at[a, pl.ds(b0, count), :, self.all]
            return self.parts.at[pl.ds(b0, count), a, :, self.all]

        def term(self, ref, b0, count):
            return ref.at[pl.ds(b0, count), :, self.all]

        def total(self, b, cols):
            return sums.at[at(self.b + b, 4), :, cols]

        def copy(self, m):
            src, dst, to = (
                lambda: (self.block(2, 0, 2), self.term(self.opp_up, 0, 2), self.dn),
                lambda: (self.block(2, 2, 2), self.term(self.opp_dn, 0, 2), self.up),
                lambda: (self.block(-1, 2, 2), self.term(self.from_up, 2, 2), self.dn),
                lambda: (self.block(1, 0, 2), self.term(self.from_dn, 0, 2), self.up),
                lambda: (self.block(-1, 0, 2), self.term(self.from_up, 0, 2), self.dn),
                lambda: (self.block(1, 2, 2), self.term(self.from_dn, 2, 2), self.up),
                lambda: (self.total(2, self.low), opp2_up.at[:, self.low], self.dn2),
                lambda: (self.total(2, self.high), opp2_dn.at[:, self.high], self.up2),
                lambda: (self.total(-1, self.high), from2_up.at[:, self.high], self.dn2),
                lambda: (self.total(1, self.low), from2_dn.at[:, self.low], self.up2),
                lambda: (self.total(-1, self.low), from2_up.at[:, self.low], self.dn2),
                lambda: (self.total(1, self.high), from2_dn.at[:, self.high], self.up2),
            )[m]()
            return self.message(m, src, dst, to)

        def message(self, m, src, dst, to):
            index = self.base + m
            return remote(src, dst, r_send.at[index], r_recv.at[index], to)

        def send_far(self):
            for first in range(self.start, self.stop, 640):
                width = min(640, self.stop - first)
                cols = pl.ds(first, width)
                product = jnp.dot(grad_t[...], bwd[:, cols], preferred_element_type=F32)
                parts[:, :, :, cols] = product.astype(BF16).reshape(NX, NZ, SHARE, width)
            go(self.copy(0))
            go(self.copy(1))

        def send_near(self):
            go(self.copy(2))
            go(self.copy(3))

        def relay(self, side):
            self.copy(side).wait_recv()
            if side == 0:
                add_into(self.block(-1, 0, 2), self.term(self.opp_up, 0, 2))
            else:
                add_into(self.block(1, 2, 2), self.term(self.opp_dn, 0, 2))
            go(self.copy(4 + side))

        def folded(self):
            for m in (2, 3, 4, 5):
                self.copy(m).wait_recv()
            return (
                self.block(0, 0, 4)[...].astype(F32)
                + self.term(self.from_up, 0, 4)[...].astype(F32)
                + self.term(self.from_dn, 0, 4)[...].astype(F32)
            )

        def fold(self):
            self.term(sums, 0, 4)[...] = self.folded().astype(BF16)
            for m in (6, 7, 8, 9):
                go(self.copy(m))

        def relay2(self, side):
            self.copy(6 + side).wait_recv()
            if side == 0:
                add_into(self.total(-1, self.low), opp2_up.at[:, self.low])
            else:
                add_into(self.total(1, self.high), opp2_dn.at[:, self.high])
            go(self.copy(10 + side))

        def finish(self):
            cols = self.all
            for m in (8, 9, 10, 11):
                self.copy(m).wait_recv()
            total = (
                parts[x, z, :, cols].astype(F32)
                + from_up[self.b, :, cols].astype(F32)
                + from_dn[self.b, :, cols].astype(F32)
                + from2_up[:, cols].astype(F32)
                + from2_dn[:, cols].astype(F32)
            )
            o_down[:, cols] = (total * (1.0 / 16)).astype(BF16)

    class ReduceUp(Reduce):
        def send_far(self):
            cols = self.all
            product = jnp.zeros((R, cols.size), F32)
            for i in range(NX):
                product += jnp.dot(act_ts[i], grads[i, :, cols], preferred_element_type=F32)
            u_parts[:, :, :, cols] = product.astype(BF16).reshape(NX, NZ, SHARE, cols.size)
            go(self.copy(0))
            go(self.copy(1))

        def owner(self, m):
            k, to = ((1, right), (-1, left), (2, opposite))[m]
            place = o_up.at[:, quarter(0, self.start, self.stop - self.start)]
            return self.message(6 + m, ready.at[at(x + k, NX), :, self.all], place, to)

        def fold(self):
            ready[:, :, self.all] = (self.folded() * (1.0 / 16)).astype(BF16)
            for m in (2, 0, 1):
                go(self.owner(m))
            o_up[:, quarter(0, self.start, self.stop - self.start)] = ready[x, :, self.all]

        def finish(self):
            for m in range(3):
                self.owner(m).wait_recv()

    def input_grad(i):
        cols = piece(i)
        product = jnp.dot(slope_act[...], weight(0, cols), preferred_element_type=F32)
        o_input_grad[:, cols] = (grad[:, cols].astype(F32) + product).astype(BF16)

    down_place = (parts, opp_up, opp_dn, from_up, from_dn)
    up_place = (u_parts, u_opp_up, u_opp_dn, u_from_up, u_from_dn)
    dz = Reduce(0, down_place, 0, 640, False)
    d0 = Reduce(1, down_place, 640, 1664, True)
    d1 = Reduce(2, down_place, 1664, 2688, True)
    d2 = Reduce(3, down_place, 2688, 3584, True)
    u0 = ReduceUp(4, up_place, 0, 512, False)
    u1 = ReduceUp(5, up_place, 512, 896, False)

    down.start1()
    down.start2(0)
    both.start1()
    up.start2(0)
    both.start2(0)
    up.start1()
    loads[3].wait()
    rows_far()
    rows_near()
    choose_rows()
    down.near2(0, 1)
    down.near2(0, 0)
    both.near1(0)
    down.near1(0)
    down.near1(1)
    both.near1(1)
    up.near2(0, 0)
    up.near2(0, 1)
    both.near2(0, 0)
    both.near2(0, 1)
    rows_relay(1)
    rows_relay(0)
    up.near1(0)
    up.near1(1)
    down.near2(3, 1)
    both.near2(3, 0)
    both.near2(3, 1)
    down.far2(0)
    down.near2(1, 1)
    down.far1()
    both.far1()
    down.near2(3, 0)
    both.near2(1, 0)
    both.near2(1, 1)
    down.near2(1, 0)
    up.near2(3, 1)
    up.far2(0)
    both.far2(0)
    up.near2(1, 1)
    rows_done()
    up.far1()
    both.far2(3)
    down.far2(3)
    up.near2(3, 0)
    down.far2(1)
    both.near2(2, 0)
    both.near2(2, 1)
    up.near2(1, 0)
    down.near2(2, 1)
    down.near2(2, 0)
    up.far2(3)
    both.far2(1)
    up.near2(2, 0)
    both.far2(2)
    up.far2(1)
    down.far2(2)
    partial(0, fwd, 0)
    up.near2(2, 1)
    up.far2(2)
    backward_rows()
    partial(1, grad, 1)
    act[...] = gelu(summed(0)).astype(BF16)
    outputs(0)
    outputs(1)
    backward_act()
    act_send()
    outputs(2)
    slopes()
    d1.send_far()
    dz.send_far()
    act_relay()
    d0.send_far()
    dz.send_near()
    d1.send_near()
    d0.send_near()
    d2.send_far()
    d1.relay(1)
    d1.relay(0)
    d2.send_near()
    outputs(3)
    send_forward(range(last), far)
    send_forward([last], ends)
    dz.relay(0)
    dz.relay(1)
    d0.relay(0)
    act_done()
    u0.send_far()
    d0.relay(1)
    u1.send_far()
    u0.send_near()
    dz.fold()
    d2.relay(0)
    u1.send_near()
    input_grad(0)
    u0.relay(0)
    u0.relay(1)
    d2.relay(1)
    input_grad(1)
    u1.relay(0)
    u1.relay(1)
    input_grad(2)
    pass_on()
    d1.fold()
    input_grad(3)
    dz.relay2(0)
    d0.fold()
    dz.relay2(1)
    u0.fold()
    u1.fold()
    d2.fold()
    d1.relay2(1)
    d1.relay2(0)
    dz.finish()
    d0.relay2(0)
    d0.relay2(1)
    u0.finish()
    u1.finish()
    d2.relay2(0)
    d2.relay2(1)
    d1.finish()
    d0.finish()
    d2.finish()

    for copy in forward_copies + shift_copies:
        copy.wait_recv()
    for copy in pending + forward_copies[:last]:
        copy.wait_send()
    pl.when(jnp.logical_not(detours))(forward_copies[last].wait_send)
    pl.when(detours)(detour_in.wait_send)
    for i in range(HANDED, PIECES):
        pl.when(core == 0)(shift_copies[i].wait_send)
        pl.when(core == 0)(pass_copies[i].wait_send)
        pl.when(core == 1)(hand_copies[i].wait_send)
    pl.when(stops)(detour_out.wait_send)


def write_out(*refs):
    copies = [
        pltpu.make_async_copy(refs[i], refs[5 + i], refs[10].at[i]) for i in range(5)
    ]
    for copy in copies:
        copy.start()
    for copy in copies:
        copy.wait()


def local(section_in, vision_rows, alternate, grad_in, parked, w_down, w_up):
    rows = jax.ShapeDtypeStruct((ROWS, D), BF16)
    shares = jax.ShapeDtypeStruct((SHARE, D), BF16)
    dma = pltpu.SemaphoreType.DMA
    outs = pl.pallas_call(
        kernel,
        out_shape=(pltpu.VMEM((ROWS, D), BF16),) * 3 + (pltpu.VMEM((SHARE, D), BF16),) * 2,
        in_specs=[pl.BlockSpec(memory_space=pltpu.HBM)] * 7,
        out_specs=[pl.BlockSpec(memory_space=pltpu.VMEM)] * 5,
        scratch_shapes=[
            pltpu.VMEM((ROWS, D), BF16),
            pltpu.VMEM((VISION, D), BF16),
            pltpu.VMEM((1, ROWS), jnp.int32),
            pltpu.VMEM((ROWS, D), BF16),
            pltpu.VMEM((ROWS, D), BF16),
            pltpu.VMEM((ROWS, D), BF16),
            pltpu.VMEM((ROWS, D), BF16),
            pltpu.VMEM((2, NX, NZ, SHARE, D), BF16),
            pltpu.VMEM((NX, NZ, SHARE, D), BF16),
            pltpu.VMEM((3, ROWS, R), BF16),
            pltpu.VMEM((3, ROWS, R), BF16),
            pltpu.VMEM((ROWS, R), F32),
            pltpu.VMEM((ROWS, R), BF16),
            pltpu.VMEM((ROWS, R), BF16),
            pltpu.VMEM((NX, R, ROWS), BF16),
            pltpu.VMEM((R, ROWS), BF16),
            pltpu.VMEM((NX, ROWS, PIECE), BF16),
            pltpu.VMEM((ROWS, CUT), BF16),
            pltpu.VMEM((ROWS, PIECE - CUT), BF16),
            pltpu.VMEM((ROWS, (PIECES - HANDED) * PIECE), BF16),
            pltpu.VMEM((ROWS, PIECE), BF16),
            pltpu.VMEM((2, SHARE, D), BF16),
            pltpu.VMEM((2, SHARE, D), BF16),
            pltpu.VMEM((4, SHARE, D), BF16),
            pltpu.VMEM((4, SHARE, D), BF16),
            pltpu.VMEM((SHARE, D), BF16),
            pltpu.VMEM((SHARE, D), BF16),
            pltpu.VMEM((SHARE, D), BF16),
            pltpu.VMEM((SHARE, D), BF16),
            pltpu.VMEM((4, SHARE, D), BF16),
            pltpu.VMEM((NX, NZ, SHARE, PIECE), BF16),
            pltpu.VMEM((2, SHARE, PIECE), BF16),
            pltpu.VMEM((2, SHARE, PIECE), BF16),
            pltpu.VMEM((4, SHARE, PIECE), BF16),
            pltpu.VMEM((4, SHARE, PIECE), BF16),
            pltpu.VMEM((4, SHARE, PIECE), BF16),
            dma((6,)),
            dma((3 * N_GATHER,)),
            dma((3 * N_GATHER,)),
            dma((6 * N_REDUCE,)),
            dma((6 * N_REDUCE,)),
            dma((3,)),
            dma((3,)),
            dma((4 * PIECES,)),
            dma((4 * PIECES,)),
            dma((9,)),
            dma((9,)),
            pltpu.SemaphoreType.REGULAR,
            pltpu.SemaphoreType.REGULAR,
        ],
        compiler_params=pltpu.CompilerParams(
            collective_id=0, has_side_effects=True, vmem_limit_bytes=40 * 2**20
        ),
        cost_estimate=pl.CostEstimate(
            flops=14 * ROWS * D * R, bytes_accessed=12 * ROWS * D, transcendentals=3 * ROWS * R
        ),
        name="relay_tick",
    )(*(
        pltpu.with_memory_space_constraint(operand, pltpu.HBM)
        for operand in (
            section_in[0, 0], vision_rows[0], alternate, grad_in[0, 0], parked[0, 0],
            w_down[0], w_up[0],
        )
    ))
    received, stash, input_grad, up_grad, down_grad = pl.pallas_call(
        write_out,
        out_shape=(rows, rows, rows, shares, shares),
        in_specs=[pl.BlockSpec(memory_space=pltpu.VMEM)] * 5,
        out_specs=[pl.BlockSpec(memory_space=pltpu.HBM)] * 5,
        scratch_shapes=[dma((5,))],
        name="write_out",
    )(*(pltpu.with_memory_space_constraint(out, pltpu.VMEM) for out in outs))
    return (
        received[None, None],
        stash[None, None],
        input_grad[None, None],
        up_grad[None],
        down_grad[None],
    )


def solution(mesh):
    rows = P("section", "dp", None, "mp")
    shares = P("section", "dp", "mp")
    return jax.shard_map(
        local,
        mesh=mesh,
        in_specs=(rows, P("dp", None, "mp"), P("dp", None), rows, rows, shares, shares),
        out_specs=(rows, rows, rows, shares, shares),
        check_vma=False,
    )
```

```python
import functools
import math

import jax
import jax.numpy as jnp
from jax import lax
from jax.experimental import pallas as pl
from jax.experimental.pallas import tpu as pltpu
from jax.sharding import PartitionSpec as P

MESH = pl.DeviceIdType.MESH
BF16, F32 = jnp.bfloat16, jnp.float32

D = 3584
R = 256
ROWS = 104
VISION = 24
SHARE = 16
PIECES = 4
PIECE = D // PIECES
CUT = 512
HANDED = 2
HAND = 3 * PIECES
NX, NZ = 4, 4
SPLIT = 768

N_GATHER = 16
N_REDUCE = 12

NT = (((1,), (1,)), ((), ()))
TN = (((0,), (0,)), ((), ()))

SCALE = math.sqrt(2 / math.pi)


def gelu(v):
    return 0.5 * v * (1.0 + jnp.tanh(SCALE * (v + 0.044715 * (v * v * v))))


def gelu_slope(v):
    t = jnp.tanh(SCALE * (v + 0.044715 * (v * v * v)))
    return 0.5 * (1.0 + t) + 0.5 * v * (1.0 - t * t) * (SCALE * (1.0 + 3 * 0.044715 * (v * v)))


def kernel(
    section_ref, vision_ref, alternate_ref, grad_ref, parked_ref, wd_ref, wu_ref,
    o_section, o_parked, o_input_grad, o_up, o_down,
    sec, vis, alt, grad, fwd, bwd, out, weights, parts,
    pre_out, pre_in, bwd_pre, act, slope_act, act_ts, grad_t, grads, by_right, by_left,
    hand, stop, opp_up, opp_dn, from_up, from_dn, opp2_up, opp2_dn, from2_up, from2_dn, sums,
    u_parts, u_opp_up, u_opp_dn, u_from_up, u_from_dn, ready,
    local_sem, g_send, g_recv, r_send, r_recv, m_send, m_recv, y_send, y_recv, x_send, x_recv, y_go, xz_go,
):
    section = lax.axis_index("section")
    dp = lax.axis_index("dp")
    mp = lax.axis_index("mp")
    x, z = lax.div(dp, NZ), lax.rem(dp, NZ)

    def at(value, count):
        return lax.rem(value + count, count)

    def chunk(xi, zi):
        return at(xi, NX) * NZ + at(zi, NZ)

    mirror = {"section": 15 - section}
    following = {"section": lax.rem(section + 1, 16)}
    preceding = {"section": lax.rem(section + 15, 16)}
    other = {"mp": 1 - mp}
    right, left = {"dp": chunk(x + 1, z)}, {"dp": chunk(x - 1, z)}
    opposite = {"dp": chunk(x + 2, z)}
    plus, minus = {"dp": chunk(x, z + 1)}, {"dp": chunk(x, z - 1)}

    pending = []

    def remote(src, dst, send, recv, to):
        copy = pltpu.make_async_remote_copy(
            src_ref=src, dst_ref=dst, send_sem=send, recv_sem=recv,
            device_id=to, device_id_type=MESH,
        )
        return copy

    def go(copy):
        copy.start()
        pending.append(copy)

    w_refs = (wd_ref, wu_ref)
    loads = [
        pltpu.make_async_copy(section_ref, sec, local_sem.at[0]),
        pltpu.make_async_copy(vision_ref, vis, local_sem.at[1]),
        pltpu.make_async_copy(alternate_ref, alt, local_sem.at[2]),
        pltpu.make_async_copy(grad_ref, grad, local_sem.at[3]),
        pltpu.make_async_copy(wd_ref, weights.at[0, x, z], local_sem.at[4]),
        pltpu.make_async_copy(wu_ref, weights.at[1, x, z], local_sem.at[5]),
    ]
    y, core = lax.div(section, 2), lax.rem(section, 2)
    turn = lax.rem(y, 4)
    near = jnp.logical_or(turn == 0, turn == 3)
    far = jnp.logical_not(near)
    detours, stops, ends = turn == 2, turn == 0, turn == 1
    next_chip = {"section": lax.rem(section + 2, 16)}
    stop_at = {"section": lax.rem(section + 12, 16)}
    stop_to = {"section": lax.rem(y + 5, 8) * 2 + 1 - core}

    barrier = pltpu.get_barrier_semaphore()

    def greet(*partners):
        for partner in partners:
            pl.semaphore_signal(barrier, inc=1, device_id=partner, device_id_type=MESH)

    def chip_y(value):
        return {"section": 2 * lax.rem(value + 8, 8)}

    mate = {"section": section + 1 - 2 * core}
    greet(mate, chip_y(7 - y), chip_y(y + 1), chip_y(y - 1))
    pl.when(detours)(lambda: greet(chip_y(y - 2)))
    pl.when(stops)(lambda: greet(chip_y(y + 2), chip_y(y + 5)))
    pl.when(ends)(lambda: greet(chip_y(y + 3)))
    greet(*({**to, "section": 2 * y + 1} for to in (right, left, opposite, plus, minus, other)))
    for load in loads:
        load.start()
    extra = jnp.where(stops, 2, jnp.where(turn == 3, 0, 1))

    @pl.when(core == 0)
    def _():
        pl.semaphore_wait(barrier, 7 + 2 * extra)
        pl.semaphore_signal(y_go, inc=1, device_id=mate, device_id_type=MESH)

    @pl.when(core == 1)
    def _():
        pl.semaphore_wait(y_go, 1)

    def piece(i):
        return pl.ds(i * PIECE, PIECE)

    def y_piece(src, dst, index, i, to):
        return remote(
            src.at[:, piece(i)], dst.at[:, piece(i)], y_send.at[index], y_recv.at[index], to
        )

    parked_copies = [y_piece(parked_ref, bwd, i, i, mirror) for i in range(PIECES)]
    forward_copies = [y_piece(fwd, o_parked, PIECES + i, i, mirror) for i in range(PIECES)]
    shift_copies = [y_piece(out, o_section, 2 * PIECES + i, i, following) for i in range(PIECES)]
    for copy in parked_copies:
        go(copy)

    @pl.when(core == 1)
    def _():
        pl.semaphore_wait(barrier, 13)
        pl.semaphore_signal(xz_go, inc=1, device_id=mate, device_id_type=MESH)

    @pl.when(core == 0)
    def _():
        pl.semaphore_wait(xz_go, 1)

    def send_forward(pieces, when):
        @pl.when(when)
        def _():
            for i in pieces:
                forward_copies[i].start()

    hand_copies, pass_copies = {}, {}
    for i in range(HANDED, PIECES):
        held = hand.at[:, pl.ds((i - HANDED) * PIECE, PIECE)]
        hand_copies[i] = remote(
            out.at[:, piece(i)], held, y_send.at[HAND + i], y_recv.at[HAND + i], preceding
        )
        pass_copies[i] = remote(
            held, o_section.at[:, piece(i)],
            y_send.at[HAND + i], y_recv.at[2 * PIECES + i], next_chip,
        )

    last = PIECES - 1
    detour_in = remote(
        fwd.at[:, piece(last)], stop, y_send.at[3 * PIECES], y_recv.at[3 * PIECES], stop_at
    )
    detour_out = remote(
        stop, o_parked.at[:, piece(last)],
        y_send.at[3 * PIECES + 1], y_recv.at[PIECES + last], stop_to,
    )

    class Gather:
        def __init__(self, number, w, start, stop, x_first):
            self.base, self.w, self.start, self.stop = number * N_GATHER, w, start, stop
            self.x_first = x_first
            self.a, self.b = (x, z) if x_first else (z, x)
            xs, zs = (right, left), (plus, minus)
            (self.up, self.dn), (self.up2, self.dn2) = (xs, zs) if x_first else (zs, xs)
            middle = (start + stop) // 2
            self.all = pl.ds(start, stop - start)
            self.low, self.high = pl.ds(start, middle - start), pl.ds(middle, stop - middle)

        def copy(self, m, to, a=0, b=0, cols=None):
            cols = self.all if cols is None else cols
            a, b = at(self.a + a, 4), at(self.b + b, 4)
            xi, zi = (a, b) if self.x_first else (b, a)
            place = weights.at[self.w, xi, zi, :, cols]
            index = self.base + m
            return remote(place, place, g_send.at[index], g_recv.at[index], to)

        def start1(self):
            go(self.copy(0, self.up))
            go(self.copy(1, self.dn))

        def start2(self, k):
            go(self.copy(4 + k, self.up2, a=k))
            go(self.copy(8 + k, self.dn2, a=k))

        def near1(self, side):
            self.copy(side, (self.up, self.dn)[side]).wait_recv()
            if side == 0:
                go(self.copy(2, self.up, a=-1, cols=self.low))
                self.start2(3)
            else:
                go(self.copy(3, self.dn, a=1, cols=self.high))
                self.start2(1)

        def far1(self):
            self.copy(2, self.up, cols=self.low).wait_recv()
            self.copy(3, self.dn, cols=self.high).wait_recv()
            self.start2(2)

        def near2(self, k, side):
            self.copy(4 + 4 * side + k, (self.up2, self.dn2)[side]).wait_recv()
            if k % 2 == 0 and side == 0:
                go(self.copy(12 + k // 2, self.up2, a=k, b=-1))
            if k % 2 == 1 and side == 1:
                go(self.copy(14 + k // 2, self.dn2, a=k, b=1))

        def far2(self, k):
            if k % 2 == 0:
                self.copy(12 + k // 2, self.up2).wait_recv()
            else:
                self.copy(14 + k // 2, self.dn2).wait_recv()

    down = Gather(0, 0, SPLIT, D, False)
    up = Gather(1, 1, SPLIT, D, False)
    both = Gather(2, slice(None), 0, SPLIT, True)

    def exchange(slot):
        return remote(
            pre_out.at[slot], pre_in.at[slot], m_send.at[slot], m_recv.at[slot], other
        )

    def weight(w, cols):
        block = weights[w, :, :, :, cols]
        return block.reshape(R, block.shape[-1])

    def partial(slot, rows, w):
        total = jnp.zeros((ROWS, R), F32)
        for i in range(PIECES):
            total += lax.dot_general(
                rows[:, piece(i)], weight(w, piece(i)), NT, preferred_element_type=F32
            )
        send_partial(slot, total)

    def send_partial(slot, total):
        pre_out[slot] = total.astype(BF16)
        go(exchange(slot))

    def summed(slot):
        exchange(slot).wait_recv()
        return pre_out[slot].astype(F32) + pre_in[slot].astype(F32)

    for load in loads[4:]:
        load.wait()
    def choose_rows():
        for load in loads[:3]:
            load.wait()
        picks = jnp.where(section == 0, alt[...], -1)
        chosen_t = (lax.broadcasted_iota(jnp.int32, (VISION, ROWS), 0) == picks).astype(BF16)
        hit = lax.dot_general(
            chosen_t, jnp.ones((VISION, PIECE), BF16), TN, preferred_element_type=F32
        )

        for i in range(PIECES):
            cols = piece(i)
            chosen = lax.dot_general(chosen_t, vis[:, cols], TN, preferred_element_type=F32)
            fwd[:, cols] = jnp.where(hit > 0.5, chosen, sec[:, cols].astype(F32)).astype(BF16)
        pl.when(detours)(detour_in.start)
        send_forward(range(PIECES), near)

    def quarter(k, first=0, size=PIECE):
        return pl.ds(pl.multiple_of(at(x + k, NX) * PIECE + first, 128), size)

    def x_copy(m, src, dst, to):
        return remote(src, dst, x_send.at[m], x_recv.at[m], to)

    lows, highs = pl.ds(0, CUT), pl.ds(CUT, PIECE - CUT)
    from_x = [at(x + k, NX) for k in range(-1, 2)]
    row_copies = [
        x_copy(0, grad.at[:, quarter(1)], grads.at[x], right),
        x_copy(1, grad.at[:, quarter(-1)], grads.at[x], left),
        x_copy(2, grad.at[:, quarter(2, 0, CUT)], by_right, right),
        x_copy(3, grad.at[:, quarter(2, CUT, PIECE - CUT)], by_left, left),
        x_copy(4, by_right, grads.at[from_x[0], :, lows], right),
        x_copy(5, by_left, grads.at[from_x[2], :, highs], left),
    ]
    act_copies = [
        x_copy(6, act_ts.at[x], act_ts.at[x], right),
        x_copy(7, act_ts.at[x], act_ts.at[x], left),
        x_copy(8, act_ts.at[from_x[0]], act_ts.at[from_x[0]], right),
    ]

    def rows_far():
        go(row_copies[2])
        go(row_copies[3])

    def rows_near():
        go(row_copies[0])
        go(row_copies[1])
        grads[x] = grad[:, quarter(0)]

    def rows_relay(side):
        row_copies[2 + side].wait_recv()
        go(row_copies[4 + side])

    def rows_done():
        for m in (0, 1, 4, 5):
            row_copies[m].wait_recv()

    def act_send():
        go(act_copies[0])
        go(act_copies[1])

    def act_relay():
        act_copies[0].wait_recv()
        go(act_copies[2])

    def act_done():
        act_copies[1].wait_recv()
        act_copies[2].wait_recv()

    def backward_rows():
        total = jnp.zeros((ROWS, R), F32)
        for i in range(PIECES):
            parked_copies[i].wait_recv()
            cols = piece(i)
            total += lax.dot_general(
                bwd[:, cols], weight(0, cols), NT, preferred_element_type=F32
            )
        send_partial(2, total)

        @pl.when(stops)
        def _():
            detour_in.wait_recv()
            detour_out.start()

    def backward_act():
        bwd_pre[...] = summed(2)
        act_ts[x] = gelu(bwd_pre[...]).astype(BF16).T

    def slopes():
        pre_grad = (summed(1) * gelu_slope(bwd_pre[...])).astype(BF16)
        slope_act[...] = pre_grad
        grad_t[...] = pre_grad.T

    def outputs(i):
        cols = piece(i)
        product = jnp.dot(act[...], weight(1, cols), preferred_element_type=F32)
        out[:, cols] = (fwd[:, cols].astype(F32) + product).astype(BF16)
        if i < HANDED:
            go(shift_copies[i])
        else:
            pl.when(core == 0)(shift_copies[i].start)
            pl.when(core == 1)(hand_copies[i].start)

    def pass_on():
        @pl.when(core == 0)
        def _():
            for i in range(HANDED, PIECES):
                hand_copies[i].wait_recv()
                pass_copies[i].start()

    def add_into(total, term):
        total[...] = (total[...].astype(F32) + term[...].astype(F32)).astype(BF16)

    class Reduce:
        def __init__(self, number, place, start, stop, x_first):
            self.base, self.start, self.stop = number * N_REDUCE, start, stop
            self.parts, self.opp_up, self.opp_dn, self.from_up, self.from_dn = place
            self.x_first = x_first
            self.a, self.b = (x, z) if x_first else (z, x)
            xs, zs = (right, left), (plus, minus)
            (self.up, self.dn), (self.up2, self.dn2) = (xs, zs) if x_first else (zs, xs)
            middle = start + (stop - start + 128) // 256 * 128
            self.all = pl.ds(start, stop - start)
            self.low, self.high = pl.ds(start, middle - start), pl.ds(middle, stop - middle)

        def block(self, a, b0, count):
            a = at(self.a + a, 4)
            if self.x_first:
                return self.parts.at[a, pl.ds(b0, count), :, self.all]
            return self.parts.at[pl.ds(b0, count), a, :, self.all]

        def term(self, ref, b0, count):
            return ref.at[pl.ds(b0, count), :, self.all]

        def total(self, b, cols):
            return sums.at[at(self.b + b, 4), :, cols]

        def copy(self, m):
            src, dst, to = (
                lambda: (self.block(2, 0, 2), self.term(self.opp_up, 0, 2), self.dn),
                lambda: (self.block(2, 2, 2), self.term(self.opp_dn, 0, 2), self.up),
                lambda: (self.block(-1, 2, 2), self.term(self.from_up, 2, 2), self.dn),
                lambda: (self.block(1, 0, 2), self.term(self.from_dn, 0, 2), self.up),
                lambda: (self.block(-1, 0, 2), self.term(self.from_up, 0, 2), self.dn),
                lambda: (self.block(1, 2, 2), self.term(self.from_dn, 2, 2), self.up),
                lambda: (self.total(2, self.low), opp2_up.at[:, self.low], self.dn2),
                lambda: (self.total(2, self.high), opp2_dn.at[:, self.high], self.up2),
                lambda: (self.total(-1, self.high), from2_up.at[:, self.high], self.dn2),
                lambda: (self.total(1, self.low), from2_dn.at[:, self.low], self.up2),
                lambda: (self.total(-1, self.low), from2_up.at[:, self.low], self.dn2),
                lambda: (self.total(1, self.high), from2_dn.at[:, self.high], self.up2),
            )[m]()
            return self.message(m, src, dst, to)

        def message(self, m, src, dst, to):
            index = self.base + m
            return remote(src, dst, r_send.at[index], r_recv.at[index], to)

        def send_far(self):
            for first in range(self.start, self.stop, 640):
                width = min(640, self.stop - first)
                cols = pl.ds(first, width)
                product = jnp.dot(grad_t[...], bwd[:, cols], preferred_element_type=F32)
                parts[:, :, :, cols] = product.astype(BF16).reshape(NX, NZ, SHARE, width)
            go(self.copy(0))
            go(self.copy(1))

        def send_near(self):
            go(self.copy(2))
            go(self.copy(3))

        def relay(self, side):
            self.copy(side).wait_recv()
            if side == 0:
                add_into(self.block(-1, 0, 2), self.term(self.opp_up, 0, 2))
            else:
                add_into(self.block(1, 2, 2), self.term(self.opp_dn, 0, 2))
            go(self.copy(4 + side))

        def folded(self):
            for m in (2, 3, 4, 5):
                self.copy(m).wait_recv()
            return (
                self.block(0, 0, 4)[...].astype(F32)
                + self.term(self.from_up, 0, 4)[...].astype(F32)
                + self.term(self.from_dn, 0, 4)[...].astype(F32)
            )

        def fold(self):
            self.term(sums, 0, 4)[...] = self.folded().astype(BF16)
            for m in (6, 7, 8, 9):
                go(self.copy(m))

        def relay2(self, side):
            self.copy(6 + side).wait_recv()
            if side == 0:
                add_into(self.total(-1, self.low), opp2_up.at[:, self.low])
            else:
                add_into(self.total(1, self.high), opp2_dn.at[:, self.high])
            go(self.copy(10 + side))

        def finish(self):
            cols = self.all
            for m in (8, 9, 10, 11):
                self.copy(m).wait_recv()
            total = (
                parts[x, z, :, cols].astype(F32)
                + from_up[self.b, :, cols].astype(F32)
                + from_dn[self.b, :, cols].astype(F32)
                + from2_up[:, cols].astype(F32)
                + from2_dn[:, cols].astype(F32)
            )
            o_down[:, cols] = (total * (1.0 / 16)).astype(BF16)

    class ReduceUp(Reduce):
        def send_far(self):
            cols = self.all
            product = jnp.zeros((R, cols.size), F32)
            for i in range(NX):
                product += jnp.dot(act_ts[i], grads[i, :, cols], preferred_element_type=F32)
            u_parts[:, :, :, cols] = product.astype(BF16).reshape(NX, NZ, SHARE, cols.size)
            go(self.copy(0))
            go(self.copy(1))

        def owner(self, m):
            k, to = ((1, right), (-1, left), (2, opposite))[m]
            place = o_up.at[:, quarter(0, self.start, self.stop - self.start)]
            return self.message(6 + m, ready.at[at(x + k, NX), :, self.all], place, to)

        def fold(self):
            ready[:, :, self.all] = (self.folded() * (1.0 / 16)).astype(BF16)
            for m in (2, 0, 1):
                go(self.owner(m))
            o_up[:, quarter(0, self.start, self.stop - self.start)] = ready[x, :, self.all]

        def finish(self):
            for m in range(3):
                self.owner(m).wait_recv()

    def input_grad(i):
        cols = piece(i)
        product = jnp.dot(slope_act[...], weight(0, cols), preferred_element_type=F32)
        o_input_grad[:, cols] = (grad[:, cols].astype(F32) + product).astype(BF16)

    down_place = (parts, opp_up, opp_dn, from_up, from_dn)
    up_place = (u_parts, u_opp_up, u_opp_dn, u_from_up, u_from_dn)
    dz = Reduce(0, down_place, 0, 768, False)
    d0 = Reduce(1, down_place, 768, 3584, True)
    u0 = ReduceUp(2, up_place, 0, 512, False)
    u1 = ReduceUp(3, up_place, 512, 896, False)

    both.start1()
    up.start1()
    up.start2(0)
    down.start1()
    both.start2(0)
    down.start2(0)
    loads[3].wait()
    rows_far()
    rows_near()
    choose_rows()
    up.near1(0)
    up.near1(1)
    down.near1(0)
    down.near1(1)
    both.near1(1)
    both.near2(0, 0)
    both.near1(0)
    up.near2(0, 1)
    both.near2(0, 1)
    up.far1()
    up.near2(0, 0)
    down.near2(0, 1)
    down.far1()
    down.near2(0, 0)
    rows_relay(1)
    both.near2(1, 0)
    both.near2(1, 1)
    rows_relay(0)
    both.far2(0)
    both.near2(3, 1)
    both.near2(3, 0)
    both.far2(1)
    up.near2(3, 1)
    up.near2(3, 0)
    up.near2(1, 1)
    both.far2(3)
    up.near2(1, 0)
    down.near2(3, 1)
    down.near2(3, 0)
    down.near2(1, 1)
    down.near2(1, 0)
    both.far1()
    up.near2(2, 1)
    up.near2(2, 0)
    down.near2(2, 1)
    up.far2(0)
    both.near2(2, 0)
    both.near2(2, 1)
    down.near2(2, 0)
    up.far2(3)
    down.far2(0)
    up.far2(1)
    both.far2(2)
    rows_done()
    down.far2(3)
    up.far2(2)
    partial(1, grad, 1)
    down.far2(1)
    down.far2(2)
    backward_rows()
    partial(0, fwd, 0)
    backward_act()
    act_send()
    slopes()
    dz.send_far()
    d0.send_far()
    d0.send_near()
    dz.send_near()
    dz.relay(0)
    dz.relay(1)
    act[...] = gelu(summed(0)).astype(BF16)
    outputs(0)
    outputs(1)
    outputs(2)
    act_relay()
    outputs(3)
    send_forward(range(last), far)
    send_forward([last], ends)
    d0.relay(0)
    input_grad(0)
    input_grad(1)
    d0.relay(1)
    input_grad(2)
    pass_on()
    input_grad(3)
    act_done()
    u0.send_far()
    u0.send_near()
    u1.send_far()
    d0.fold()
    dz.fold()
    u0.relay(1)
    u0.relay(0)
    u1.send_near()
    u1.relay(0)
    u1.relay(1)
    dz.relay2(1)
    dz.relay2(0)
    d0.relay2(0)
    d0.relay2(1)
    u0.fold()
    dz.finish()
    u1.fold()
    d0.finish()
    u0.finish()
    u1.finish()

    for copy in forward_copies + shift_copies:
        copy.wait_recv()
    for copy in pending + forward_copies[:last]:
        copy.wait_send()
    pl.when(jnp.logical_not(detours))(forward_copies[last].wait_send)
    pl.when(detours)(detour_in.wait_send)
    for i in range(HANDED, PIECES):
        pl.when(core == 0)(shift_copies[i].wait_send)
        pl.when(core == 0)(pass_copies[i].wait_send)
        pl.when(core == 1)(hand_copies[i].wait_send)
    pl.when(stops)(detour_out.wait_send)


def write_out(*refs):
    copies = [
        pltpu.make_async_copy(refs[i], refs[5 + i], refs[10].at[i]) for i in range(5)
    ]
    for copy in copies:
        copy.start()
    for copy in copies:
        copy.wait()


def local(section_in, vision_rows, alternate, grad_in, parked, w_down, w_up):
    rows = jax.ShapeDtypeStruct((ROWS, D), BF16)
    shares = jax.ShapeDtypeStruct((SHARE, D), BF16)
    dma = pltpu.SemaphoreType.DMA
    outs = pl.pallas_call(
        kernel,
        out_shape=(pltpu.VMEM((ROWS, D), BF16),) * 3 + (pltpu.VMEM((SHARE, D), BF16),) * 2,
        in_specs=[pl.BlockSpec(memory_space=pltpu.HBM)] * 7,
        out_specs=[pl.BlockSpec(memory_space=pltpu.VMEM)] * 5,
        scratch_shapes=[
            pltpu.VMEM((ROWS, D), BF16),
            pltpu.VMEM((VISION, D), BF16),
            pltpu.VMEM((1, ROWS), jnp.int32),
            pltpu.VMEM((ROWS, D), BF16),
            pltpu.VMEM((ROWS, D), BF16),
            pltpu.VMEM((ROWS, D), BF16),
            pltpu.VMEM((ROWS, D), BF16),
            pltpu.VMEM((2, NX, NZ, SHARE, D), BF16),
            pltpu.VMEM((NX, NZ, SHARE, D), BF16),
            pltpu.VMEM((3, ROWS, R), BF16),
            pltpu.VMEM((3, ROWS, R), BF16),
            pltpu.VMEM((ROWS, R), F32),
            pltpu.VMEM((ROWS, R), BF16),
            pltpu.VMEM((ROWS, R), BF16),
            pltpu.VMEM((NX, R, ROWS), BF16),
            pltpu.VMEM((R, ROWS), BF16),
            pltpu.VMEM((NX, ROWS, PIECE), BF16),
            pltpu.VMEM((ROWS, CUT), BF16),
            pltpu.VMEM((ROWS, PIECE - CUT), BF16),
            pltpu.VMEM((ROWS, (PIECES - HANDED) * PIECE), BF16),
            pltpu.VMEM((ROWS, PIECE), BF16),
            pltpu.VMEM((2, SHARE, D), BF16),
            pltpu.VMEM((2, SHARE, D), BF16),
            pltpu.VMEM((4, SHARE, D), BF16),
            pltpu.VMEM((4, SHARE, D), BF16),
            pltpu.VMEM((SHARE, D), BF16),
            pltpu.VMEM((SHARE, D), BF16),
            pltpu.VMEM((SHARE, D), BF16),
            pltpu.VMEM((SHARE, D), BF16),
            pltpu.VMEM((4, SHARE, D), BF16),
            pltpu.VMEM((NX, NZ, SHARE, PIECE), BF16),
            pltpu.VMEM((2, SHARE, PIECE), BF16),
            pltpu.VMEM((2, SHARE, PIECE), BF16),
            pltpu.VMEM((4, SHARE, PIECE), BF16),
            pltpu.VMEM((4, SHARE, PIECE), BF16),
            pltpu.VMEM((4, SHARE, PIECE), BF16),
            dma((6,)),
            dma((3 * N_GATHER,)),
            dma((3 * N_GATHER,)),
            dma((4 * N_REDUCE,)),
            dma((4 * N_REDUCE,)),
            dma((3,)),
            dma((3,)),
            dma((4 * PIECES,)),
            dma((4 * PIECES,)),
            dma((9,)),
            dma((9,)),
            pltpu.SemaphoreType.REGULAR,
            pltpu.SemaphoreType.REGULAR,
        ],
        compiler_params=pltpu.CompilerParams(
            collective_id=0, has_side_effects=True, vmem_limit_bytes=40 * 2**20
        ),
        cost_estimate=pl.CostEstimate(
            flops=14 * ROWS * D * R, bytes_accessed=12 * ROWS * D, transcendentals=3 * ROWS * R
        ),
        name="relay_tick",
    )(*(
        pltpu.with_memory_space_constraint(operand, pltpu.HBM)
        for operand in (
            section_in[0, 0], vision_rows[0], alternate, grad_in[0, 0], parked[0, 0],
            w_down[0], w_up[0],
        )
    ))
    received, stash, input_grad, up_grad, down_grad = pl.pallas_call(
        write_out,
        out_shape=(rows, rows, rows, shares, shares),
        in_specs=[pl.BlockSpec(memory_space=pltpu.VMEM)] * 5,
        out_specs=[pl.BlockSpec(memory_space=pltpu.HBM)] * 5,
        scratch_shapes=[dma((5,))],
        name="write_out",
    )(*(pltpu.with_memory_space_constraint(out, pltpu.VMEM) for out in outs))
    return (
        received[None, None],
        stash[None, None],
        input_grad[None, None],
        up_grad[None],
        down_grad[None],
    )


def solution(mesh):
    rows = P("section", "dp", None, "mp")
    shares = P("section", "dp", "mp")
    return jax.shard_map(
        local,
        mesh=mesh,
        in_specs=(rows, P("dp", None, "mp"), P("dp", None), rows, rows, shares, shares),
        out_specs=(rows, rows, rows, shares, shares),
        check_vma=False,
    )
```

```python
import functools
import math

import jax
import jax.numpy as jnp
from jax import lax
from jax.experimental import pallas as pl
from jax.experimental.pallas import tpu as pltpu
from jax.sharding import PartitionSpec as P

MESH = pl.DeviceIdType.MESH
BF16, F32 = jnp.bfloat16, jnp.float32

D = 3584
R = 256
ROWS = 104
VISION = 24
SHARE = 16
PIECES = 4
PIECE = D // PIECES
CUT = 512
HANDED = 2
HAND = 3 * PIECES
NX, NZ = 4, 4
SPLIT = 1024

N_GATHER = 16
N_REDUCE = 12

NT = (((1,), (1,)), ((), ()))
TN = (((0,), (0,)), ((), ()))

SCALE = math.sqrt(2 / math.pi)


def gelu(v):
    return 0.5 * v * (1.0 + jnp.tanh(SCALE * (v + 0.044715 * (v * v * v))))


def gelu_slope(v):
    t = jnp.tanh(SCALE * (v + 0.044715 * (v * v * v)))
    return 0.5 * (1.0 + t) + 0.5 * v * (1.0 - t * t) * (SCALE * (1.0 + 3 * 0.044715 * (v * v)))


def kernel(
    section_ref, vision_ref, alternate_ref, grad_ref, parked_ref, wd_ref, wu_ref,
    o_section, o_parked, o_input_grad, o_up, o_down,
    sec, vis, alt, grad, fwd, bwd, out, weights, parts,
    pre_out, pre_in, bwd_pre, act, slope_act, act_ts, grad_t, grads, by_right, by_left,
    hand, stop, opp_up, opp_dn, from_up, from_dn, opp2_up, opp2_dn, from2_up, from2_dn, sums,
    u_parts, u_opp_up, u_opp_dn, u_from_up, u_from_dn, ready,
    local_sem, g_send, g_recv, r_send, r_recv, m_send, m_recv, y_send, y_recv, x_send, x_recv, y_go, xz_go,
):
    section = lax.axis_index("section")
    dp = lax.axis_index("dp")
    mp = lax.axis_index("mp")
    x, z = lax.div(dp, NZ), lax.rem(dp, NZ)

    def at(value, count):
        return lax.rem(value + count, count)

    def chunk(xi, zi):
        return at(xi, NX) * NZ + at(zi, NZ)

    mirror = {"section": 15 - section}
    following = {"section": lax.rem(section + 1, 16)}
    preceding = {"section": lax.rem(section + 15, 16)}
    other = {"mp": 1 - mp}
    right, left = {"dp": chunk(x + 1, z)}, {"dp": chunk(x - 1, z)}
    opposite = {"dp": chunk(x + 2, z)}
    plus, minus = {"dp": chunk(x, z + 1)}, {"dp": chunk(x, z - 1)}

    pending = []

    def remote(src, dst, send, recv, to):
        copy = pltpu.make_async_remote_copy(
            src_ref=src, dst_ref=dst, send_sem=send, recv_sem=recv,
            device_id=to, device_id_type=MESH,
        )
        return copy

    def go(copy):
        copy.start()
        pending.append(copy)

    w_refs = (wd_ref, wu_ref)
    loads = [
        pltpu.make_async_copy(section_ref, sec, local_sem.at[0]),
        pltpu.make_async_copy(vision_ref, vis, local_sem.at[1]),
        pltpu.make_async_copy(alternate_ref, alt, local_sem.at[2]),
        pltpu.make_async_copy(grad_ref, grad, local_sem.at[3]),
        pltpu.make_async_copy(wd_ref, weights.at[0, x, z], local_sem.at[4]),
        pltpu.make_async_copy(wu_ref, weights.at[1, x, z], local_sem.at[5]),
    ]
    y, core = lax.div(section, 2), lax.rem(section, 2)
    turn = lax.rem(y, 4)
    near = jnp.logical_or(turn == 0, turn == 3)
    far = jnp.logical_not(near)
    detours, stops, ends = turn == 2, turn == 0, turn == 1
    next_chip = {"section": lax.rem(section + 2, 16)}
    stop_at = {"section": lax.rem(section + 12, 16)}
    stop_to = {"section": lax.rem(y + 5, 8) * 2 + 1 - core}

    barrier = pltpu.get_barrier_semaphore()

    def greet(*partners):
        for partner in partners:
            pl.semaphore_signal(barrier, inc=1, device_id=partner, device_id_type=MESH)

    def chip_y(value):
        return {"section": 2 * lax.rem(value + 8, 8)}

    mate = {"section": section + 1 - 2 * core}
    greet(mate, chip_y(7 - y), chip_y(y + 1), chip_y(y - 1))
    pl.when(detours)(lambda: greet(chip_y(y - 2)))
    pl.when(stops)(lambda: greet(chip_y(y + 2), chip_y(y + 5)))
    pl.when(ends)(lambda: greet(chip_y(y + 3)))
    greet(*({**to, "section": 2 * y + 1} for to in (right, left, opposite, plus, minus, other)))
    for load in loads:
        load.start()
    extra = jnp.where(stops, 2, jnp.where(turn == 3, 0, 1))

    @pl.when(core == 0)
    def _():
        pl.semaphore_wait(barrier, 7 + 2 * extra)
        pl.semaphore_signal(y_go, inc=1, device_id=mate, device_id_type=MESH)

    @pl.when(core == 1)
    def _():
        pl.semaphore_wait(y_go, 1)

    def piece(i):
        return pl.ds(i * PIECE, PIECE)

    def y_piece(src, dst, index, i, to):
        return remote(
            src.at[:, piece(i)], dst.at[:, piece(i)], y_send.at[index], y_recv.at[index], to
        )

    parked_copies = [y_piece(parked_ref, bwd, i, i, mirror) for i in range(PIECES)]
    forward_copies = [y_piece(fwd, o_parked, PIECES + i, i, mirror) for i in range(PIECES)]
    shift_copies = [y_piece(out, o_section, 2 * PIECES + i, i, following) for i in range(PIECES)]
    for copy in parked_copies:
        go(copy)

    @pl.when(core == 1)
    def _():
        pl.semaphore_wait(barrier, 13)
        pl.semaphore_signal(xz_go, inc=1, device_id=mate, device_id_type=MESH)

    @pl.when(core == 0)
    def _():
        pl.semaphore_wait(xz_go, 1)

    def send_forward(pieces, when):
        @pl.when(when)
        def _():
            for i in pieces:
                forward_copies[i].start()

    hand_copies, pass_copies = {}, {}
    for i in range(HANDED, PIECES):
        held = hand.at[:, pl.ds((i - HANDED) * PIECE, PIECE)]
        hand_copies[i] = remote(
            out.at[:, piece(i)], held, y_send.at[HAND + i], y_recv.at[HAND + i], preceding
        )
        pass_copies[i] = remote(
            held, o_section.at[:, piece(i)],
            y_send.at[HAND + i], y_recv.at[2 * PIECES + i], next_chip,
        )

    last = PIECES - 1
    detour_in = remote(
        fwd.at[:, piece(last)], stop, y_send.at[3 * PIECES], y_recv.at[3 * PIECES], stop_at
    )
    detour_out = remote(
        stop, o_parked.at[:, piece(last)],
        y_send.at[3 * PIECES + 1], y_recv.at[PIECES + last], stop_to,
    )

    class Gather:
        def __init__(self, number, w, start, stop, x_first):
            self.base, self.w, self.start, self.stop = number * N_GATHER, w, start, stop
            self.x_first = x_first
            self.a, self.b = (x, z) if x_first else (z, x)
            xs, zs = (right, left), (plus, minus)
            (self.up, self.dn), (self.up2, self.dn2) = (xs, zs) if x_first else (zs, xs)
            middle = (start + stop) // 2
            self.all = pl.ds(start, stop - start)
            self.low, self.high = pl.ds(start, middle - start), pl.ds(middle, stop - middle)

        def copy(self, m, to, a=0, b=0, cols=None):
            cols = self.all if cols is None else cols
            a, b = at(self.a + a, 4), at(self.b + b, 4)
            xi, zi = (a, b) if self.x_first else (b, a)
            place = weights.at[self.w, xi, zi, :, cols]
            index = self.base + m
            return remote(place, place, g_send.at[index], g_recv.at[index], to)

        def start1(self):
            go(self.copy(0, self.up))
            go(self.copy(1, self.dn))

        def start2(self, k):
            go(self.copy(4 + k, self.up2, a=k))
            go(self.copy(8 + k, self.dn2, a=k))

        def near1(self, side):
            self.copy(side, (self.up, self.dn)[side]).wait_recv()
            if side == 0:
                go(self.copy(2, self.up, a=-1, cols=self.low))
                self.start2(3)
            else:
                go(self.copy(3, self.dn, a=1, cols=self.high))
                self.start2(1)

        def far1(self):
            self.copy(2, self.up, cols=self.low).wait_recv()
            self.copy(3, self.dn, cols=self.high).wait_recv()
            self.start2(2)

        def near2(self, k, side):
            self.copy(4 + 4 * side + k, (self.up2, self.dn2)[side]).wait_recv()
            if k % 2 == 0 and side == 0:
                go(self.copy(12 + k // 2, self.up2, a=k, b=-1))
            if k % 2 == 1 and side == 1:
                go(self.copy(14 + k // 2, self.dn2, a=k, b=1))

        def far2(self, k):
            if k % 2 == 0:
                self.copy(12 + k // 2, self.up2).wait_recv()
            else:
                self.copy(14 + k // 2, self.dn2).wait_recv()

    down = Gather(0, 0, SPLIT, D, False)
    up = Gather(1, 1, SPLIT, D, False)
    both = Gather(2, slice(None), 0, SPLIT, True)

    def exchange(slot):
        return remote(
            pre_out.at[slot], pre_in.at[slot], m_send.at[slot], m_recv.at[slot], other
        )

    def weight(w, cols):
        block = weights[w, :, :, :, cols]
        return block.reshape(R, block.shape[-1])

    def partial(slot, rows, w):
        total = jnp.zeros((ROWS, R), F32)
        for i in range(PIECES):
            total += lax.dot_general(
                rows[:, piece(i)], weight(w, piece(i)), NT, preferred_element_type=F32
            )
        send_partial(slot, total)

    def send_partial(slot, total):
        pre_out[slot] = total.astype(BF16)
        go(exchange(slot))

    def summed(slot):
        exchange(slot).wait_recv()
        return pre_out[slot].astype(F32) + pre_in[slot].astype(F32)

    for load in loads[4:]:
        load.wait()
    def choose_rows():
        for load in loads[:3]:
            load.wait()
        picks = jnp.where(section == 0, alt[...], -1)
        chosen_t = (lax.broadcasted_iota(jnp.int32, (VISION, ROWS), 0) == picks).astype(BF16)
        hit = lax.dot_general(
            chosen_t, jnp.ones((VISION, PIECE), BF16), TN, preferred_element_type=F32
        )

        for i in range(PIECES):
            cols = piece(i)
            chosen = lax.dot_general(chosen_t, vis[:, cols], TN, preferred_element_type=F32)
            fwd[:, cols] = jnp.where(hit > 0.5, chosen, sec[:, cols].astype(F32)).astype(BF16)
        pl.when(detours)(detour_in.start)
        send_forward(range(PIECES), near)

    def quarter(k, first=0, size=PIECE):
        return pl.ds(pl.multiple_of(at(x + k, NX) * PIECE + first, 128), size)

    def x_copy(m, src, dst, to):
        return remote(src, dst, x_send.at[m], x_recv.at[m], to)

    lows, highs = pl.ds(0, CUT), pl.ds(CUT, PIECE - CUT)
    from_x = [at(x + k, NX) for k in range(-1, 2)]
    row_copies = [
        x_copy(0, grad.at[:, quarter(1)], grads.at[x], right),
        x_copy(1, grad.at[:, quarter(-1)], grads.at[x], left),
        x_copy(2, grad.at[:, quarter(2, 0, CUT)], by_right, right),
        x_copy(3, grad.at[:, quarter(2, CUT, PIECE - CUT)], by_left, left),
        x_copy(4, by_right, grads.at[from_x[0], :, lows], right),
        x_copy(5, by_left, grads.at[from_x[2], :, highs], left),
    ]
    act_copies = [
        x_copy(6, act_ts.at[x], act_ts.at[x], right),
        x_copy(7, act_ts.at[x], act_ts.at[x], left),
        x_copy(8, act_ts.at[from_x[0]], act_ts.at[from_x[0]], right),
    ]

    def rows_far():
        go(row_copies[2])
        go(row_copies[3])

    def rows_near():
        go(row_copies[0])
        go(row_copies[1])
        grads[x] = grad[:, quarter(0)]

    def rows_relay(side):
        row_copies[2 + side].wait_recv()
        go(row_copies[4 + side])

    def rows_done():
        for m in (0, 1, 4, 5):
            row_copies[m].wait_recv()

    def act_send():
        go(act_copies[0])
        go(act_copies[1])

    def act_relay():
        act_copies[0].wait_recv()
        go(act_copies[2])

    def act_done():
        act_copies[1].wait_recv()
        act_copies[2].wait_recv()

    def backward_rows():
        total = jnp.zeros((ROWS, R), F32)
        for i in range(PIECES):
            parked_copies[i].wait_recv()
            cols = piece(i)
            total += lax.dot_general(
                bwd[:, cols], weight(0, cols), NT, preferred_element_type=F32
            )
        send_partial(2, total)

        @pl.when(stops)
        def _():
            detour_in.wait_recv()
            detour_out.start()

    def backward_act():
        bwd_pre[...] = summed(2)
        act_ts[x] = gelu(bwd_pre[...]).astype(BF16).T

    def slopes():
        pre_grad = (summed(1) * gelu_slope(bwd_pre[...])).astype(BF16)
        slope_act[...] = pre_grad
        grad_t[...] = pre_grad.T

    def outputs(i):
        cols = piece(i)
        product = jnp.dot(act[...], weight(1, cols), preferred_element_type=F32)
        out[:, cols] = (fwd[:, cols].astype(F32) + product).astype(BF16)
        if i < HANDED:
            go(shift_copies[i])
        else:
            pl.when(core == 0)(shift_copies[i].start)
            pl.when(core == 1)(hand_copies[i].start)

    def pass_on():
        @pl.when(core == 0)
        def _():
            for i in range(HANDED, PIECES):
                hand_copies[i].wait_recv()
                pass_copies[i].start()

    def add_into(total, term):
        total[...] = (total[...].astype(F32) + term[...].astype(F32)).astype(BF16)

    class Reduce:
        def __init__(self, number, place, start, stop, x_first):
            self.base, self.start, self.stop = number * N_REDUCE, start, stop
            self.parts, self.opp_up, self.opp_dn, self.from_up, self.from_dn = place
            self.x_first = x_first
            self.a, self.b = (x, z) if x_first else (z, x)
            xs, zs = (right, left), (plus, minus)
            (self.up, self.dn), (self.up2, self.dn2) = (xs, zs) if x_first else (zs, xs)
            middle = start + (stop - start + 128) // 256 * 128
            self.all = pl.ds(start, stop - start)
            self.low, self.high = pl.ds(start, middle - start), pl.ds(middle, stop - middle)

        def block(self, a, b0, count):
            a = at(self.a + a, 4)
            if self.x_first:
                return self.parts.at[a, pl.ds(b0, count), :, self.all]
            return self.parts.at[pl.ds(b0, count), a, :, self.all]

        def term(self, ref, b0, count):
            return ref.at[pl.ds(b0, count), :, self.all]

        def total(self, b, cols):
            return sums.at[at(self.b + b, 4), :, cols]

        def copy(self, m):
            src, dst, to = (
                lambda: (self.block(2, 0, 2), self.term(self.opp_up, 0, 2), self.dn),
                lambda: (self.block(2, 2, 2), self.term(self.opp_dn, 0, 2), self.up),
                lambda: (self.block(-1, 2, 2), self.term(self.from_up, 2, 2), self.dn),
                lambda: (self.block(1, 0, 2), self.term(self.from_dn, 0, 2), self.up),
                lambda: (self.block(-1, 0, 2), self.term(self.from_up, 0, 2), self.dn),
                lambda: (self.block(1, 2, 2), self.term(self.from_dn, 2, 2), self.up),
                lambda: (self.total(2, self.low), opp2_up.at[:, self.low], self.dn2),
                lambda: (self.total(2, self.high), opp2_dn.at[:, self.high], self.up2),
                lambda: (self.total(-1, self.high), from2_up.at[:, self.high], self.dn2),
                lambda: (self.total(1, self.low), from2_dn.at[:, self.low], self.up2),
                lambda: (self.total(-1, self.low), from2_up.at[:, self.low], self.dn2),
                lambda: (self.total(1, self.high), from2_dn.at[:, self.high], self.up2),
            )[m]()
            return self.message(m, src, dst, to)

        def message(self, m, src, dst, to):
            index = self.base + m
            return remote(src, dst, r_send.at[index], r_recv.at[index], to)

        def send_far(self):
            for first in range(self.start, self.stop, 640):
                width = min(640, self.stop - first)
                cols = pl.ds(first, width)
                product = jnp.dot(grad_t[...], bwd[:, cols], preferred_element_type=F32)
                parts[:, :, :, cols] = product.astype(BF16).reshape(NX, NZ, SHARE, width)
            go(self.copy(0))
            go(self.copy(1))

        def send_near(self):
            go(self.copy(2))
            go(self.copy(3))

        def relay(self, side):
            self.copy(side).wait_recv()
            if side == 0:
                add_into(self.block(-1, 0, 2), self.term(self.opp_up, 0, 2))
            else:
                add_into(self.block(1, 2, 2), self.term(self.opp_dn, 0, 2))
            go(self.copy(4 + side))

        def folded(self):
            for m in (2, 3, 4, 5):
                self.copy(m).wait_recv()
            return (
                self.block(0, 0, 4)[...].astype(F32)
                + self.term(self.from_up, 0, 4)[...].astype(F32)
                + self.term(self.from_dn, 0, 4)[...].astype(F32)
            )

        def fold(self):
            self.term(sums, 0, 4)[...] = self.folded().astype(BF16)
            for m in (6, 7, 8, 9):
                go(self.copy(m))

        def relay2(self, side):
            self.copy(6 + side).wait_recv()
            if side == 0:
                add_into(self.total(-1, self.low), opp2_up.at[:, self.low])
            else:
                add_into(self.total(1, self.high), opp2_dn.at[:, self.high])
            go(self.copy(10 + side))

        def finish(self):
            cols = self.all
            for m in (8, 9, 10, 11):
                self.copy(m).wait_recv()
            total = (
                parts[x, z, :, cols].astype(F32)
                + from_up[self.b, :, cols].astype(F32)
                + from_dn[self.b, :, cols].astype(F32)
                + from2_up[:, cols].astype(F32)
                + from2_dn[:, cols].astype(F32)
            )
            o_down[:, cols] = (total * (1.0 / 16)).astype(BF16)

    class ReduceUp(Reduce):
        def send_far(self):
            cols = self.all
            product = jnp.zeros((R, cols.size), F32)
            for i in range(NX):
                product += jnp.dot(act_ts[i], grads[i, :, cols], preferred_element_type=F32)
            u_parts[:, :, :, cols] = product.astype(BF16).reshape(NX, NZ, SHARE, cols.size)
            go(self.copy(0))
            go(self.copy(1))

        def owner(self, m):
            k, to = ((1, right), (-1, left), (2, opposite))[m]
            place = o_up.at[:, quarter(0, self.start, self.stop - self.start)]
            return self.message(6 + m, ready.at[at(x + k, NX), :, self.all], place, to)

        def fold(self):
            ready[:, :, self.all] = (self.folded() * (1.0 / 16)).astype(BF16)
            for m in (2, 0, 1):
                go(self.owner(m))
            o_up[:, quarter(0, self.start, self.stop - self.start)] = ready[x, :, self.all]

        def finish(self):
            for m in range(3):
                self.owner(m).wait_recv()

    def input_grad(i):
        cols = piece(i)
        product = jnp.dot(slope_act[...], weight(0, cols), preferred_element_type=F32)
        o_input_grad[:, cols] = (grad[:, cols].astype(F32) + product).astype(BF16)

    down_place = (parts, opp_up, opp_dn, from_up, from_dn)
    up_place = (u_parts, u_opp_up, u_opp_dn, u_from_up, u_from_dn)
    dz = Reduce(0, down_place, 0, 768, False)
    d0 = Reduce(1, down_place, 768, 2176, True)
    d1 = Reduce(2, down_place, 2176, 3584, True)
    u0 = ReduceUp(3, up_place, 0, 384, False)
    u1 = ReduceUp(4, up_place, 384, 896, False)

    both.start1()
    down.start1()
    up.start2(0)
    both.start2(0)
    down.start2(0)
    up.start1()
    loads[3].wait()
    rows_far()
    rows_near()
    choose_rows()
    both.near1(0)
    both.near1(1)
    up.near2(0, 0)
    up.near2(0, 1)
    down.near2(0, 0)
    down.near2(0, 1)
    rows_relay(1)
    both.far1()
    both.near2(0, 0)
    both.near2(0, 1)
    rows_relay(0)
    down.near1(0)
    down.near1(1)
    up.near1(1)
    up.near1(0)
    up.far2(0)
    down.near2(3, 1)
    down.near2(1, 1)
    down.far2(0)
    both.near2(3, 1)
    both.near2(1, 1)
    up.near2(1, 1)
    up.near2(3, 1)
    both.near2(3, 0)
    both.near2(1, 0)
    both.near2(2, 1)
    down.far1()
    down.near2(3, 0)
    down.near2(1, 0)
    up.far1()
    rows_done()
    up.near2(1, 0)
    both.near2(2, 0)
    up.near2(3, 0)
    both.far2(0)
    down.far2(3)
    down.far2(1)
    down.near2(2, 0)
    both.far2(3)
    both.far2(1)
    up.near2(2, 0)
    both.far2(2)
    up.far2(1)
    up.far2(3)
    down.near2(2, 1)
    down.far2(2)
    backward_rows()
    up.near2(2, 1)
    partial(0, fwd, 0)
    up.far2(2)
    partial(1, grad, 1)
    backward_act()
    act_send()
    act[...] = gelu(summed(0)).astype(BF16)
    outputs(0)
    outputs(1)
    outputs(2)
    slopes()
    dz.send_far()
    act_relay()
    dz.send_near()
    d0.send_far()
    d1.send_far()
    d0.send_near()
    d1.send_near()
    outputs(3)
    send_forward(range(last), far)
    send_forward([last], ends)
    act_done()
    u0.send_far()
    u0.send_near()
    u1.send_far()
    dz.relay(1)
    dz.relay(0)
    u1.send_near()
    input_grad(0)
    d0.relay(0)
    input_grad(1)
    pass_on()
    d0.relay(1)
    u0.relay(0)
    u0.relay(1)
    input_grad(2)
    input_grad(3)
    d1.relay(0)
    d1.relay(1)
    u1.relay(0)
    u1.relay(1)
    d0.fold()
    u0.fold()
    dz.fold()
    d1.fold()
    u0.finish()
    dz.relay2(0)
    dz.relay2(1)
    u1.fold()
    d0.relay2(0)
    d0.relay2(1)
    dz.finish()
    d1.relay2(0)
    d1.relay2(1)
    u1.finish()
    d0.finish()
    d1.finish()

    for copy in forward_copies + shift_copies:
        copy.wait_recv()
    for copy in pending + forward_copies[:last]:
        copy.wait_send()
    pl.when(jnp.logical_not(detours))(forward_copies[last].wait_send)
    pl.when(detours)(detour_in.wait_send)
    for i in range(HANDED, PIECES):
        pl.when(core == 0)(shift_copies[i].wait_send)
        pl.when(core == 0)(pass_copies[i].wait_send)
        pl.when(core == 1)(hand_copies[i].wait_send)
    pl.when(stops)(detour_out.wait_send)


def write_out(*refs):
    copies = [
        pltpu.make_async_copy(refs[i], refs[5 + i], refs[10].at[i]) for i in range(5)
    ]
    for copy in copies:
        copy.start()
    for copy in copies:
        copy.wait()


def local(section_in, vision_rows, alternate, grad_in, parked, w_down, w_up):
    rows = jax.ShapeDtypeStruct((ROWS, D), BF16)
    shares = jax.ShapeDtypeStruct((SHARE, D), BF16)
    dma = pltpu.SemaphoreType.DMA
    outs = pl.pallas_call(
        kernel,
        out_shape=(pltpu.VMEM((ROWS, D), BF16),) * 3 + (pltpu.VMEM((SHARE, D), BF16),) * 2,
        in_specs=[pl.BlockSpec(memory_space=pltpu.HBM)] * 7,
        out_specs=[pl.BlockSpec(memory_space=pltpu.VMEM)] * 5,
        scratch_shapes=[
            pltpu.VMEM((ROWS, D), BF16),
            pltpu.VMEM((VISION, D), BF16),
            pltpu.VMEM((1, ROWS), jnp.int32),
            pltpu.VMEM((ROWS, D), BF16),
            pltpu.VMEM((ROWS, D), BF16),
            pltpu.VMEM((ROWS, D), BF16),
            pltpu.VMEM((ROWS, D), BF16),
            pltpu.VMEM((2, NX, NZ, SHARE, D), BF16),
            pltpu.VMEM((NX, NZ, SHARE, D), BF16),
            pltpu.VMEM((3, ROWS, R), BF16),
            pltpu.VMEM((3, ROWS, R), BF16),
            pltpu.VMEM((ROWS, R), F32),
            pltpu.VMEM((ROWS, R), BF16),
            pltpu.VMEM((ROWS, R), BF16),
            pltpu.VMEM((NX, R, ROWS), BF16),
            pltpu.VMEM((R, ROWS), BF16),
            pltpu.VMEM((NX, ROWS, PIECE), BF16),
            pltpu.VMEM((ROWS, CUT), BF16),
            pltpu.VMEM((ROWS, PIECE - CUT), BF16),
            pltpu.VMEM((ROWS, (PIECES - HANDED) * PIECE), BF16),
            pltpu.VMEM((ROWS, PIECE), BF16),
            pltpu.VMEM((2, SHARE, D), BF16),
            pltpu.VMEM((2, SHARE, D), BF16),
            pltpu.VMEM((4, SHARE, D), BF16),
            pltpu.VMEM((4, SHARE, D), BF16),
            pltpu.VMEM((SHARE, D), BF16),
            pltpu.VMEM((SHARE, D), BF16),
            pltpu.VMEM((SHARE, D), BF16),
            pltpu.VMEM((SHARE, D), BF16),
            pltpu.VMEM((4, SHARE, D), BF16),
            pltpu.VMEM((NX, NZ, SHARE, PIECE), BF16),
            pltpu.VMEM((2, SHARE, PIECE), BF16),
            pltpu.VMEM((2, SHARE, PIECE), BF16),
            pltpu.VMEM((4, SHARE, PIECE), BF16),
            pltpu.VMEM((4, SHARE, PIECE), BF16),
            pltpu.VMEM((4, SHARE, PIECE), BF16),
            dma((6,)),
            dma((3 * N_GATHER,)),
            dma((3 * N_GATHER,)),
            dma((5 * N_REDUCE,)),
            dma((5 * N_REDUCE,)),
            dma((3,)),
            dma((3,)),
            dma((4 * PIECES,)),
            dma((4 * PIECES,)),
            dma((9,)),
            dma((9,)),
            pltpu.SemaphoreType.REGULAR,
            pltpu.SemaphoreType.REGULAR,
        ],
        compiler_params=pltpu.CompilerParams(
            collective_id=0, has_side_effects=True, vmem_limit_bytes=40 * 2**20
        ),
        cost_estimate=pl.CostEstimate(
            flops=14 * ROWS * D * R, bytes_accessed=12 * ROWS * D, transcendentals=3 * ROWS * R
        ),
        name="relay_tick",
    )(*(
        pltpu.with_memory_space_constraint(operand, pltpu.HBM)
        for operand in (
            section_in[0, 0], vision_rows[0], alternate, grad_in[0, 0], parked[0, 0],
            w_down[0], w_up[0],
        )
    ))
    received, stash, input_grad, up_grad, down_grad = pl.pallas_call(
        write_out,
        out_shape=(rows, rows, rows, shares, shares),
        in_specs=[pl.BlockSpec(memory_space=pltpu.VMEM)] * 5,
        out_specs=[pl.BlockSpec(memory_space=pltpu.HBM)] * 5,
        scratch_shapes=[dma((5,))],
        name="write_out",
    )(*(pltpu.with_memory_space_constraint(out, pltpu.VMEM) for out in outs))
    return (
        received[None, None],
        stash[None, None],
        input_grad[None, None],
        up_grad[None],
        down_grad[None],
    )


def solution(mesh):
    rows = P("section", "dp", None, "mp")
    shares = P("section", "dp", "mp")
    return jax.shard_map(
        local,
        mesh=mesh,
        in_specs=(rows, P("dp", None, "mp"), P("dp", None), rows, rows, shares, shares),
        out_specs=(rows, rows, rows, shares, shares),
        check_vma=False,
    )
```
